32 devices in a mesh: dom: 8 (over z, y), sub: 4 (over x, core).
Axes of the slice: x: 2, y: 2, z: 4, core: 2. Of those that a mesh axis runs over, the one named last changes fastest.
Arguments:
- features: bfloat16 [32768, 256], P(('dom', 'sub')), may hold values from -6 to 6
- cotangent: bfloat16 [32768, 256], P(('dom', 'sub')), may hold values from -6 to 6
- w_self_one: bfloat16 [256, 256], replicated, may hold values from -0.375 to 0.375
- w_nbr_one: bfloat16 [256, 256], replicated, may hold values from -0.375 to 0.375
- bias_one: float32 [256], replicated, may hold values from -4 to 4
- w_self_two: bfloat16 [256, 256], replicated, may hold values from -0.375 to 0.375
- w_nbr_two: bfloat16 [256, 256], replicated, may hold values from -0.375 to 0.375
- in_count: int32 [32768], P(('dom', 'sub')), may hold values from 0 to 7
- send_list: int32 [32, 32, 4], P(('dom', 'sub')), may hold values from 0 to 1023
- src_slot: int32 [32, 2048], P(('dom', 'sub')), may hold values from 0 to 1151
- dst_slot: int32 [32, 2048], P(('dom', 'sub')), may hold values from 0 to 1151
- edge_count: int32 [32], P(('dom', 'sub')), may hold values from 512 to 2048, as said below
Outputs:
- grad_features: bfloat16 [32768, 256], P(('dom', 'sub'))
- grad_weights: float32 [4, 256, 256], replicated
- grad_bias: float32 [256], replicated
The draws below stay inside these ranges and needn't reach their ends.
Inputs may be any that keep to these rules, and one draw needn't show every extreme that they name: Each device's first edge_count slots are live; one device has all 2048 live in every draw.
All inputs are finite; a program needn't handle non-finite values.
Results may differ from the reference program's by a relative error of at most 0.0056.
Values may be sent and summed in bfloat16 or wider, within the bound.
No kernel may reach another device: no remote copies, remote signals or barrier semaphores. Data moves between devices by JAX's collectives and lax.ppermute only.
A program may use at most 64 MiB of HBM per device.

```python
import jax
import jax.numpy as jnp
from jax import lax

D = 256
NODE_DEV = 1024
CAP = 4
E_DEV = 2048
DEV_COUNT = 32
NODES = 32768
SLOTS = 1152
N_DOM = 8
N_SUB = 4


def draw_edge_count(key, part):
    first_key, second_key = jax.random.split(jax.random.fold_in(key, 17))
    counts = jax.random.randint(first_key, (N_DOM * N_SUB,), E_DEV // 4, E_DEV + 1)
    fullest = jax.random.randint(second_key, (), 0, N_DOM * N_SUB)
    return jnp.where(jnp.arange(N_DOM * N_SUB) == fullest, E_DEV, counts).astype(jnp.int32)


def set_ends(result, key, least, high):
    index_at = [jax.random.randint(jax.random.fold_in(key, axis), (), 0, length) for axis, length in enumerate(result.shape)]
    main_axis = result.shape.index(max(result.shape))
    neighbour = index_at[:main_axis] + [(index_at[main_axis] + 1) % result.shape[main_axis]] + index_at[main_axis + 1:]
    return result.at[tuple(index_at)].set(least).at[tuple(neighbour)].set(high)


def level_of(stream_key, extent, cuts, least, top_value):
    def one(dim, parts):
        steps = jax.random.uniform(jax.random.fold_in(jax.random.fold_in(stream_key, 6), dim), (parts,), jnp.float32, least / len(cuts), top_value / len(cuts))
        return jnp.repeat(jnp.exp(steps), extent[dim] // parts).reshape((-1,) + (1,) * (len(extent) - dim - 1))

    gain = one(*cuts[0])
    for cut in cuts[1:]:
        gain = gain * one(*cut)
    return gain


def centred(key, dims, scale, bound, cuts=(), held_as=jnp.bfloat16):
    values = scale * jax.random.normal(key, dims, jnp.float32)
    if cuts:
        values = values * level_of(key, dims, cuts, -0.22, 0.18)
    return jnp.clip(values, -bound, bound).astype(held_as)


def setup_inputs(seed: int = 0) -> dict:
    key_of = jax.random.split(jax.random.key(seed), 13)
    return {
        "features": centred(key_of[0], (NODES, D), 1.0, 6.0, ((0, 32),)),
        "cotangent": centred(key_of[1], (NODES, D), 1.0, 6.0, ((0, 32),)),
        "w_self_one": centred(key_of[2], (D, D), D ** -0.5, 0.375),
        "w_nbr_one": centred(key_of[3], (D, D), D ** -0.5, 0.375),
        "bias_one": centred(key_of[4], (D,), 0.7, 4.0, (), jnp.float32),
        "w_self_two": centred(key_of[5], (D, D), D ** -0.5, 0.375),
        "w_nbr_two": centred(key_of[6], (D, D), D ** -0.5, 0.375),
        "in_count": set_ends(jax.random.randint(key_of[7], (NODES,), 0, 8), jax.random.fold_in(key_of[7], 1), 0, 7).astype(jnp.int32),
        "send_list": set_ends(jax.random.randint(key_of[8], (DEV_COUNT, DEV_COUNT, CAP), 0, NODE_DEV), jax.random.fold_in(key_of[8], 1), 0, NODE_DEV - 1).astype(jnp.int32),
        "src_slot": set_ends(jax.random.randint(key_of[9], (DEV_COUNT, E_DEV), 0, SLOTS), jax.random.fold_in(key_of[9], 1), 0, SLOTS - 1).astype(jnp.int32),
        "dst_slot": set_ends(jax.random.randint(key_of[10], (DEV_COUNT, E_DEV), 0, SLOTS), jax.random.fold_in(key_of[10], 1), 0, SLOTS - 1).astype(jnp.int32),
        "edge_count": draw_edge_count(jax.random.fold_in(key_of[12], 71), 0),
    }


def global_nodes(slot, send_list):
    device_ids = jnp.arange(N_DOM * N_SUB, dtype=jnp.int32)[:, None]
    mirror_pos = jnp.clip(slot - NODE_DEV, 0, N_DOM * N_SUB * CAP - 1)
    owner_dev = mirror_pos // CAP
    within = mirror_pos % CAP
    remote = owner_dev * NODE_DEV + send_list[owner_dev, device_ids, within]
    return jnp.where(slot < NODE_DEV, device_ids * NODE_DEV + slot, remote).astype(jnp.int32)

def spread(values, from_node, into_node, live_mask, nodes):

    def one_device(total, pieces):
        from_row, into_row, live_row = pieces
        picked = jnp.where(live_row[:, None], values[from_row].astype(jnp.float32), 0.0)
        return (total.at[into_row].add(picked), None)
    start = jnp.zeros((nodes, values.shape[1]), jnp.float32)
    total, _ = lax.scan(one_device, start, (from_node, into_node, live_mask))
    return total

def silu_grad(value):
    sig = jax.nn.sigmoid(value)
    return sig * (1.0 + value * (1.0 - sig))

def tdot(left, right):
    return jnp.dot(left.T, right, preferred_element_type=jnp.float32)

def reference(features, cotangent, w_self_one, w_nbr_one, bias_one, w_self_two, w_nbr_two, in_count, send_list, src_slot, dst_slot, edge_count):
    nodes = features.shape[0]
    sources = global_nodes(src_slot, send_list)
    targets = global_nodes(dst_slot, send_list)
    live_mask = jnp.arange(E_DEV, dtype=jnp.int32)[None, :] < edge_count[:, None]
    inverse = (1.0 / jnp.maximum(in_count, 1).astype(jnp.float32))[:, None]
    mean_one = (spread(features, sources, targets, live_mask, nodes) * inverse).astype(jnp.bfloat16)
    z_one = jnp.dot(features, w_self_one, preferred_element_type=jnp.float32) + jnp.dot(mean_one, w_nbr_one, preferred_element_type=jnp.float32) + bias_one
    h_one = jax.nn.silu(z_one).astype(jnp.bfloat16)
    mean_two = (spread(h_one, sources, targets, live_mask, nodes) * inverse).astype(jnp.bfloat16)
    message_two = (jnp.dot(cotangent, w_nbr_two.T, preferred_element_type=jnp.float32) * inverse).astype(jnp.bfloat16)
    grad_h_one = jnp.dot(cotangent, w_self_two.T, preferred_element_type=jnp.float32) + spread(message_two, targets, sources, live_mask, nodes)
    grad_z_one = (grad_h_one * silu_grad(z_one)).astype(jnp.bfloat16)
    message_one = (jnp.dot(grad_z_one, w_nbr_one.T, preferred_element_type=jnp.float32) * inverse).astype(jnp.bfloat16)
    grad_features = (jnp.dot(grad_z_one, w_self_one.T, preferred_element_type=jnp.float32) + spread(message_one, targets, sources, live_mask, nodes)).astype(jnp.bfloat16)
    norm_factor = jnp.float32(nodes) ** (-0.5)
    grad_weights = jnp.stack([tdot(features, grad_z_one), tdot(mean_one, grad_z_one), tdot(h_one, cotangent), tdot(mean_two, cotangent)]) * norm_factor
    grad_bias = lax.optimization_barrier(jnp.sum(grad_z_one.astype(jnp.float32), axis=0)) * norm_factor
    return (grad_features, grad_weights, grad_bias)
```

```python
import jax
import jax.numpy as jnp
from jax import lax
from jax.sharding import PartitionSpec as P

AXES = ("dom", "sub")


def tdot(left, right):
    return lax.dot_general(
        left, right, (((0,), (0,)), ((), ())), preferred_element_type=jnp.float32
    )


def dot_transposed(left, right):
    return lax.dot_general(
        left, right, (((1,), (1,)), ((), ())), preferred_element_type=jnp.float32
    )


def dot(left, right):
    return jnp.dot(left, right, preferred_element_type=jnp.float32)


def exchange(rows):
    return lax.all_to_all(rows, AXES, split_axis=0, concat_axis=0, tiled=True)


def shards(
    features,
    cotangent,
    w_self_one,
    w_nbr_one,
    bias_one,
    w_self_two,
    w_nbr_two,
    in_count,
    send_list,
    src_slot,
    dst_slot,
    edge_count,
):
    node_dev, width = features.shape
    devices = lax.axis_size("dom") * lax.axis_size("sub")
    per_peer = send_list.shape[2]
    mirrors = devices * per_peer
    slots = node_dev + mirrors
    edges = src_slot.shape[1]
    core = lax.axis_index("sub") % 2
    swap = [(i, i ^ 1) for i in range(devices)]
    bf16 = jnp.bfloat16
    f32 = jnp.float32

    inverse = (1.0 / jnp.maximum(in_count, 1).astype(f32))[:, None]
    owners = send_list[0].reshape(-1)
    placing = (jnp.arange(node_dev, dtype=jnp.int32)[:, None] == owners[None, :]).astype(bf16)

    scaled = (cotangent.astype(f32) * inverse).astype(bf16)
    table = jnp.concatenate([features, scaled], axis=1)
    picked = tdot(placing, table).astype(bf16)
    mirrored = exchange(picked.reshape(devices, per_peer, 2 * width)).reshape(mirrors, 2 * width)

    live = jnp.arange(edges, dtype=jnp.int32) < edge_count[0]
    slot_ids = jnp.arange(slots, dtype=jnp.int32)[:, None]
    from_hot = (jnp.where(live, src_slot[0], -1)[None, :] == slot_ids).astype(bf16)
    into_hot = (dst_slot[0][None, :] == slot_ids).astype(bf16)
    counts = dot_transposed(into_hot, from_hot).astype(bf16)

    forward = dot(counts[:, :node_dev], features) + dot(counts[:, node_dev:], mirrored[:, :width])
    backward = tdot(counts[:node_dev], scaled) + tdot(counts[node_dev:], mirrored[:, width:])
    partial_sums = jnp.concatenate([forward[node_dev:], backward[node_dev:]], axis=1).astype(bf16)
    returned = exchange(partial_sums.reshape(devices, per_peer, 2 * width)).reshape(
        mirrors, 2 * width
    )
    placed = dot(placing, returned)
    mean_one = ((forward[:node_dev] + placed[:, :width]) * inverse).astype(bf16)
    pulled = (backward[:node_dev] + placed[:, width:]).astype(bf16)

    z_one = dot(features, w_self_one) + dot(mean_one, w_nbr_one) + bias_one
    sigmoid = jax.nn.sigmoid(z_one)
    h_one = (z_one * sigmoid).astype(bf16)
    grad_h_one = dot_transposed(cotangent, w_self_two) + dot_transposed(pulled, w_nbr_two)
    grad_z_one = (grad_h_one * (sigmoid * (1.0 + z_one * (1.0 - sigmoid)))).astype(bf16)
    message_one = (dot_transposed(grad_z_one, w_nbr_one) * inverse).astype(bf16)

    weights = jnp.concatenate(
        [
            tdot(features, grad_z_one),
            tdot(mean_one, grad_z_one),
            tdot(h_one, cotangent),
            tdot(h_one, pulled),
        ],
        axis=0,
    )
    half = weights.shape[0] // 2
    chunk = half // devices
    sent_half = lax.dynamic_slice_in_dim(weights, (1 - core) * half, half).astype(bf16)
    own_half = lax.dynamic_slice_in_dim(weights, core * half, half)
    chip_half = (own_half + lax.ppermute(sent_half, AXES, swap).astype(f32)).astype(bf16)
    bias_sum = jnp.sum(grad_z_one.astype(f32), axis=0, keepdims=True)
    bias_high = bias_sum.astype(bf16)
    bias_low = (bias_sum - bias_high.astype(f32)).astype(bf16)
    bias_rows = jnp.concatenate([bias_high, bias_low, jnp.zeros((2, width), bf16)], axis=0)

    picked = tdot(placing, message_one).astype(bf16)
    payload = jnp.concatenate(
        [
            picked.reshape(devices, per_peer, width),
            jnp.broadcast_to(bias_rows[None], (devices, 4, width)),
            chip_half.reshape(devices, chunk, width),
        ],
        axis=1,
    )
    payload = exchange(payload)
    mirrored = payload[:, :per_peer].reshape(mirrors, width)
    bias_parts = payload[:, per_peer : per_peer + 2].astype(f32)
    chunk_parts = payload[:, per_peer + 4 :].astype(f32)

    norm_factor = f32(node_dev * devices) ** (-0.5)
    grad_bias = jnp.sum(bias_parts, axis=(0, 1)) * norm_factor
    owned = (
        jnp.sum(chunk_parts.reshape(devices // 2, 2, chunk, width), axis=0) * norm_factor
    ).astype(bf16)

    backward = tdot(counts[:node_dev], message_one) + tdot(counts[node_dev:], mirrored)
    payload = jnp.concatenate(
        [
            backward[node_dev:].astype(bf16).reshape(devices, per_peer, width),
            jnp.zeros((devices, 4, width), bf16),
            jnp.broadcast_to(owned[None], (devices // 2, 2, chunk, width)).reshape(
                devices, chunk, width
            ),
        ],
        axis=1,
    )
    payload = exchange(payload)
    returned = payload[:, :per_peer].reshape(mirrors, width)
    mine = payload[:, per_peer + 4 :].reshape(half, width)
    other = lax.ppermute(mine, AXES, swap)
    first = jnp.where(core == 0, mine, other)
    second = jnp.where(core == 0, other, mine)
    grad_weights = (
        jnp.concatenate([first, second], axis=0).astype(f32).reshape(4, width, width)
    )
    grad_features = (
        dot_transposed(grad_z_one, w_self_one) + backward[:node_dev] + dot(placing, returned)
    ).astype(bf16)
    return (grad_features, grad_weights, grad_bias)


def solution(mesh):
    by_device = P(AXES)
    return jax.shard_map(
        shards,
        mesh=mesh,
        in_specs=(
            P(AXES, None),
            P(AXES, None),
            P(),
            P(),
            P(),
            P(),
            P(),
            by_device,
            P(AXES, None, None),
            P(AXES, None),
            P(AXES, None),
            by_device,
        ),
        out_specs=(P(AXES, None), P(), P()),
        check_vma=False,
    )
```

```python
import functools

import jax
import jax.numpy as jnp
from jax import lax
from jax.experimental import pallas as pl
from jax.experimental.pallas import tpu as pltpu
from jax.sharding import PartitionSpec as P

AXES = ("dom", "sub")
BF16 = jnp.bfloat16
F8 = jnp.float8_e4m3fn
F32 = jnp.float32
I32 = jnp.int32
LANES = 128
BLOCK = 256
VMEM_LIMIT = 24 * 2**20


def tdot(left, right):
    return lax.dot_general(left, right, (((0,), (0,)), ((), ())), preferred_element_type=F32)


def dot_transposed(left, right):
    return lax.dot_general(left, right, (((1,), (1,)), ((), ())), preferred_element_type=F32)


def dot(left, right):
    return jnp.dot(left, right, preferred_element_type=F32)


def exchange(rows):
    return lax.all_to_all(rows, AXES, split_axis=0, concat_axis=0, tiled=True)


def run(kernel, name, outs, vmem=(), hbm=(), smem=(), scratch=(), flops=0, moved=0):
    in_place = pl.BlockSpec(memory_space=pltpu.VMEM)
    remote = pl.BlockSpec(memory_space=pltpu.HBM)
    return pl.pallas_call(
        kernel,
        out_shape=tuple(outs),
        in_specs=[pl.BlockSpec(memory_space=pltpu.SMEM)] * len(smem)
        + [remote] * len(hbm)
        + [in_place] * len(vmem),
        out_specs=tuple(remote if out.memory_space == pltpu.HBM else in_place for out in outs),
        scratch_shapes=tuple(scratch),
        compiler_params=pltpu.CompilerParams(vmem_limit_bytes=VMEM_LIMIT),
        cost_estimate=pl.CostEstimate(flops=flops, bytes_accessed=moved, transcendentals=0),
        name=name,
    )(
        *smem,
        *[pltpu.with_memory_space_constraint(arg, pltpu.HBM) for arg in hbm],
        *[pltpu.with_memory_space_constraint(arg, pltpu.VMEM) for arg in vmem],
    )


def staged(*arrays):
    buffers = [pltpu.VMEM(array.shape, array.dtype) for array in arrays]
    return buffers + [pltpu.SemaphoreType.DMA((len(arrays),))]


def start_all(sources, buffers, semaphores):
    copies = [
        pltpu.make_async_copy(source, buffer, semaphores.at[index])
        for index, (source, buffer) in enumerate(zip(sources, buffers))
    ]
    for copy in copies:
        copy.start()
    return copies


def iota(shape, dim):
    return lax.broadcasted_iota(I32, shape, dim)


def one_hot(mask, dtype):
    return jnp.where(mask, 1.0, 0.0).astype(dtype)


def inverse_columns(in_count):
    return (1.0 / jnp.maximum(in_count[...], 1).astype(F32)).T


def send(array, out, semaphore):
    copy = pltpu.make_async_copy(array, out, semaphore)
    copy.start()
    copy.wait()


def pick_rows(
    features_at,
    cotangent_at,
    in_count_at,
    sent_at,
    payload,
    scaled,
    picking,
    features,
    cotangent,
    in_count,
    sent,
    semaphores,
    rows_out,
    out_semaphore,
):
    node_dev, width = features.shape
    per_peer, devices = sent.shape
    mirrors = devices * per_peer
    copies = start_all(
        [sent_at, in_count_at, cotangent_at, features_at],
        [sent, in_count, cotangent, features],
        semaphores,
    )
    copies[0].wait()
    spread_out = one_hot(
        iota((mirrors, devices), 0) // per_peer == iota((mirrors, devices), 1), BF16
    )
    high = dot_transposed(spread_out, (sent[...] >> 5).astype(F32).astype(BF16))
    low = dot_transposed(spread_out, (sent[...] & 31).astype(F32).astype(BF16))
    within = iota((mirrors, per_peer), 0) % per_peer == iota((mirrors, per_peer), 1)
    owner = jnp.sum(jnp.where(within, high * 32.0 + low, 0.0), axis=1, keepdims=True).astype(I32)
    picks = one_hot(iota((mirrors, node_dev), 1) == owner, BF16)
    picking[...] = picks
    copies[1].wait()
    columns = inverse_columns(in_count)
    copies[2].wait()
    for block in range(node_dev // LANES):
        rows = pl.ds(block * LANES, LANES)
        scaled[rows, :] = (
            cotangent[rows, :].astype(F32) * columns[:, block : block + 1]
        ).astype(BF16)
    back = dot(picks, scaled[...])
    copies[3].wait()
    front = dot(picks, features[...])
    rows_out[...] = (
        jnp.concatenate([front, back], axis=1)
        .reshape(devices, per_peer, 2 * width)
        .astype(BF16)
    )
    send(rows_out, payload, out_semaphore)


def count_edges(
    edge_count,
    sources_at,
    targets_at,
    features_at,
    scaled,
    counts_out,
    mirror_out,
    partial_out,
    sources,
    targets,
    features,
    semaphores,
    from_hot,
    into_hot,
    counts,
    out_semaphores,
):
    node_dev, width = features.shape
    slots, edges = into_hot.shape
    copies = start_all(
        [sources_at, targets_at, features_at], [sources, targets, features], semaphores
    )
    copies[0].wait()
    edge_ids = iota(sources.shape, 0) * LANES + iota(sources.shape, 1)
    source_columns = jnp.where(edge_ids < edge_count[0], sources[...], -1).T
    lane_ids = iota((LANES, slots), 1)
    for block in range(edges // LANES):
        from_hot[pl.ds(block * LANES, LANES), :] = one_hot(
            lane_ids == source_columns[:, block : block + 1], F8
        )
    copies[1].wait()
    row_ids = iota((LANES, LANES), 0)
    sends = []
    for start in range(0, slots, BLOCK):
        size = min(BLOCK, slots - start)
        for block in range(edges // LANES):
            target_row = targets[block : block + 1, :]
            for part in range(start, start + size, LANES):
                into_hot[pl.ds(part, LANES), pl.ds(block * LANES, LANES)] = one_hot(
                    row_ids + part == target_row, F8
                )
        rows = pl.ds(start, size)
        counts[rows, :] = dot(into_hot[rows, :], from_hot[...]).astype(BF16)
        copy = pltpu.make_async_copy(
            counts.at[rows], counts_out.at[rows], out_semaphores.at[start // BLOCK]
        )
        copy.start()
        sends.append(copy)
    copies[2].wait()
    mirror_out[...] = counts[node_dev:, node_dev:]
    partial_out[:, :width] = dot(counts[node_dev:, :node_dev], features[...])
    partial_out[:, width:] = tdot(counts[:node_dev, node_dev:], scaled[...])
    for copy in sends:
        copy.wait()


def mirror_sums(partial_in, mirror_counts, mirrored, payload, rows_out, out_semaphore):
    width = partial_in.shape[1] // 2
    received = mirrored[...]
    front = partial_in[:, :width] + dot(mirror_counts[...], received[:, :width])
    back = partial_in[:, width:] + tdot(mirror_counts[...], received[:, width:])
    rows_out[...] = (
        jnp.concatenate([front, back], axis=1).reshape(rows_out.shape).astype(BF16)
    )
    send(rows_out, payload, out_semaphore)


def local_sums(
    counts_at, features_at, scaled, mirrored, forward, backward, counts, features, semaphores
):
    node_dev, width = features.shape
    slots = counts.shape[0]
    blocks = [(start, min(BLOCK, slots - start)) for start in range(0, slots, BLOCK)]
    feature_copy = pltpu.make_async_copy(features_at, features, semaphores.at[len(blocks)])
    feature_copy.start()
    copies = []
    for index, (start, size) in enumerate(blocks):
        rows = pl.ds(start, size)
        copy = pltpu.make_async_copy(counts_at.at[rows], counts.at[rows], semaphores.at[index])
        copy.start()
        copies.append(copy)
    feature_copy.wait()
    for (start, size), copy in zip(blocks, copies):
        copy.wait()
        if start < node_dev:
            rows = pl.ds(start, size)
            forward[rows, :] = dot(counts[rows, :node_dev], features[...]) + dot(
                counts[rows, node_dev:], mirrored[:, :width]
            )
    for start in range(0, node_dev, BLOCK):
        rows = pl.ds(start, BLOCK)
        backward[rows, :] = tdot(counts[:node_dev, rows], scaled[...]) + tdot(
            counts[node_dev:, rows], mirrored[:, width:]
        )


def middle(
    core,
    features_at,
    cotangent_at,
    in_count_at,
    forward,
    backward,
    returned,
    picking,
    w_self_one,
    w_nbr_one,
    bias_one,
    w_self_two,
    w_nbr_two,
    grad_z,
    sent_half,
    own_half,
    bias_rows,
    features,
    cotangent,
    in_count,
    semaphores,
    mean_one,
    h_one,
    pulled,
):
    node_dev, width = features.shape
    copies = start_all(
        [in_count_at, features_at, cotangent_at], [in_count, features, cotangent], semaphores
    )
    copies[0].wait()
    columns = inverse_columns(in_count)
    for start in range(0, node_dev, BLOCK):
        rows = pl.ds(start, BLOCK)
        placed = tdot(picking[:, rows], returned[...])
        inverse = jnp.concatenate(
            [columns[:, b : b + 1] for b in range(start // LANES, (start + BLOCK) // LANES)],
            axis=0,
        )
        mean_one[rows, :] = ((forward[rows, :] + placed[:, :width]) * inverse).astype(BF16)
        pulled[rows, :] = (backward[rows, :] + placed[:, width:]).astype(BF16)
    copies[1].wait()
    copies[2].wait()
    bias_total = jnp.zeros((1, width), F32)
    for start in range(0, node_dev, BLOCK):
        rows = pl.ds(start, BLOCK)
        z_one = (
            dot(features[rows, :], w_self_one[...])
            + dot(mean_one[rows, :], w_nbr_one[...])
            + bias_one[...]
        )
        sigmoid = 1.0 / (1.0 + jnp.exp(-z_one))
        grad_h = dot_transposed(cotangent[rows, :], w_self_two[...]) + dot_transposed(
            pulled[rows, :], w_nbr_two[...]
        )
        grad = (grad_h * (sigmoid * (1.0 + z_one * (1.0 - sigmoid)))).astype(BF16)
        h_one[rows, :] = (z_one * sigmoid).astype(BF16)
        grad_z[rows, :] = grad
        bias_total += jnp.sum(grad.astype(F32), axis=0, keepdims=True)
    bias_high = bias_total.astype(BF16)
    bias_rows[0:1, :] = bias_high
    bias_rows[1:2, :] = (bias_total - bias_high.astype(F32)).astype(BF16)
    bias_rows[2:, :] = jnp.zeros((bias_rows.shape[0] - 2, width), BF16)

    def early():
        return tdot(features[...], grad_z[...]), tdot(mean_one[...], grad_z[...])

    def late():
        return tdot(h_one[...], cotangent[...]), tdot(h_one[...], pulled[...])

    for parity, (sent, owned) in enumerate(((late, early), (early, late))):

        @pl.when(core[0] == parity)
        def _(sent=sent, owned=owned):
            top, bottom = sent()
            sent_half[:width, :] = top.astype(BF16)
            sent_half[width:, :] = bottom.astype(BF16)
            top, bottom = owned()
            own_half[:width, :] = top
            own_half[width:, :] = bottom


def messages(in_count, grad_z, w_nbr_one, picking, message_one, picked):
    node_dev, width = grad_z.shape
    columns = inverse_columns(in_count)
    for start in range(0, node_dev, BLOCK):
        rows = pl.ds(start, BLOCK)
        inverse = jnp.concatenate(
            [columns[:, b : b + 1] for b in range(start // LANES, (start + BLOCK) // LANES)],
            axis=0,
        )
        message_one[rows, :] = (
            dot_transposed(grad_z[rows, :], w_nbr_one[...]) * inverse
        ).astype(BF16)
    picked[...] = dot(picking[...], message_one[...])


def join_first(own_half, other_half, picked, bias_rows, payload, rows_out, out_semaphore):
    devices, _, width = rows_out.shape
    per_peer = picked.shape[0] // devices
    chunk = own_half.shape[0] // devices
    chip_half = own_half[...] + other_half[...].astype(F32)
    rows_out[:, :chunk, :] = chip_half.reshape(devices, chunk, width).astype(BF16)
    rows_out[:, chunk : chunk + per_peer, :] = (
        picked[...].reshape(devices, per_peer, width).astype(BF16)
    )
    rows_out[:, chunk + per_peer :, :] = jnp.broadcast_to(
        bias_rows[:4, :][None], (devices, 4, width)
    )
    send(rows_out, payload, out_semaphore)


def local_back(
    counts_at, message_one, grad_z, w_self_one, mirror_out, local_out, counts, semaphore
):
    node_dev, width = grad_z.shape
    copy = pltpu.make_async_copy(counts_at.at[pl.ds(0, node_dev)], counts, semaphore)
    copy.start()
    for start in range(0, node_dev, BLOCK):
        rows = pl.ds(start, BLOCK)
        local_out[rows, :] = dot_transposed(grad_z[rows, :], w_self_one[...])
    copy.wait()
    mirror_out[...] = tdot(counts[:, node_dev:], message_one[...])
    for start in range(0, node_dev, BLOCK):
        rows = pl.ds(start, BLOCK)
        local_out[rows, :] += tdot(counts[:, rows], message_one[...])


def join_second(
    chunk, norm_factor, received, mirror_partial, mirror_counts, payload, mirrored_out, bias_out, rows_out, out_semaphore
):
    devices, _, width = rows_out.shape
    mirrors = mirror_partial.shape[0]
    per_peer = mirrors // devices
    owned = (
        jnp.sum(
            received[:, :chunk, :].astype(F32).reshape(devices // 2, 2, chunk, width), axis=0
        )
        * norm_factor
    )
    mirrored = (
        received[:, chunk : chunk + per_peer, :].astype(F32).reshape(mirrors, width).astype(BF16)
    )
    mirrored_out[...] = mirrored
    partial_sums = mirror_partial[...] + tdot(mirror_counts[...], mirrored)
    rows_out[:, :chunk, :] = (
        jnp.broadcast_to(owned[None], (devices // 2, 2, chunk, width))
        .reshape(devices, chunk, width)
        .astype(BF16)
    )
    rows_out[:, chunk : chunk + per_peer, :] = partial_sums.reshape(
        devices, per_peer, width
    ).astype(BF16)
    rows_out[:, chunk + per_peer :, :] = jnp.zeros((devices, 4, width), BF16)
    copy = pltpu.make_async_copy(rows_out, payload, out_semaphore)
    copy.start()
    bias_out[...] = (
        jnp.sum(
            received[:, chunk + per_peer : chunk + per_peer + 2, :].astype(F32),
            axis=(0, 1),
            keepdims=True,
        ).reshape(1, width)
        * norm_factor
    )
    copy.wait()


def shards(
    features,
    cotangent,
    w_self_one,
    w_nbr_one,
    bias_one,
    w_self_two,
    w_nbr_two,
    in_count,
    send_list,
    src_slot,
    dst_slot,
    edge_count,
):
    node_dev, width = features.shape
    devices = lax.axis_size("dom") * lax.axis_size("sub")
    per_peer = send_list.shape[2]
    mirrors = devices * per_peer
    slots = node_dev + mirrors
    edges = src_slot.shape[1]
    core = lax.axis_index("sub") % 2
    swap = [(i, i ^ 1) for i in range(devices)]
    in_count = in_count.reshape(-1, LANES)
    sent = send_list[0].T
    sources = src_slot.reshape(-1, LANES)
    targets = dst_slot.reshape(-1, LANES)
    blocks = -(-slots // BLOCK)

    payload_shape = (devices, per_peer, 2 * width)
    payload, scaled, picking = run(
        pick_rows,
        "pick_rows",
        [
            pltpu.HBM(payload_shape, BF16),
            pltpu.VMEM((node_dev, width), BF16),
            pltpu.VMEM((mirrors, node_dev), BF16),
        ],
        hbm=[features, cotangent, in_count, sent],
        scratch=staged(features, cotangent, in_count, sent)
        + [pltpu.VMEM(payload_shape, BF16), pltpu.SemaphoreType.DMA],
        flops=4 * mirrors * node_dev * width,
    )
    mirrored = exchange(payload).reshape(mirrors, 2 * width)

    counts, mirror_counts, partial_sums = run(
        count_edges,
        "count_edges",
        [
            pltpu.HBM((slots, slots), BF16),
            pltpu.VMEM((mirrors, mirrors), BF16),
            pltpu.VMEM((mirrors, 2 * width), F32),
        ],
        smem=[edge_count],
        hbm=[sources, targets, features],
        vmem=[scaled],
        scratch=staged(sources, targets, features)
        + [
            pltpu.VMEM((edges, slots), F8),
            pltpu.VMEM((slots, edges), F8),
            pltpu.VMEM((slots, slots), BF16),
            pltpu.SemaphoreType.DMA((blocks,)),
        ],
        flops=2 * slots * edges * slots,
    )
    (payload,) = run(
        mirror_sums,
        "mirror_sums",
        [pltpu.HBM(payload_shape, BF16)],
        vmem=[partial_sums, mirror_counts, mirrored],
        scratch=[pltpu.VMEM(payload_shape, BF16), pltpu.SemaphoreType.DMA],
        flops=4 * mirrors * mirrors * width,
    )
    returned = exchange(payload).reshape(mirrors, 2 * width)
    forward, backward = run(
        local_sums,
        "local_sums",
        [pltpu.VMEM((node_dev, width), F32)] * 2,
        hbm=[counts, features],
        vmem=[scaled, mirrored],
        scratch=[
            pltpu.VMEM((slots, slots), BF16),
            pltpu.VMEM((node_dev, width), BF16),
            pltpu.SemaphoreType.DMA((blocks + 1,)),
        ],
        flops=4 * node_dev * slots * width,
    )

    half = 2 * width
    chunk = half // devices
    grad_z_one, sent_half, own_half, bias_rows = run(
        middle,
        "middle",
        [
            pltpu.VMEM((node_dev, width), BF16),
            pltpu.VMEM((half, width), BF16),
            pltpu.VMEM((half, width), F32),
            pltpu.VMEM((16, width), BF16),
        ],
        smem=[core.reshape(1)],
        hbm=[features, cotangent, in_count],
        vmem=[
            forward,
            backward,
            returned,
            picking,
            w_self_one,
            w_nbr_one,
            bias_one.reshape(1, -1),
            w_self_two,
            w_nbr_two,
        ],
        scratch=staged(features, cotangent, in_count)
        + [pltpu.VMEM((node_dev, width), BF16)] * 3,
        flops=24 * node_dev * width * width,
    )
    other_half = lax.ppermute(sent_half, AXES, swap)
    message_one, picked = run(
        messages,
        "messages",
        [pltpu.VMEM((node_dev, width), BF16), pltpu.VMEM((mirrors, width), F32)],
        vmem=[in_count, grad_z_one, w_nbr_one, picking],
        flops=2 * node_dev * width * width,
    )

    payload_shape = (devices, chunk + per_peer + 4, width)
    (payload,) = run(
        join_first,
        "join_first",
        [pltpu.HBM(payload_shape, BF16)],
        vmem=[own_half, other_half, picked, bias_rows],
        scratch=[pltpu.VMEM(payload_shape, BF16), pltpu.SemaphoreType.DMA],
    )
    received = exchange(payload)
    mirror_back, local_grad = run(
        local_back,
        "local_back",
        [pltpu.VMEM((mirrors, width), F32), pltpu.VMEM((node_dev, width), F32)],
        hbm=[counts],
        vmem=[message_one, grad_z_one, w_self_one],
        scratch=[pltpu.VMEM((node_dev, slots), BF16), pltpu.SemaphoreType.DMA],
        flops=2 * node_dev * (slots + width) * width,
    )
    norm_factor = float(node_dev * devices) ** -0.5
    payload, mirrored, grad_bias = run(
        functools.partial(join_second, chunk, norm_factor),
        "join_second",
        [
            pltpu.HBM(payload_shape, BF16),
            pltpu.VMEM((mirrors, width), BF16),
            pltpu.VMEM((1, width), F32),
        ],
        vmem=[received, mirror_back, mirror_counts],
        scratch=[pltpu.VMEM(payload_shape, BF16), pltpu.SemaphoreType.DMA],
    )
    received = exchange(payload)
    local_grad = local_grad + tdot(counts[node_dev:, :node_dev], mirrored)
    returned = received[:, chunk : chunk + per_peer].reshape(mirrors, width)
    mine = received[:, :chunk].reshape(half, width)
    other = lax.ppermute(mine, AXES, swap)
    first = jnp.where(core == 0, mine, other)
    second = jnp.where(core == 0, other, mine)
    grad_weights = jnp.concatenate([first, second], axis=0).astype(F32).reshape(4, width, width)
    grad_features = (local_grad + tdot(picking, returned)).astype(BF16)
    return (grad_features, grad_weights, grad_bias.reshape(width))


def solution(mesh):
    by_device = P(AXES)
    return jax.shard_map(
        shards,
        mesh=mesh,
        in_specs=(
            P(AXES, None),
            P(AXES, None),
            P(),
            P(),
            P(),
            P(),
            P(),
            by_device,
            P(AXES, None, None),
            P(AXES, None),
            P(AXES, None),
            by_device,
        ),
        out_specs=(P(AXES, None), P(), P()),
        check_vma=False,
    )
```

```python
import functools

import jax
import jax.numpy as jnp
from jax import lax
from jax.experimental import pallas as pl
from jax.experimental.pallas import tpu as pltpu
from jax.sharding import PartitionSpec as P

AXES = ("dom", "sub")
BF16 = jnp.bfloat16
F8 = jnp.float8_e4m3fn
F32 = jnp.float32
I32 = jnp.int32
I16 = jnp.int16
LANES = 128
BLOCK = 256
VMEM_LIMIT = 24 * 2**20


def tdot(left, right):
    return lax.dot_general(left, right, (((0,), (0,)), ((), ())), preferred_element_type=F32)


def dot_transposed(left, right):
    return lax.dot_general(left, right, (((1,), (1,)), ((), ())), preferred_element_type=F32)


def dot(left, right):
    return jnp.dot(left, right, preferred_element_type=F32)


def exchange(rows):
    return lax.all_to_all(rows, AXES, split_axis=0, concat_axis=0, tiled=True)


def run(kernel, name, outs, vmem=(), hbm=(), smem=(), scratch=(), flops=0, moved=0, aliases=None):
    in_place = pl.BlockSpec(memory_space=pltpu.VMEM)
    remote = pl.BlockSpec(memory_space=pltpu.HBM)
    return pl.pallas_call(
        kernel,
        out_shape=tuple(outs),
        in_specs=[pl.BlockSpec(memory_space=pltpu.SMEM)] * len(smem)
        + [remote] * len(hbm)
        + [in_place] * len(vmem),
        out_specs=tuple(remote if out.memory_space == pltpu.HBM else in_place for out in outs),
        scratch_shapes=tuple(scratch),
        compiler_params=pltpu.CompilerParams(vmem_limit_bytes=VMEM_LIMIT),
        cost_estimate=pl.CostEstimate(flops=flops, bytes_accessed=moved, transcendentals=0),
        input_output_aliases=aliases or {},
        name=name,
    )(
        *smem,
        *[pltpu.with_memory_space_constraint(arg, pltpu.HBM) for arg in hbm],
        *[pltpu.with_memory_space_constraint(arg, pltpu.VMEM) for arg in vmem],
    )


def staged_for(count, *arrays):
    buffers = [pltpu.VMEM(array.shape, array.dtype) for array in arrays]
    return buffers + [pltpu.SemaphoreType.DMA((count,))]


def start_all(sources, buffers, semaphores):
    copies = [
        pltpu.make_async_copy(source, buffer, semaphores.at[index])
        for index, (source, buffer) in enumerate(zip(sources, buffers))
    ]
    for copy in copies:
        copy.start()
    return copies


def iota(shape, dim, dtype=I32):
    return lax.broadcasted_iota(dtype, shape, dim)


def one_hot(mask, dtype):
    return jnp.where(mask, 1.0, 0.0).astype(dtype)


def edge_hot(mask):
    return jnp.where(mask, jnp.ones(mask.shape, BF16), jnp.zeros(mask.shape, BF16)).astype(F8)


def by_peer(rows, devices):
    return rows.reshape(devices, rows.shape[0] // devices, rows.shape[1]).astype(BF16)


def by_row(parts):
    return parts.astype(F32).reshape(parts.shape[0] * parts.shape[1], parts.shape[2])


def inverse_columns(in_count):
    return (1.0 / jnp.maximum(in_count[...], 1).astype(F32)).T


def send(array, out, semaphore):
    copy = pltpu.make_async_copy(array, out, semaphore)
    copy.start()
    copy.wait()


def pick_rows(
    edge_count,
    features_at,
    cotangent_at,
    in_count_at,
    sent_at,
    sources_at,
    targets_at,
    payload,
    scaled,
    picking,
    source_columns,
    targets,
    features,
    cotangent,
    in_count,
    sent,
    sources,
    semaphores,
    rows_out,
    out_semaphore,
):
    node_dev, width = features.shape
    per_peer, devices = sent.shape
    mirrors = devices * per_peer
    copies = start_all(
        [sent_at, in_count_at, cotangent_at, features_at, sources_at, targets_at],
        [sent, in_count, cotangent, features, sources, targets],
        semaphores,
    )
    copies[0].wait()
    spread_out = one_hot(
        iota((mirrors, devices), 0) // per_peer == iota((mirrors, devices), 1), BF16
    )
    high = dot_transposed(spread_out, (sent[...] >> 5).astype(F32).astype(BF16))
    low = dot_transposed(spread_out, (sent[...] & 31).astype(F32).astype(BF16))
    within = iota((mirrors, per_peer), 0) % per_peer == iota((mirrors, per_peer), 1)
    owner = jnp.sum(jnp.where(within, high * 32.0 + low, 0.0), axis=1, keepdims=True).astype(I32)
    picked = iota((mirrors, node_dev), 1) == owner
    picks = one_hot(picked, BF16)
    picking[...] = picks
    copies[1].wait()
    inverse_rows = 1.0 / jnp.maximum(in_count[...], 1).astype(F32)
    owner_inverse = jnp.zeros((mirrors, LANES), F32)
    for block in range(node_dev // LANES):
        lanes = slice(block * LANES, (block + 1) * LANES)
        owner_inverse += jnp.where(picked[:, lanes], inverse_rows[block : block + 1, :], 0.0)
    owner_inverse = jnp.sum(owner_inverse, axis=1, keepdims=True)
    copies[2].wait()
    back = dot(picks, cotangent[...]) * owner_inverse
    rows_out[:, :, width:] = by_peer(back, devices)
    copies[3].wait()
    rows_out[:, :, :width] = by_peer(dot(picks, features[...]), devices)
    out_copy = pltpu.make_async_copy(rows_out, payload, out_semaphore)
    out_copy.start()
    columns = inverse_rows.T
    for block in range(node_dev // LANES):
        rows = pl.ds(block * LANES, LANES)
        scaled[rows, :] = (
            cotangent[rows, :].astype(F32) * columns[:, block : block + 1]
        ).astype(BF16)
    copies[4].wait()
    edge_ids = iota(sources.shape, 0) * LANES + iota(sources.shape, 1)
    source_columns[...] = jnp.where(edge_ids < edge_count[0], sources[...], -1).T
    copies[5].wait()
    out_copy.wait()


def count_edges(
    features_at,
    scaled,
    source_columns,
    targets,
    counts_out,
    mirror_out,
    partial_out,
    features,
    semaphore,
    from_hot,
    into_hot,
    counts,
    out_semaphores,
):
    node_dev, width = features.shape
    slots, edges = into_hot.shape
    feature_copy = pltpu.make_async_copy(features_at, features, semaphore)
    feature_copy.start()
    lane_ids = iota((LANES, slots), 1, I16)
    for block in range(edges // LANES):
        column = jnp.broadcast_to(source_columns[:, block : block + 1], (LANES, LANES)).astype(I16)
        column = jnp.concatenate([column] * (slots // LANES), axis=1)
        from_hot[pl.ds(block * LANES, LANES), :] = edge_hot(lane_ids == column)
    row_ids = iota((LANES, LANES), 0, I16)
    target_rows = targets[...].astype(I16)
    sends = []
    for start in range(0, slots, BLOCK):
        size = min(BLOCK, slots - start)
        for block in range(edges // LANES):
            target_row = target_rows[block : block + 1, :]
            for part in range(start, start + size, LANES):
                into_hot[pl.ds(part, LANES), pl.ds(block * LANES, LANES)] = edge_hot(
                    row_ids + jnp.int16(part) == target_row
                )
        rows = pl.ds(start, size)
        counts[rows, :] = dot(into_hot[rows, :], from_hot[...]).astype(BF16)
        copy = pltpu.make_async_copy(
            counts.at[rows], counts_out.at[rows], out_semaphores.at[start // BLOCK]
        )
        copy.start()
        sends.append(copy)
    feature_copy.wait()
    mirror_out[...] = counts[node_dev:, node_dev:]
    partial_out[:, :width] = dot(counts[node_dev:, :node_dev], features[...])
    partial_out[:, width:] = tdot(counts[:node_dev, node_dev:], scaled[...])
    for copy in sends:
        copy.wait()


def mirror_sums(partial_in, mirror_counts, mirrored, payload, rows_out, out_semaphore):
    devices, _, columns = rows_out.shape
    width = columns // 2
    received = mirrored[...]
    front = partial_in[:, :width] + dot(mirror_counts[...], received[:, :width])
    back = partial_in[:, width:] + tdot(mirror_counts[...], received[:, width:])
    rows_out[:, :, :width] = by_peer(front, devices)
    rows_out[:, :, width:] = by_peer(back, devices)
    send(rows_out, payload, out_semaphore)


def local_sums(
    counts_at, features_at, scaled, mirrored, forward, backward, counts, features, semaphores
):
    node_dev, width = features.shape
    slots = counts.shape[0]
    blocks = [(start, min(BLOCK, slots - start)) for start in range(0, slots, BLOCK)]
    feature_copy = pltpu.make_async_copy(features_at, features, semaphores.at[len(blocks)])
    feature_copy.start()
    copies = []
    for index, (start, size) in enumerate(blocks):
        rows = pl.ds(start, size)
        copy = pltpu.make_async_copy(counts_at.at[rows], counts.at[rows], semaphores.at[index])
        copy.start()
        copies.append(copy)
    feature_copy.wait()
    for (start, size), copy in zip(blocks, copies):
        copy.wait()
        if start < node_dev:
            rows = pl.ds(start, size)
            forward[rows, :] = dot(counts[rows, :node_dev], features[...]) + dot(
                counts[rows, node_dev:], mirrored[:, :width]
            )
    for start in range(0, node_dev, BLOCK):
        rows = pl.ds(start, BLOCK)
        backward[rows, :] = tdot(counts[:node_dev, rows], scaled[...]) + tdot(
            counts[node_dev:, rows], mirrored[:, width:]
        )


def middle(
    core,
    in_count_at,
    w_nbr_one_at,
    w_self_one_at,
    bias_one_at,
    features_at,
    w_nbr_two_at,
    w_self_two_at,
    cotangent_at,
    forward,
    backward,
    returned,
    picking,
    grad_z,
    sent_half,
    own_half,
    bias_rows,
    in_count,
    w_nbr_one,
    w_self_one,
    bias_one,
    features,
    w_nbr_two,
    w_self_two,
    cotangent,
    semaphores,
    mean_one,
    h_one,
    pulled,
    slope,
):
    node_dev, width = features.shape
    copies = start_all(
        [
            in_count_at,
            w_nbr_one_at,
            w_self_one_at,
            bias_one_at,
            features_at,
            w_nbr_two_at,
            w_self_two_at,
            cotangent_at,
        ],
        [in_count, w_nbr_one, w_self_one, bias_one, features, w_nbr_two, w_self_two, cotangent],
        semaphores,
    )
    blocks = [pl.ds(start, BLOCK) for start in range(0, node_dev, BLOCK)]
    copies[0].wait()
    columns = inverse_columns(in_count)
    for index, rows in enumerate(blocks):
        placed = tdot(picking[:, rows], returned[...])
        first = index * BLOCK // LANES
        inverse = jnp.concatenate(
            [columns[:, b : b + 1] for b in range(first, first + BLOCK // LANES)], axis=0
        )
        mean_one[rows, :] = ((forward[rows, :] + placed[:, :width]) * inverse).astype(BF16)
        pulled[rows, :] = (backward[rows, :] + placed[:, width:]).astype(BF16)
    for copy in copies[1:5]:
        copy.wait()
    for rows in blocks:
        z_one = (
            dot(features[rows, :], w_self_one[...])
            + dot(mean_one[rows, :], w_nbr_one[...])
            + bias_one[...]
        )
        sigmoid = 1.0 / (1.0 + jnp.exp(-z_one))
        h_one[rows, :] = (z_one * sigmoid).astype(BF16)
        slope[rows, :] = sigmoid * (1.0 + z_one * (1.0 - sigmoid))
    for copy in copies[5:]:
        copy.wait()
    bias_total = jnp.zeros((1, width), F32)
    for rows in blocks:
        grad_h = dot_transposed(cotangent[rows, :], w_self_two[...]) + dot_transposed(
            pulled[rows, :], w_nbr_two[...]
        )
        grad = (grad_h * slope[rows, :]).astype(BF16)
        grad_z[rows, :] = grad
        bias_total += jnp.sum(grad.astype(F32), axis=0, keepdims=True)
    bias_high = bias_total.astype(BF16).astype(F32)
    bias_low = bias_total - bias_high
    for row, part in enumerate((bias_high, bias_low)):
        for block in range(width // LANES):
            bias_rows[row * (width // LANES) + block : row * (width // LANES) + block + 1, :] = (
                part[:, block * LANES : (block + 1) * LANES]
            )

    def early():
        return tdot(features[...], grad_z[...]), tdot(mean_one[...], grad_z[...])

    def late():
        return tdot(h_one[...], cotangent[...]), tdot(h_one[...], pulled[...])

    for parity, (sent, owned) in enumerate(((late, early), (early, late))):

        @pl.when(core[0] == parity)
        def _(sent=sent, owned=owned):
            top, bottom = sent()
            sent_half[:width, :] = top.astype(BF16)
            sent_half[width:, :] = bottom.astype(BF16)
            top, bottom = owned()
            own_half[:width, :] = top
            own_half[width:, :] = bottom


def messages(in_count, grad_z, w_nbr_one, picking, message_one, picked):
    node_dev, width = grad_z.shape
    columns = inverse_columns(in_count)
    for start in range(0, node_dev, BLOCK):
        rows = pl.ds(start, BLOCK)
        inverse = jnp.concatenate(
            [columns[:, b : b + 1] for b in range(start // LANES, (start + BLOCK) // LANES)],
            axis=0,
        )
        message_one[rows, :] = (
            dot_transposed(grad_z[rows, :], w_nbr_one[...]) * inverse
        ).astype(BF16)
    picked[...] = dot(picking[...], message_one[...])


def join_first(own_half, other_half, picked, bias_rows, payload, rows_out, out_semaphore):
    devices, per_peer, _ = rows_out.shape
    mirrors, width = picked.shape
    groups = own_half.shape[0] // mirrors
    rows_out[:, :, :width] = by_peer(picked[...], devices)
    for group in range(groups):
        rows = pl.ds(group * mirrors, mirrors)
        rows_out[:, :, (group + 1) * width : (group + 2) * width] = by_peer(
            own_half[rows, :] + other_half[rows, :].astype(F32), devices
        )
    rows_out[:, :, (groups + 1) * width :] = jnp.broadcast_to(
        bias_rows[...][None], (devices, per_peer, LANES)
    ).astype(BF16)
    send(rows_out, payload, out_semaphore)


def local_back(
    counts_at,
    message_one,
    grad_z,
    w_self_one,
    mirror_out,
    local_out,
    mirror_rows,
    counts,
    semaphores,
):
    node_dev, width = grad_z.shape
    copies = [
        pltpu.make_async_copy(counts_at.at[pl.ds(0, node_dev)], counts, semaphores.at[0]),
        pltpu.make_async_copy(
            counts_at.at[pl.ds(node_dev, mirror_rows.shape[0])], mirror_rows, semaphores.at[1]
        ),
    ]
    for copy in copies:
        copy.start()
    for start in range(0, node_dev, BLOCK):
        rows = pl.ds(start, BLOCK)
        local_out[rows, :] = dot_transposed(grad_z[rows, :], w_self_one[...])
    copies[0].wait()
    mirror_out[...] = tdot(counts[:, node_dev:], message_one[...])
    for start in range(0, node_dev, BLOCK):
        rows = pl.ds(start, BLOCK)
        local_out[rows, :] += tdot(counts[:, rows], message_one[...])
    copies[1].wait()


def join_second(
    norm_factor,
    received,
    mirror_partial,
    mirror_counts,
    payload,
    mirrored_out,
    bias_out,
    bias_total,
    semaphore,
):
    devices, per_peer, _ = payload.shape
    mirrors, width = mirror_partial.shape
    groups = payload.shape[2] // width - 1
    mirrored = by_row(received[:, :, :width]).astype(BF16)
    mirrored_out[...] = mirrored
    partial_sums = mirror_partial[...] + tdot(mirror_counts[...], mirrored)
    payload[:, :, :width] = by_peer(partial_sums, devices)
    for group in range(groups):
        lanes = slice((group + 1) * width, (group + 2) * width)
        owned = (
            jnp.sum(
                received[:, :, lanes].astype(F32).reshape(devices // 2, 2, per_peer, width), axis=0
            )
            * norm_factor
        ).astype(BF16)
        payload[:, :, lanes] = jnp.broadcast_to(
            owned[None], (devices // 2, 2, per_peer, width)
        ).reshape(devices, per_peer, width)
    sums = (
        jnp.sum(received[:, :, (groups + 1) * width :].astype(F32), axis=0) * norm_factor
    )
    parts = width // LANES
    for block in range(parts):
        bias_total[:, block * LANES : (block + 1) * LANES] = (
            sums[block : block + 1, :] + sums[parts + block : parts + block + 1, :]
        )
    send(bias_total, bias_out, semaphore)


def finish(
    core,
    received,
    mirrored,
    picking,
    mirror_rows,
    local_grad,
    features_at,
    weights_at,
    features_out,
    weights_out,
    semaphores,
):
    devices, per_peer, _ = received.shape
    node_dev, width = local_grad.shape
    mirrors = picking.shape[0]
    half = weights_out.shape[0]
    for group in range(half // mirrors):
        weights_out[pl.ds(group * mirrors, mirrors), :] = by_row(
            received[:, :, (group + 1) * width : (group + 2) * width]
        )
    mine = pl.multiple_of(core[0] * half, half)
    weights_copy = pltpu.make_async_copy(
        weights_out, weights_at.at[pl.ds(mine, half)], semaphores.at[0]
    )
    weights_copy.start()
    returned = by_row(received[:, :, :width]).astype(BF16)
    for start in range(0, node_dev, BLOCK):
        rows = pl.ds(start, BLOCK)
        features_out[rows, :] = (
            local_grad[rows, :]
            + tdot(picking[:, rows], returned)
            + tdot(mirror_rows[:, rows], mirrored[...])
        ).astype(BF16)
    features_copy = pltpu.make_async_copy(features_out, features_at, semaphores.at[1])
    features_copy.start()
    weights_copy.wait()
    features_copy.wait()


def finish_other(core, weights_in, received, weights_at, weights_out, semaphore):
    half, width = weights_out.shape
    devices, per_peer, columns = received.shape
    mirrors = devices * per_peer
    for group in range(half // mirrors):
        weights_out[pl.ds(group * mirrors, mirrors), :] = by_row(
            received[:, :, (group + 1) * width : (group + 2) * width]
        )
    other = pl.multiple_of((1 - core[0]) * half, half)
    send(weights_out, weights_at.at[pl.ds(other, half)], semaphore)


def shards(
    features,
    cotangent,
    w_self_one,
    w_nbr_one,
    bias_one,
    w_self_two,
    w_nbr_two,
    in_count,
    send_list,
    src_slot,
    dst_slot,
    edge_count,
):
    node_dev, width = features.shape
    devices = lax.axis_size("dom") * lax.axis_size("sub")
    per_peer = send_list.shape[2]
    mirrors = devices * per_peer
    slots = node_dev + mirrors
    edges = src_slot.shape[1]
    core = lax.axis_index("sub") % 2
    swap = [(i, i ^ 1) for i in range(devices)]
    in_count = in_count.reshape(-1, LANES)
    sent = send_list[0].T
    sources = src_slot.reshape(-1, LANES)
    targets = dst_slot.reshape(-1, LANES)
    blocks = -(-slots // BLOCK)

    payload_shape = (devices, per_peer, 2 * width)
    payload, scaled, picking, source_columns, targets = run(
        pick_rows,
        "pick_rows",
        [
            pltpu.HBM(payload_shape, BF16),
            pltpu.VMEM((node_dev, width), BF16),
            pltpu.VMEM((mirrors, node_dev), BF16),
            pltpu.VMEM((LANES, edges // LANES), I32),
            pltpu.VMEM(targets.shape, I32),
        ],
        smem=[edge_count],
        hbm=[features, cotangent, in_count, sent, sources, targets],
        scratch=staged_for(6, features, cotangent, in_count, sent, sources)
        + [pltpu.VMEM(payload_shape, BF16), pltpu.SemaphoreType.DMA],
        flops=4 * mirrors * node_dev * width,
    )
    mirrored = exchange(payload).reshape(mirrors, 2 * width)

    counts, mirror_counts, partial_sums = run(
        count_edges,
        "count_edges",
        [
            pltpu.HBM((slots, slots), BF16),
            pltpu.VMEM((mirrors, mirrors), BF16),
            pltpu.VMEM((mirrors, 2 * width), F32),
        ],
        hbm=[features],
        vmem=[scaled, source_columns, targets],
        scratch=[
            pltpu.VMEM((node_dev, width), BF16),
            pltpu.SemaphoreType.DMA,
            pltpu.VMEM((edges, slots), F8),
            pltpu.VMEM((slots, edges), F8),
            pltpu.VMEM((slots, slots), BF16),
            pltpu.SemaphoreType.DMA((blocks,)),
        ],
        flops=2 * slots * edges * slots,
    )
    (payload,) = run(
        mirror_sums,
        "mirror_sums",
        [pltpu.HBM(payload_shape, BF16)],
        vmem=[partial_sums, mirror_counts, mirrored],
        scratch=[pltpu.VMEM(payload_shape, BF16), pltpu.SemaphoreType.DMA],
        flops=4 * mirrors * mirrors * width,
    )
    returned = exchange(payload).reshape(mirrors, 2 * width)
    forward, backward = run(
        local_sums,
        "local_sums",
        [pltpu.VMEM((node_dev, width), F32)] * 2,
        hbm=[counts, features],
        vmem=[scaled, mirrored],
        scratch=[
            pltpu.VMEM((slots, slots), BF16),
            pltpu.VMEM((node_dev, width), BF16),
            pltpu.SemaphoreType.DMA((blocks + 1,)),
        ],
        flops=4 * node_dev * slots * width,
    )

    half = 2 * width
    loaded = [
        in_count,
        w_nbr_one,
        w_self_one,
        bias_one.reshape(1, -1),
        features,
        w_nbr_two,
        w_self_two,
        cotangent,
    ]
    grad_z_one, sent_half, own_half, bias_rows = run(
        middle,
        "middle",
        [
            pltpu.VMEM((node_dev, width), BF16),
            pltpu.VMEM((half, width), BF16),
            pltpu.VMEM((half, width), F32),
            pltpu.VMEM((2 * width // LANES, LANES), F32),
        ],
        smem=[core.reshape(1)],
        hbm=loaded,
        vmem=[forward, backward, returned, picking],
        scratch=staged_for(len(loaded), *loaded)
        + [pltpu.VMEM((node_dev, width), BF16)] * 3
        + [pltpu.VMEM((node_dev, width), F32)],
        flops=24 * node_dev * width * width,
    )
    other_half = lax.ppermute(sent_half, AXES, swap)
    message_one, picked = run(
        messages,
        "messages",
        [pltpu.VMEM((node_dev, width), BF16), pltpu.VMEM((mirrors, width), F32)],
        vmem=[in_count, grad_z_one, w_nbr_one, picking],
        flops=2 * node_dev * width * width,
    )

    columns = width * (half // mirrors + 1)
    payload_shape = (devices, per_peer, columns + LANES)
    (payload,) = run(
        join_first,
        "join_first",
        [pltpu.HBM(payload_shape, BF16)],
        vmem=[own_half, other_half, picked, bias_rows],
        scratch=[pltpu.VMEM(payload_shape, BF16), pltpu.SemaphoreType.DMA],
    )
    received = exchange(payload)
    mirror_back, local_grad, mirror_rows = run(
        local_back,
        "local_back",
        [
            pltpu.VMEM((mirrors, width), F32),
            pltpu.VMEM((node_dev, width), F32),
            pltpu.VMEM((mirrors, slots), BF16),
        ],
        hbm=[counts],
        vmem=[message_one, grad_z_one, w_self_one],
        scratch=[pltpu.VMEM((node_dev, slots), BF16), pltpu.SemaphoreType.DMA((2,))],
        flops=2 * node_dev * (slots + width) * width,
    )
    norm_factor = float(node_dev * devices) ** -0.5
    payload, mirrored, grad_bias = run(
        functools.partial(join_second, norm_factor),
        "join_second",
        [
            pltpu.VMEM((devices, per_peer, columns), BF16),
            pltpu.VMEM((mirrors, width), BF16),
            pltpu.HBM((1, width), F32),
        ],
        vmem=[received, mirror_back, mirror_counts],
        scratch=[pltpu.VMEM((1, width), F32), pltpu.SemaphoreType.DMA],
    )
    received = exchange(payload)
    other = lax.ppermute(received, AXES, swap)
    grad_features, grad_weights = run(
        finish,
        "finish",
        [pltpu.HBM((node_dev, width), BF16), pltpu.HBM((2 * half, width), F32)],
        smem=[core.reshape(1)],
        vmem=[received, mirrored, picking, mirror_rows, local_grad],
        scratch=[
            pltpu.VMEM((node_dev, width), BF16),
            pltpu.VMEM((half, width), F32),
            pltpu.SemaphoreType.DMA((2,)),
        ],
        flops=6 * node_dev * mirrors * width,
    )
    (grad_weights,) = run(
        finish_other,
        "finish_other",
        [pltpu.HBM((2 * half, width), F32)],
        smem=[core.reshape(1)],
        hbm=[grad_weights],
        vmem=[other],
        scratch=[pltpu.VMEM((half, width), F32), pltpu.SemaphoreType.DMA],
        aliases={1: 0},
    )
    return (
        grad_features,
        grad_weights.reshape(4, width, width),
        grad_bias.reshape(width),
    )


def solution(mesh):
    by_device = P(AXES)
    return jax.shard_map(
        shards,
        mesh=mesh,
        in_specs=(
            P(AXES, None),
            P(AXES, None),
            P(),
            P(),
            P(),
            P(),
            P(),
            by_device,
            P(AXES, None, None),
            P(AXES, None),
            P(AXES, None),
            by_device,
        ),
        out_specs=(P(AXES, None), P(), P()),
        check_vma=False,
    )
```

```python
import functools

import jax
import jax.numpy as jnp
from jax import lax
from jax.experimental import pallas as pl
from jax.experimental.pallas import tpu as pltpu
from jax.sharding import PartitionSpec as P

AXES = ("dom", "sub")
BF16 = jnp.bfloat16
F8 = jnp.float8_e4m3fn
F32 = jnp.float32
I32 = jnp.int32
I16 = jnp.int16
LANES = 128
BLOCK = 256
VMEM_LIMIT = 24 * 2**20


def tdot(left, right):
    return lax.dot_general(left, right, (((0,), (0,)), ((), ())), preferred_element_type=F32)


def dot_transposed(left, right):
    return lax.dot_general(left, right, (((1,), (1,)), ((), ())), preferred_element_type=F32)


def dot(left, right):
    return jnp.dot(left, right, preferred_element_type=F32)


def exchange(rows):
    return lax.all_to_all(rows, AXES, split_axis=0, concat_axis=0, tiled=True)


def run(kernel, name, outs, vmem=(), hbm=(), smem=(), scratch=(), flops=0, moved=0, aliases=None):
    in_place = pl.BlockSpec(memory_space=pltpu.VMEM)
    remote = pl.BlockSpec(memory_space=pltpu.HBM)
    return pl.pallas_call(
        kernel,
        out_shape=tuple(outs),
        in_specs=[pl.BlockSpec(memory_space=pltpu.SMEM)] * len(smem)
        + [remote] * len(hbm)
        + [in_place] * len(vmem),
        out_specs=tuple(remote if out.memory_space == pltpu.HBM else in_place for out in outs),
        scratch_shapes=tuple(scratch),
        compiler_params=pltpu.CompilerParams(vmem_limit_bytes=VMEM_LIMIT),
        cost_estimate=pl.CostEstimate(flops=flops, bytes_accessed=moved, transcendentals=0),
        input_output_aliases=aliases or {},
        name=name,
    )(
        *smem,
        *[pltpu.with_memory_space_constraint(arg, pltpu.HBM) for arg in hbm],
        *[pltpu.with_memory_space_constraint(arg, pltpu.VMEM) for arg in vmem],
    )


def staged_for(count, *arrays):
    buffers = [pltpu.VMEM(array.shape, array.dtype) for array in arrays]
    return buffers + [pltpu.SemaphoreType.DMA((count,))]


def start_all(sources, buffers, semaphores):
    copies = [
        pltpu.make_async_copy(source, buffer, semaphores.at[index])
        for index, (source, buffer) in enumerate(zip(sources, buffers))
    ]
    for copy in copies:
        copy.start()
    return copies


def iota(shape, dim, dtype=I32):
    return lax.broadcasted_iota(dtype, shape, dim)


def one_hot(mask, dtype):
    return jnp.where(mask, 1.0, 0.0).astype(dtype)


def edge_hot(mask):
    return jnp.where(mask, jnp.ones(mask.shape, BF16), jnp.zeros(mask.shape, BF16)).astype(F8)


def by_peer(rows, devices):
    return rows.reshape(devices, rows.shape[0] // devices, rows.shape[1]).astype(BF16)


def by_row(parts):
    return parts.astype(F32).reshape(parts.shape[0] * parts.shape[1], parts.shape[2])


def inverse_columns(in_count):
    return (1.0 / jnp.maximum(in_count[...], 1).astype(F32)).T


def send(array, out, semaphore):
    copy = pltpu.make_async_copy(array, out, semaphore)
    copy.start()
    copy.wait()


def pick_rows(
    edge_count,
    features_at,
    cotangent_at,
    in_count_at,
    sent_at,
    sources_at,
    targets_at,
    payload,
    picking,
    source_columns,
    targets,
    features,
    cotangent,
    in_count,
    sent,
    sources,
    semaphores,
    rows_out,
    out_semaphore,
):
    node_dev, width = features.shape
    per_peer, devices = sent.shape
    mirrors = devices * per_peer
    copies = start_all(
        [sent_at, in_count_at, cotangent_at, features_at, sources_at, targets_at],
        [sent, in_count, cotangent, features, sources, targets],
        semaphores,
    )
    copies[0].wait()
    spread_out = one_hot(
        iota((mirrors, devices), 0) // per_peer == iota((mirrors, devices), 1), BF16
    )
    high = dot_transposed(spread_out, (sent[...] >> 5).astype(F32).astype(BF16))
    low = dot_transposed(spread_out, (sent[...] & 31).astype(F32).astype(BF16))
    within = iota((mirrors, per_peer), 0) % per_peer == iota((mirrors, per_peer), 1)
    owner = jnp.sum(jnp.where(within, high * 32.0 + low, 0.0), axis=1, keepdims=True).astype(I32)
    picked = iota((mirrors, node_dev), 1) == owner
    picks = one_hot(picked, BF16)
    picking[...] = picks
    copies[1].wait()
    inverse_rows = 1.0 / jnp.maximum(in_count[...], 1).astype(F32)
    owner_inverse = jnp.zeros((mirrors, LANES), F32)
    for block in range(node_dev // LANES):
        lanes = slice(block * LANES, (block + 1) * LANES)
        owner_inverse += jnp.where(picked[:, lanes], inverse_rows[block : block + 1, :], 0.0)
    owner_inverse = jnp.sum(owner_inverse, axis=1, keepdims=True)
    copies[2].wait()
    back = dot(picks, cotangent[...]) * owner_inverse
    rows_out[:, :, width:] = by_peer(back, devices)
    copies[3].wait()
    rows_out[:, :, :width] = by_peer(dot(picks, features[...]), devices)
    out_copy = pltpu.make_async_copy(rows_out, payload, out_semaphore)
    out_copy.start()
    copies[4].wait()
    edge_ids = iota(sources.shape, 0) * LANES + iota(sources.shape, 1)
    source_columns[...] = jnp.where(edge_ids < edge_count[0], sources[...], -1).T
    copies[5].wait()
    out_copy.wait()


def count_edges(
    features_at,
    cotangent_at,
    in_count_at,
    source_columns,
    targets,
    counts_out,
    scaled_out,
    mirror_out,
    partial_out,
    features,
    cotangent,
    in_count,
    semaphores,
    scaled,
    from_hot,
    into_hot,
    counts,
    out_semaphores,
):
    node_dev, width = features.shape
    slots, edges = into_hot.shape
    loads = start_all(
        [features_at, cotangent_at, in_count_at], [features, cotangent, in_count], semaphores
    )
    lane_ids = iota((LANES, slots), 1, I16)
    for block in range(edges // LANES):
        column = jnp.broadcast_to(source_columns[:, block : block + 1], (LANES, LANES)).astype(I16)
        column = jnp.concatenate([column] * (slots // LANES), axis=1)
        from_hot[pl.ds(block * LANES, LANES), :] = edge_hot(lane_ids == column)
    row_ids = iota((LANES, LANES), 0, I16)
    target_rows = targets[...].astype(I16)
    sends = []
    for start in range(0, slots, BLOCK):
        size = min(BLOCK, slots - start)
        for block in range(edges // LANES):
            target_row = target_rows[block : block + 1, :]
            for part in range(start, start + size, LANES):
                into_hot[pl.ds(part, LANES), pl.ds(block * LANES, LANES)] = edge_hot(
                    row_ids + jnp.int16(part) == target_row
                )
        rows = pl.ds(start, size)
        counts[rows, :] = dot(into_hot[rows, :], from_hot[...]).astype(BF16)
        copy = pltpu.make_async_copy(
            counts.at[rows], counts_out.at[rows], out_semaphores.at[start // BLOCK]
        )
        copy.start()
        sends.append(copy)
    for copy in loads:
        copy.wait()
    columns = inverse_columns(in_count)
    for index, start in enumerate(range(0, node_dev, BLOCK)):
        rows = pl.ds(start, BLOCK)
        scaled[rows, :] = (
            cotangent[rows, :].astype(F32) * block_inverse(columns, index)
        ).astype(BF16)
    copy = pltpu.make_async_copy(scaled, scaled_out, out_semaphores.at[len(sends)])
    copy.start()
    sends.append(copy)
    mirror_out[...] = counts[node_dev:, node_dev:]
    partial_out[:, :width] = dot(counts[node_dev:, :node_dev], features[...])
    partial_out[:, width:] = tdot(counts[:node_dev, node_dev:], scaled[...])
    for copy in sends:
        copy.wait()


def mirror_sums(partial_in, mirror_counts, mirrored, payload, rows_out, out_semaphore):
    devices, _, columns = rows_out.shape
    width = columns // 2
    received = mirrored[...]
    front = partial_in[:, :width] + dot(mirror_counts[...], received[:, :width])
    back = partial_in[:, width:] + tdot(mirror_counts[...], received[:, width:])
    rows_out[:, :, :width] = by_peer(front, devices)
    rows_out[:, :, width:] = by_peer(back, devices)
    send(rows_out, payload, out_semaphore)


def local_sums(
    counts_at,
    features_at,
    w_nbr_one_at,
    w_self_one_at,
    bias_one_at,
    in_count_at,
    scaled_at,
    mirrored,
    forward,
    features,
    w_nbr_one,
    w_self_one,
    bias_one,
    in_count,
    backward_at,
    counts,
    scaled,
    backward,
    block_semaphores,
    out_semaphores,
    semaphores,
):
    node_dev, width = features.shape
    slots = counts.shape[0]
    blocks = [(start, min(BLOCK, slots - start)) for start in range(0, slots, BLOCK)]
    loads = start_all([features_at], [features], semaphores)
    copies = []
    for index, (start, size) in enumerate(blocks):
        rows = pl.ds(start, size)
        copy = pltpu.make_async_copy(
            counts_at.at[rows], counts.at[rows], block_semaphores.at[index]
        )
        copy.start()
        copies.append(copy)
    for index, (source, buffer) in enumerate(
        (
            (scaled_at, scaled),
            (w_nbr_one_at, w_nbr_one),
            (w_self_one_at, w_self_one),
            (bias_one_at, bias_one),
            (in_count_at, in_count),
        )
    ):
        copy = pltpu.make_async_copy(source, buffer, semaphores.at[index + 1])
        copy.start()
        loads.append(copy)
    loads[0].wait()
    for (start, size), copy in zip(blocks, copies):
        copy.wait()
        if start < node_dev:
            rows = pl.ds(start, size)
            forward[rows, :] = dot(counts[rows, :node_dev], features[...]) + dot(
                counts[rows, node_dev:], mirrored[:, :width]
            )
    loads[1].wait()
    sends = []
    for index, start in enumerate(range(0, node_dev, BLOCK)):
        rows = pl.ds(start, BLOCK)
        backward[rows, :] = tdot(counts[:node_dev, rows], scaled[...]) + tdot(
            counts[node_dev:, rows], mirrored[:, width:]
        )
        copy = pltpu.make_async_copy(
            backward.at[rows], backward_at.at[rows], out_semaphores.at[index]
        )
        copy.start()
        sends.append(copy)
    for copy in loads[2:] + sends:
        copy.wait()


def block_inverse(columns, index):
    first = index * BLOCK // LANES
    return jnp.concatenate(
        [columns[:, b : b + 1] for b in range(first, first + BLOCK // LANES)], axis=0
    )


def middle(
    core,
    w_nbr_two_at,
    w_self_two_at,
    cotangent_at,
    backward_at,
    forward,
    returned,
    picking,
    features,
    w_nbr_one,
    w_self_one,
    bias_one,
    in_count,
    grad_z,
    sent_half,
    bias_rows,
    mean_one,
    h_one,
    pulled,
    cotangent,
    w_nbr_two,
    w_self_two,
    backward,
    semaphores,
    slope,
):
    node_dev, width = features.shape
    copies = start_all(
        [backward_at, w_nbr_two_at, w_self_two_at, cotangent_at],
        [backward, w_nbr_two, w_self_two, cotangent],
        semaphores,
    )
    blocks = [pl.ds(start, BLOCK) for start in range(0, node_dev, BLOCK)]
    columns = inverse_columns(in_count)
    for index, rows in enumerate(blocks):
        placed = tdot(picking[:, rows], returned[:, :width])
        mean = ((forward[rows, :] + placed) * block_inverse(columns, index)).astype(BF16)
        mean_one[rows, :] = mean
        z_one = (
            dot(features[rows, :], w_self_one[...]) + dot(mean, w_nbr_one[...]) + bias_one[...]
        )
        sigmoid = 1.0 / (1.0 + jnp.exp(-z_one))
        h_one[rows, :] = (z_one * sigmoid).astype(BF16)
        slope[rows, :] = sigmoid * (1.0 + z_one * (1.0 - sigmoid))
    for copy in copies:
        copy.wait()
    bias_total = jnp.zeros((1, width), F32)
    for rows in blocks:
        pull = (backward[rows, :] + tdot(picking[:, rows], returned[:, width:])).astype(BF16)
        pulled[rows, :] = pull
        grad_h = dot_transposed(cotangent[rows, :], w_self_two[...]) + dot_transposed(
            pull, w_nbr_two[...]
        )
        grad = (grad_h * slope[rows, :]).astype(BF16)
        grad_z[rows, :] = grad
        bias_total += jnp.sum(grad.astype(F32), axis=0, keepdims=True)
    bias_high = bias_total.astype(BF16).astype(F32)
    bias_low = bias_total - bias_high
    for row, part in enumerate((bias_high, bias_low)):
        for block in range(width // LANES):
            bias_rows[row * (width // LANES) + block : row * (width // LANES) + block + 1, :] = (
                part[:, block * LANES : (block + 1) * LANES]
            )

    @pl.when(core[0] == 0)
    def _():
        sent_half[:width, :] = tdot(h_one[...], cotangent[...]).astype(BF16)
        sent_half[width:, :] = tdot(h_one[...], pulled[...]).astype(BF16)

    @pl.when(core[0] == 1)
    def _():
        sent_half[:width, :] = tdot(features[...], grad_z[...]).astype(BF16)
        sent_half[width:, :] = tdot(mean_one[...], grad_z[...]).astype(BF16)


def messages(
    core,
    in_count,
    grad_z,
    w_nbr_one,
    picking,
    features,
    mean_one,
    h_one,
    cotangent,
    pulled,
    message_one,
    picked,
    own_half,
):
    node_dev, width = grad_z.shape
    columns = inverse_columns(in_count)
    for index, start in enumerate(range(0, node_dev, BLOCK)):
        rows = pl.ds(start, BLOCK)
        message_one[rows, :] = (
            dot_transposed(grad_z[rows, :], w_nbr_one[...]) * block_inverse(columns, index)
        ).astype(BF16)
    picked[...] = dot(picking[...], message_one[...])

    @pl.when(core[0] == 0)
    def _():
        own_half[:width, :] = tdot(features[...], grad_z[...])
        own_half[width:, :] = tdot(mean_one[...], grad_z[...])

    @pl.when(core[0] == 1)
    def _():
        own_half[:width, :] = tdot(h_one[...], cotangent[...])
        own_half[width:, :] = tdot(h_one[...], pulled[...])


def join_first(own_half, other_half, picked, bias_rows, payload, rows_out, out_semaphore):
    devices, per_peer, _ = rows_out.shape
    mirrors, width = picked.shape
    groups = own_half.shape[0] // mirrors
    rows_out[:, :, :width] = by_peer(picked[...], devices)
    for group in range(groups):
        rows = pl.ds(group * mirrors, mirrors)
        rows_out[:, :, (group + 1) * width : (group + 2) * width] = by_peer(
            own_half[rows, :] + other_half[rows, :].astype(F32), devices
        )
    rows_out[:, :, (groups + 1) * width :] = jnp.broadcast_to(
        bias_rows[...][None], (devices, per_peer, LANES)
    ).astype(BF16)
    send(rows_out, payload, out_semaphore)


def local_back(
    counts_at,
    message_one,
    grad_z,
    w_self_one,
    mirror_out,
    local_out,
    mirror_rows,
    counts,
    semaphores,
):
    node_dev, width = grad_z.shape
    copies = [
        pltpu.make_async_copy(counts_at.at[pl.ds(0, node_dev)], counts, semaphores.at[0]),
        pltpu.make_async_copy(
            counts_at.at[pl.ds(node_dev, mirror_rows.shape[0])], mirror_rows, semaphores.at[1]
        ),
    ]
    for copy in copies:
        copy.start()
    for start in range(0, node_dev, BLOCK):
        rows = pl.ds(start, BLOCK)
        local_out[rows, :] = dot_transposed(grad_z[rows, :], w_self_one[...])
    copies[0].wait()
    mirror_out[...] = tdot(counts[:, node_dev:], message_one[...])
    for start in range(0, node_dev, BLOCK):
        rows = pl.ds(start, BLOCK)
        local_out[rows, :] += tdot(counts[:, rows], message_one[...])
    copies[1].wait()


def join_second(
    norm_factor,
    received,
    mirror_partial,
    mirror_counts,
    payload,
    mirrored_out,
    bias_total,
):
    devices, per_peer, _ = payload.shape
    mirrors, width = mirror_partial.shape
    groups = payload.shape[2] // width - 1
    mirrored = by_row(received[:, :, :width]).astype(BF16)
    mirrored_out[...] = mirrored
    partial_sums = mirror_partial[...] + tdot(mirror_counts[...], mirrored)
    payload[:, :, :width] = by_peer(partial_sums, devices)
    for group in range(groups):
        lanes = slice((group + 1) * width, (group + 2) * width)
        owned = (
            jnp.sum(
                received[:, :, lanes].astype(F32).reshape(devices // 2, 2, per_peer, width), axis=0
            )
            * norm_factor
        ).astype(BF16)
        payload[:, :, lanes] = jnp.broadcast_to(
            owned[None], (devices // 2, 2, per_peer, width)
        ).reshape(devices, per_peer, width)
    sums = (
        jnp.sum(received[:, :, (groups + 1) * width :].astype(F32), axis=0) * norm_factor
    )
    parts = width // LANES
    for block in range(parts):
        bias_total[:, block * LANES : (block + 1) * LANES] = (
            sums[block : block + 1, :] + sums[parts + block : parts + block + 1, :]
        )


def finish(
    core,
    received,
    mirrored,
    picking,
    mirror_rows,
    local_grad,
    bias_total,
    features_at,
    weights_at,
    bias_at,
    features_out,
    weights_out,
    semaphores,
):
    devices, per_peer, _ = received.shape
    node_dev, width = local_grad.shape
    mirrors = picking.shape[0]
    half = weights_out.shape[0]
    for group in range(half // mirrors):
        weights_out[pl.ds(group * mirrors, mirrors), :] = by_row(
            received[:, :, (group + 1) * width : (group + 2) * width]
        )
    mine = pl.multiple_of(core[0] * half, half)
    weights_copy = pltpu.make_async_copy(
        weights_out, weights_at.at[pl.ds(mine, half)], semaphores.at[0]
    )
    weights_copy.start()
    bias_copy = pltpu.make_async_copy(bias_total, bias_at, semaphores.at[2])
    bias_copy.start()
    returned = by_row(received[:, :, :width]).astype(BF16)
    for start in range(0, node_dev, BLOCK):
        rows = pl.ds(start, BLOCK)
        features_out[rows, :] = (
            local_grad[rows, :]
            + tdot(picking[:, rows], returned)
            + tdot(mirror_rows[:, rows], mirrored[...])
        ).astype(BF16)
    features_copy = pltpu.make_async_copy(features_out, features_at, semaphores.at[1])
    features_copy.start()
    weights_copy.wait()
    bias_copy.wait()
    features_copy.wait()


def finish_other(core, weights_in, received, weights_at, weights_out, semaphore):
    half, width = weights_out.shape
    devices, per_peer, columns = received.shape
    mirrors = devices * per_peer
    for group in range(half // mirrors):
        weights_out[pl.ds(group * mirrors, mirrors), :] = by_row(
            received[:, :, (group + 1) * width : (group + 2) * width]
        )
    other = pl.multiple_of((1 - core[0]) * half, half)
    send(weights_out, weights_at.at[pl.ds(other, half)], semaphore)


def shards(
    features,
    cotangent,
    w_self_one,
    w_nbr_one,
    bias_one,
    w_self_two,
    w_nbr_two,
    in_count,
    send_list,
    src_slot,
    dst_slot,
    edge_count,
):
    node_dev, width = features.shape
    devices = lax.axis_size("dom") * lax.axis_size("sub")
    per_peer = send_list.shape[2]
    mirrors = devices * per_peer
    slots = node_dev + mirrors
    edges = src_slot.shape[1]
    core = lax.axis_index("sub") % 2
    swap = [(i, i ^ 1) for i in range(devices)]
    in_count = in_count.reshape(-1, LANES)
    sent = send_list[0].T
    sources = src_slot.reshape(-1, LANES)
    targets = dst_slot.reshape(-1, LANES)
    blocks = -(-slots // BLOCK)

    payload_shape = (devices, per_peer, 2 * width)
    payload, picking, source_columns, targets = run(
        pick_rows,
        "pick_rows",
        [
            pltpu.HBM(payload_shape, BF16),
            pltpu.VMEM((mirrors, node_dev), BF16),
            pltpu.VMEM((LANES, edges // LANES), I32),
            pltpu.VMEM(targets.shape, I32),
        ],
        smem=[edge_count],
        hbm=[features, cotangent, in_count, sent, sources, targets],
        scratch=staged_for(6, features, cotangent, in_count, sent, sources)
        + [pltpu.VMEM(payload_shape, BF16), pltpu.SemaphoreType.DMA],
        flops=4 * mirrors * node_dev * width,
    )
    mirrored = exchange(payload).reshape(mirrors, 2 * width)

    rows_bf16 = pltpu.VMEM((node_dev, width), BF16)
    rows_f32 = pltpu.VMEM((node_dev, width), F32)
    counts, scaled, mirror_counts, partial_sums = run(
        count_edges,
        "count_edges",
        [
            pltpu.HBM((slots, slots), BF16),
            pltpu.HBM((node_dev, width), BF16),
            pltpu.VMEM((mirrors, mirrors), BF16),
            pltpu.VMEM((mirrors, 2 * width), F32),
        ],
        hbm=[features, cotangent, in_count],
        vmem=[source_columns, targets],
        scratch=staged_for(3, features, cotangent, in_count)
        + [
            rows_bf16,
            pltpu.VMEM((edges, slots), F8),
            pltpu.VMEM((slots, edges), F8),
            pltpu.VMEM((slots, slots), BF16),
            pltpu.SemaphoreType.DMA((blocks + 1,)),
        ],
        flops=2 * slots * edges * slots,
    )
    (payload,) = run(
        mirror_sums,
        "mirror_sums",
        [pltpu.HBM(payload_shape, BF16)],
        vmem=[partial_sums, mirror_counts, mirrored],
        scratch=[pltpu.VMEM(payload_shape, BF16), pltpu.SemaphoreType.DMA],
        flops=4 * mirrors * mirrors * width,
    )
    returned = exchange(payload).reshape(mirrors, 2 * width)
    weight = pltpu.VMEM((width, width), BF16)
    forward, features_in, w_nbr_in, w_self_in, bias_in, in_count_in, backward = run(
        local_sums,
        "local_sums",
        [
            rows_f32,
            rows_bf16,
            weight,
            weight,
            pltpu.VMEM((1, width), F32),
            pltpu.VMEM(in_count.shape, I32),
            pltpu.HBM((node_dev, width), F32),
        ],
        hbm=[counts, features, w_nbr_one, w_self_one, bias_one.reshape(1, -1), in_count, scaled],
        vmem=[mirrored],
        scratch=[
            pltpu.VMEM((slots, slots), BF16),
            rows_bf16,
            rows_f32,
            pltpu.SemaphoreType.DMA((blocks,)),
            pltpu.SemaphoreType.DMA((node_dev // BLOCK,)),
            pltpu.SemaphoreType.DMA((6,)),
        ],
        flops=4 * node_dev * slots * width,
    )

    half = 2 * width
    grad_z_one, sent_half, bias_rows, mean_one, h_one, pulled, cotangent_in = run(
        middle,
        "middle",
        [
            rows_bf16,
            pltpu.VMEM((half, width), BF16),
            pltpu.VMEM((2 * width // LANES, LANES), F32),
            rows_bf16,
            rows_bf16,
            rows_bf16,
            rows_bf16,
        ],
        smem=[core.reshape(1)],
        hbm=[w_nbr_two, w_self_two, cotangent, backward],
        vmem=[
            forward,
            returned,
            picking,
            features_in,
            w_nbr_in,
            w_self_in,
            bias_in,
            in_count_in,
        ],
        scratch=[weight, weight, rows_f32, pltpu.SemaphoreType.DMA((4,)), rows_f32],
        flops=20 * node_dev * width * width,
    )
    other_half = lax.ppermute(sent_half, AXES, swap)
    message_one, picked, own_half = run(
        messages,
        "messages",
        [rows_bf16, pltpu.VMEM((mirrors, width), F32), pltpu.VMEM((half, width), F32)],
        smem=[core.reshape(1)],
        vmem=[
            in_count_in,
            grad_z_one,
            w_nbr_in,
            picking,
            features_in,
            mean_one,
            h_one,
            cotangent_in,
            pulled,
        ],
        flops=6 * node_dev * width * width,
    )

    columns = width * (half // mirrors + 1)
    payload_shape = (devices, per_peer, columns + LANES)
    (payload,) = run(
        join_first,
        "join_first",
        [pltpu.HBM(payload_shape, BF16)],
        vmem=[own_half, other_half, picked, bias_rows],
        scratch=[pltpu.VMEM(payload_shape, BF16), pltpu.SemaphoreType.DMA],
    )
    received = exchange(payload)
    mirror_back, local_grad, mirror_rows = run(
        local_back,
        "local_back",
        [
            pltpu.VMEM((mirrors, width), F32),
            pltpu.VMEM((node_dev, width), F32),
            pltpu.VMEM((mirrors, slots), BF16),
        ],
        hbm=[counts],
        vmem=[message_one, grad_z_one, w_self_in],
        scratch=[pltpu.VMEM((node_dev, slots), BF16), pltpu.SemaphoreType.DMA((2,))],
        flops=2 * node_dev * (slots + width) * width,
    )
    norm_factor = float(node_dev * devices) ** -0.5
    payload, mirrored, bias_total = run(
        functools.partial(join_second, norm_factor),
        "join_second",
        [
            pltpu.VMEM((devices, per_peer, columns), BF16),
            pltpu.VMEM((mirrors, width), BF16),
            pltpu.VMEM((1, width), F32),
        ],
        vmem=[received, mirror_back, mirror_counts],
    )
    received = exchange(payload)
    other = lax.ppermute(received, AXES, swap)
    grad_features, grad_weights, grad_bias = run(
        finish,
        "finish",
        [
            pltpu.HBM((node_dev, width), BF16),
            pltpu.HBM((2 * half, width), F32),
            pltpu.HBM((1, width), F32),
        ],
        smem=[core.reshape(1)],
        vmem=[received, mirrored, picking, mirror_rows, local_grad, bias_total],
        scratch=[
            pltpu.VMEM((node_dev, width), BF16),
            pltpu.VMEM((half, width), F32),
            pltpu.SemaphoreType.DMA((3,)),
        ],
        flops=6 * node_dev * mirrors * width,
    )
    (grad_weights,) = run(
        finish_other,
        "finish_other",
        [pltpu.HBM((2 * half, width), F32)],
        smem=[core.reshape(1)],
        hbm=[grad_weights],
        vmem=[other],
        scratch=[pltpu.VMEM((half, width), F32), pltpu.SemaphoreType.DMA],
        aliases={1: 0},
    )
    return (
        grad_features,
        grad_weights.reshape(4, width, width),
        grad_bias.reshape(width),
    )


def solution(mesh):
    by_device = P(AXES)
    return jax.shard_map(
        shards,
        mesh=mesh,
        in_specs=(
            P(AXES, None),
            P(AXES, None),
            P(),
            P(),
            P(),
            P(),
            P(),
            by_device,
            P(AXES, None, None),
            P(AXES, None),
            P(AXES, None),
            by_device,
        ),
        out_specs=(P(AXES, None), P(), P()),
        check_vma=False,
    )
```

```python
import functools

import jax
import jax.numpy as jnp
from jax import lax
from jax.experimental import pallas as pl
from jax.experimental.pallas import tpu as pltpu
from jax.sharding import PartitionSpec as P

AXES = ("dom", "sub")
BF16 = jnp.bfloat16
F8 = jnp.float8_e4m3fn
F32 = jnp.float32
I32 = jnp.int32
I16 = jnp.int16
LANES = 128
BLOCK = 256
ROWS = 512
VMEM_LIMIT = 24 * 2**20


def tdot(left, right):
    return lax.dot_general(left, right, (((0,), (0,)), ((), ())), preferred_element_type=F32)


def dot_transposed(left, right):
    return lax.dot_general(left, right, (((1,), (1,)), ((), ())), preferred_element_type=F32)


def dot(left, right):
    return jnp.dot(left, right, preferred_element_type=F32)


def exchange(rows):
    return lax.all_to_all(rows, AXES, split_axis=0, concat_axis=0, tiled=True)


def run(kernel, name, outs, vmem=(), hbm=(), smem=(), scratch=(), flops=0, moved=0, aliases=None):
    in_place = pl.BlockSpec(memory_space=pltpu.VMEM)
    remote = pl.BlockSpec(memory_space=pltpu.HBM)
    return pl.pallas_call(
        kernel,
        out_shape=tuple(outs),
        in_specs=[pl.BlockSpec(memory_space=pltpu.SMEM)] * len(smem)
        + [remote] * len(hbm)
        + [in_place] * len(vmem),
        out_specs=tuple(remote if out.memory_space == pltpu.HBM else in_place for out in outs),
        scratch_shapes=tuple(scratch),
        compiler_params=pltpu.CompilerParams(vmem_limit_bytes=VMEM_LIMIT),
        cost_estimate=pl.CostEstimate(flops=flops, bytes_accessed=moved, transcendentals=0),
        input_output_aliases=aliases or {},
        name=name,
    )(
        *smem,
        *[pltpu.with_memory_space_constraint(arg, pltpu.HBM) for arg in hbm],
        *[pltpu.with_memory_space_constraint(arg, pltpu.VMEM) for arg in vmem],
    )


def staged_for(count, *arrays):
    buffers = [pltpu.VMEM(array.shape, array.dtype) for array in arrays]
    return buffers + [pltpu.SemaphoreType.DMA((count,))]


def start_all(sources, buffers, semaphores):
    copies = [
        pltpu.make_async_copy(source, buffer, semaphores.at[index])
        for index, (source, buffer) in enumerate(zip(sources, buffers))
    ]
    for copy in copies:
        copy.start()
    return copies


def iota(shape, dim, dtype=I32):
    return lax.broadcasted_iota(dtype, shape, dim)


def one_hot(mask, dtype):
    return jnp.where(mask, 1.0, 0.0).astype(dtype)


def edge_hot(mask):
    return jnp.where(mask, jnp.ones(mask.shape, BF16), jnp.zeros(mask.shape, BF16)).astype(F8)


def by_peer(rows, devices):
    return rows.reshape(devices, rows.shape[0] // devices, rows.shape[1]).astype(BF16)


def by_row(parts):
    return parts.astype(F32).reshape(parts.shape[0] * parts.shape[1], parts.shape[2])


def inverse_columns(in_count):
    return (1.0 / jnp.maximum(in_count[...], 1).astype(F32)).T


def send(array, out, semaphore):
    copy = pltpu.make_async_copy(array, out, semaphore)
    copy.start()
    copy.wait()


def pick_rows(
    edge_count,
    features_at,
    cotangent_at,
    in_count_at,
    sent_at,
    sources_at,
    targets_at,
    payload,
    scaled,
    picking,
    source_columns,
    targets,
    features,
    cotangent,
    in_count,
    sent,
    sources,
    semaphores,
    rows_out,
    out_semaphore,
):
    node_dev, width = features.shape
    per_peer, devices = sent.shape
    mirrors = devices * per_peer
    copies = start_all(
        [sent_at, in_count_at, cotangent_at, features_at, sources_at, targets_at],
        [sent, in_count, cotangent, features, sources, targets],
        semaphores,
    )
    copies[0].wait()
    spread_out = one_hot(
        iota((mirrors, devices), 0) // per_peer == iota((mirrors, devices), 1), BF16
    )
    high = dot_transposed(spread_out, (sent[...] >> 5).astype(F32).astype(BF16))
    low = dot_transposed(spread_out, (sent[...] & 31).astype(F32).astype(BF16))
    within = iota((mirrors, per_peer), 0) % per_peer == iota((mirrors, per_peer), 1)
    owner = jnp.sum(jnp.where(within, high * 32.0 + low, 0.0), axis=1, keepdims=True).astype(I32)
    picked = iota((mirrors, node_dev), 1) == owner
    picks = one_hot(picked, BF16)
    picking[...] = picks
    copies[1].wait()
    inverse_rows = 1.0 / jnp.maximum(in_count[...], 1).astype(F32)
    owner_inverse = jnp.zeros((mirrors, LANES), F32)
    for block in range(node_dev // LANES):
        lanes = slice(block * LANES, (block + 1) * LANES)
        owner_inverse += jnp.where(picked[:, lanes], inverse_rows[block : block + 1, :], 0.0)
    owner_inverse = jnp.sum(owner_inverse, axis=1, keepdims=True)
    copies[2].wait()
    back = dot(picks, cotangent[...]) * owner_inverse
    rows_out[:, :, width:] = by_peer(back, devices)
    copies[3].wait()
    rows_out[:, :, :width] = by_peer(dot(picks, features[...]), devices)
    out_copy = pltpu.make_async_copy(rows_out, payload, out_semaphore)
    out_copy.start()
    columns = inverse_rows.T
    for block in range(node_dev // LANES):
        rows = pl.ds(block * LANES, LANES)
        scaled[rows, :] = (
            cotangent[rows, :].astype(F32) * columns[:, block : block + 1]
        ).astype(BF16)
    copies[4].wait()
    edge_ids = iota(sources.shape, 0) * LANES + iota(sources.shape, 1)
    source_columns[...] = jnp.where(edge_ids < edge_count[0], sources[...], -1).T
    copies[5].wait()
    out_copy.wait()


def count_edges(
    features_at,
    scaled,
    source_columns,
    targets,
    counts_out,
    scaled_out,
    mirror_out,
    partial_out,
    features,
    semaphore,
    from_hot,
    into_hot,
    counts,
    out_semaphores,
):
    node_dev, width = features.shape
    slots, edges = into_hot.shape
    feature_copy = pltpu.make_async_copy(features_at, features, semaphore)
    feature_copy.start()
    sends = [
        pltpu.make_async_copy(
            scaled, scaled_out, out_semaphores.at[out_semaphores.shape[0] - 1]
        )
    ]
    sends[0].start()
    lane_ids = iota((LANES, slots), 1, I16)
    for block in range(edges // LANES):
        column = jnp.broadcast_to(source_columns[:, block : block + 1], (LANES, LANES)).astype(I16)
        column = jnp.concatenate([column] * (slots // LANES), axis=1)
        from_hot[pl.ds(block * LANES, LANES), :] = edge_hot(lane_ids == column)
    row_ids = iota((LANES, LANES), 0, I16)
    target_rows = targets[...].astype(I16)
    for start in range(0, slots, BLOCK):
        size = min(BLOCK, slots - start)
        for block in range(edges // LANES):
            target_row = target_rows[block : block + 1, :]
            for part in range(start, start + size, LANES):
                into_hot[pl.ds(part, LANES), pl.ds(block * LANES, LANES)] = edge_hot(
                    row_ids + jnp.int16(part) == target_row
                )
        rows = pl.ds(start, size)
        counts[rows, :] = dot(into_hot[rows, :], from_hot[...]).astype(BF16)
        copy = pltpu.make_async_copy(
            counts.at[rows], counts_out.at[rows], out_semaphores.at[start // BLOCK]
        )
        copy.start()
        sends.append(copy)
    feature_copy.wait()
    mirror_out[...] = counts[node_dev:, node_dev:]
    partial_out[:, :width] = dot(counts[node_dev:, :node_dev], features[...])
    partial_out[:, width:] = tdot(counts[:node_dev, node_dev:], scaled[...])
    for copy in sends:
        copy.wait()


def mirror_sums(partial_in, mirror_counts, mirrored, payload, rows_out, out_semaphore):
    devices, _, columns = rows_out.shape
    width = columns // 2
    received = mirrored[...]
    front = partial_in[:, :width] + dot(mirror_counts[...], received[:, :width])
    back = partial_in[:, width:] + tdot(mirror_counts[...], received[:, width:])
    rows_out[:, :, :width] = by_peer(front, devices)
    rows_out[:, :, width:] = by_peer(back, devices)
    send(rows_out, payload, out_semaphore)


def local_sums(
    counts_at,
    features_at,
    scaled_at,
    mirrored,
    forward,
    features,
    backward_at,
    counts,
    scaled,
    backward,
    block_semaphores,
    out_semaphores,
    semaphores,
):
    node_dev, width = features.shape
    slots = counts.shape[0]
    blocks = [(start, min(BLOCK, slots - start)) for start in range(0, slots, BLOCK)]
    loads = start_all([scaled_at], [scaled], semaphores)
    copies = []
    for index, (start, size) in enumerate(blocks):
        rows = pl.ds(start, size)
        copy = pltpu.make_async_copy(
            counts_at.at[rows], counts.at[rows], block_semaphores.at[index]
        )
        copy.start()
        copies.append(copy)
    loads.append(pltpu.make_async_copy(features_at, features, semaphores.at[1]))
    loads[1].start()
    for copy in [loads[0]] + copies:
        copy.wait()
    sends = []
    for index, start in enumerate(range(0, node_dev, BLOCK)):
        rows = pl.ds(start, BLOCK)
        backward[rows, :] = tdot(counts[:node_dev, rows], scaled[...]) + tdot(
            counts[node_dev:, rows], mirrored[:, width:]
        )
        copy = pltpu.make_async_copy(
            backward.at[rows], backward_at.at[rows], out_semaphores.at[index]
        )
        copy.start()
        sends.append(copy)
    for copy in loads[1:]:
        copy.wait()
    for start in range(0, node_dev, BLOCK):
        rows = pl.ds(start, BLOCK)
        forward[rows, :] = dot(counts[rows, :node_dev], features[...]) + dot(
            counts[rows, node_dev:], mirrored[:, :width]
        )
    for copy in sends:
        copy.wait()


def block_inverse(columns, index, size=BLOCK):
    first = index * size // LANES
    return jnp.concatenate(
        [columns[:, b : b + 1] for b in range(first, first + size // LANES)], axis=0
    )


def middle(
    core,
    cotangent_at,
    backward_at,
    forward,
    returned,
    picking,
    features,
    w_nbr_one,
    w_self_one,
    bias_one,
    w_nbr_two,
    w_self_two,
    in_count,
    grad_z,
    sent_half,
    bias_rows,
    mean_one,
    h_one,
    pulled,
    cotangent,
    backward,
    semaphores,
    slope,
):
    node_dev, width = features.shape
    blocks = [pl.ds(start, ROWS) for start in range(0, node_dev, ROWS)]
    copies = start_all(
        [backward_at, cotangent_at],
        [backward, cotangent],
        semaphores,
    )
    columns = inverse_columns(in_count)
    for index, rows in enumerate(blocks):
        placed = tdot(picking[:, rows], returned[:, :width])
        mean = ((forward[rows, :] + placed) * block_inverse(columns, index, ROWS)).astype(BF16)
        mean_one[rows, :] = mean
        z_one = (
            dot(features[rows, :], w_self_one[...]) + dot(mean, w_nbr_one[...]) + bias_one[...]
        )
        sigmoid = 1.0 / (1.0 + jnp.exp(-z_one))
        h_one[rows, :] = (z_one * sigmoid).astype(BF16)
        slope[rows, :] = sigmoid * (1.0 + z_one * (1.0 - sigmoid))
    for copy in copies:
        copy.wait()
    bias_total = jnp.zeros((1, width), F32)
    for rows in blocks:
        pull = (backward[rows, :] + tdot(picking[:, rows], returned[:, width:])).astype(BF16)
        pulled[rows, :] = pull
        grad_h = dot_transposed(cotangent[rows, :], w_self_two[...]) + dot_transposed(
            pull, w_nbr_two[...]
        )
        grad = (grad_h * slope[rows, :]).astype(BF16)
        grad_z[rows, :] = grad
        bias_total += jnp.sum(grad.astype(F32), axis=0, keepdims=True)
    bias_high = bias_total.astype(BF16).astype(F32)
    bias_low = bias_total - bias_high
    for row, part in enumerate((bias_high, bias_low)):
        for block in range(width // LANES):
            bias_rows[row * (width // LANES) + block : row * (width // LANES) + block + 1, :] = (
                part[:, block * LANES : (block + 1) * LANES]
            )

    @pl.when(core[0] == 0)
    def _():
        sent_half[:width, :] = tdot(h_one[...], cotangent[...]).astype(BF16)
        sent_half[width:, :] = tdot(h_one[...], pulled[...]).astype(BF16)

    @pl.when(core[0] == 1)
    def _():
        sent_half[:width, :] = tdot(features[...], grad_z[...]).astype(BF16)
        sent_half[width:, :] = tdot(mean_one[...], grad_z[...]).astype(BF16)


def messages(
    core,
    in_count,
    grad_z,
    w_nbr_one,
    picking,
    features,
    mean_one,
    h_one,
    cotangent,
    pulled,
    message_one,
    picked,
    own_half,
):
    node_dev, width = grad_z.shape
    columns = inverse_columns(in_count)
    for index, start in enumerate(range(0, node_dev, BLOCK)):
        rows = pl.ds(start, BLOCK)
        message_one[rows, :] = (
            dot_transposed(grad_z[rows, :], w_nbr_one[...]) * block_inverse(columns, index)
        ).astype(BF16)
    picked[...] = dot(picking[...], message_one[...])

    @pl.when(core[0] == 0)
    def _():
        own_half[:width, :] = tdot(features[...], grad_z[...])
        own_half[width:, :] = tdot(mean_one[...], grad_z[...])

    @pl.when(core[0] == 1)
    def _():
        own_half[:width, :] = tdot(h_one[...], cotangent[...])
        own_half[width:, :] = tdot(h_one[...], pulled[...])


def join_first(own_half, other_half, picked, bias_rows, payload, rows_out, out_semaphore):
    devices, per_peer, _ = rows_out.shape
    mirrors, width = picked.shape
    groups = own_half.shape[0] // mirrors
    rows_out[:, :, :width] = by_peer(picked[...], devices)
    for group in range(groups):
        rows = pl.ds(group * mirrors, mirrors)
        rows_out[:, :, (group + 1) * width : (group + 2) * width] = by_peer(
            own_half[rows, :] + other_half[rows, :].astype(F32), devices
        )
    rows_out[:, :, (groups + 1) * width :] = jnp.broadcast_to(
        bias_rows[...][None], (devices, per_peer, LANES)
    ).astype(BF16)
    send(rows_out, payload, out_semaphore)


def local_back(
    counts_at,
    message_one,
    grad_z,
    w_self_one,
    mirror_out,
    local_out,
    mirror_rows,
    counts,
    semaphores,
):
    node_dev, width = grad_z.shape
    copies = [
        pltpu.make_async_copy(counts_at.at[pl.ds(0, node_dev)], counts, semaphores.at[0]),
        pltpu.make_async_copy(
            counts_at.at[pl.ds(node_dev, mirror_rows.shape[0])], mirror_rows, semaphores.at[1]
        ),
    ]
    for copy in copies:
        copy.start()
    for start in range(0, node_dev, BLOCK):
        rows = pl.ds(start, BLOCK)
        local_out[rows, :] = dot_transposed(grad_z[rows, :], w_self_one[...])
    copies[0].wait()
    mirror_out[...] = tdot(counts[:, node_dev:], message_one[...])
    for start in range(0, node_dev, BLOCK):
        rows = pl.ds(start, BLOCK)
        local_out[rows, :] += tdot(counts[:, rows], message_one[...])
    copies[1].wait()


def join_second(
    norm_factor,
    received,
    mirror_partial,
    mirror_counts,
    payload,
    mirrored_out,
    bias_total,
):
    devices, per_peer, _ = payload.shape
    mirrors, width = mirror_partial.shape
    groups = payload.shape[2] // width - 1
    mirrored = by_row(received[:, :, :width]).astype(BF16)
    mirrored_out[...] = mirrored
    partial_sums = mirror_partial[...] + tdot(mirror_counts[...], mirrored)
    payload[:, :, :width] = by_peer(partial_sums, devices)
    for group in range(groups):
        lanes = slice((group + 1) * width, (group + 2) * width)
        owned = (
            jnp.sum(
                received[:, :, lanes].astype(F32).reshape(devices // 2, 2, per_peer, width), axis=0
            )
            * norm_factor
        ).astype(BF16)
        payload[:, :, lanes] = jnp.broadcast_to(
            owned[None], (devices // 2, 2, per_peer, width)
        ).reshape(devices, per_peer, width)
    sums = (
        jnp.sum(received[:, :, (groups + 1) * width :].astype(F32), axis=0) * norm_factor
    )
    parts = width // LANES
    for block in range(parts):
        bias_total[:, block * LANES : (block + 1) * LANES] = (
            sums[block : block + 1, :] + sums[parts + block : parts + block + 1, :]
        )


def finish(
    core,
    received,
    mirrored,
    picking,
    mirror_rows,
    local_grad,
    bias_total,
    features_at,
    weights_at,
    bias_at,
    features_out,
    weights_out,
    semaphores,
):
    devices, per_peer, _ = received.shape
    node_dev, width = local_grad.shape
    mirrors = picking.shape[0]
    half = weights_out.shape[0]
    for group in range(half // mirrors):
        weights_out[pl.ds(group * mirrors, mirrors), :] = by_row(
            received[:, :, (group + 1) * width : (group + 2) * width]
        )
    mine = pl.multiple_of(core[0] * half, half)
    weights_copy = pltpu.make_async_copy(
        weights_out, weights_at.at[pl.ds(mine, half)], semaphores.at[0]
    )
    weights_copy.start()
    bias_copy = pltpu.make_async_copy(bias_total, bias_at, semaphores.at[2])
    bias_copy.start()
    returned = by_row(received[:, :, :width]).astype(BF16)
    for start in range(0, node_dev, BLOCK):
        rows = pl.ds(start, BLOCK)
        features_out[rows, :] = (
            local_grad[rows, :]
            + tdot(picking[:, rows], returned)
            + tdot(mirror_rows[:, rows], mirrored[...])
        ).astype(BF16)
    features_copy = pltpu.make_async_copy(features_out, features_at, semaphores.at[1])
    features_copy.start()
    weights_copy.wait()
    bias_copy.wait()
    features_copy.wait()


def finish_other(core, weights_in, received, weights_at, weights_out, semaphore):
    half, width = weights_out.shape
    devices, per_peer, columns = received.shape
    mirrors = devices * per_peer
    for group in range(half // mirrors):
        weights_out[pl.ds(group * mirrors, mirrors), :] = by_row(
            received[:, :, (group + 1) * width : (group + 2) * width]
        )
    other = pl.multiple_of((1 - core[0]) * half, half)
    send(weights_out, weights_at.at[pl.ds(other, half)], semaphore)


def shards(
    features,
    cotangent,
    w_self_one,
    w_nbr_one,
    bias_one,
    w_self_two,
    w_nbr_two,
    in_count,
    send_list,
    src_slot,
    dst_slot,
    edge_count,
):
    node_dev, width = features.shape
    devices = lax.axis_size("dom") * lax.axis_size("sub")
    per_peer = send_list.shape[2]
    mirrors = devices * per_peer
    slots = node_dev + mirrors
    edges = src_slot.shape[1]
    core = lax.axis_index("sub") % 2
    swap = [(i, i ^ 1) for i in range(devices)]
    in_count = in_count.reshape(-1, LANES)
    sent = send_list[0].T
    sources = src_slot.reshape(-1, LANES)
    targets = dst_slot.reshape(-1, LANES)
    blocks = -(-slots // BLOCK)

    payload_shape = (devices, per_peer, 2 * width)
    payload, scaled, picking, source_columns, targets = run(
        pick_rows,
        "pick_rows",
        [
            pltpu.HBM(payload_shape, BF16),
            pltpu.VMEM((node_dev, width), BF16),
            pltpu.VMEM((mirrors, node_dev), BF16),
            pltpu.VMEM((LANES, edges // LANES), I32),
            pltpu.VMEM(targets.shape, I32),
        ],
        smem=[edge_count],
        hbm=[features, cotangent, in_count, sent, sources, targets],
        scratch=staged_for(6, features, cotangent, in_count, sent, sources)
        + [pltpu.VMEM(payload_shape, BF16), pltpu.SemaphoreType.DMA],
        flops=4 * mirrors * node_dev * width,
    )
    mirrored = exchange(payload).reshape(mirrors, 2 * width)

    rows_bf16 = pltpu.VMEM((node_dev, width), BF16)
    rows_f32 = pltpu.VMEM((node_dev, width), F32)
    counts, scaled, mirror_counts, partial_sums = run(
        count_edges,
        "count_edges",
        [
            pltpu.HBM((slots, slots), BF16),
            pltpu.HBM((node_dev, width), BF16),
            pltpu.VMEM((mirrors, mirrors), BF16),
            pltpu.VMEM((mirrors, 2 * width), F32),
        ],
        hbm=[features],
        vmem=[scaled, source_columns, targets],
        scratch=[
            rows_bf16,
            pltpu.SemaphoreType.DMA,
            pltpu.VMEM((edges, slots), F8),
            pltpu.VMEM((slots, edges), F8),
            pltpu.VMEM((slots, slots), BF16),
            pltpu.SemaphoreType.DMA((blocks + 1,)),
        ],
        flops=2 * slots * edges * slots,
    )
    (payload,) = run(
        mirror_sums,
        "mirror_sums",
        [pltpu.HBM(payload_shape, BF16)],
        vmem=[partial_sums, mirror_counts, mirrored],
        scratch=[pltpu.VMEM(payload_shape, BF16), pltpu.SemaphoreType.DMA],
        flops=4 * mirrors * mirrors * width,
    )
    returned = exchange(payload).reshape(mirrors, 2 * width)
    forward, features_in, backward = run(
        local_sums,
        "local_sums",
        [rows_f32, rows_bf16, pltpu.HBM((node_dev, width), F32)],
        hbm=[counts, features, scaled],
        vmem=[mirrored],
        scratch=[
            pltpu.VMEM((slots, slots), BF16),
            rows_bf16,
            rows_f32,
            pltpu.SemaphoreType.DMA((blocks,)),
            pltpu.SemaphoreType.DMA((node_dev // BLOCK,)),
            pltpu.SemaphoreType.DMA((2,)),
        ],
        flops=4 * node_dev * slots * width,
    )

    half = 2 * width
    grad_z_one, sent_half, bias_rows, mean_one, h_one, pulled, cotangent_in = run(
        middle,
        "middle",
        [
            rows_bf16,
            pltpu.VMEM((half, width), BF16),
            pltpu.VMEM((2 * width // LANES, LANES), F32),
            rows_bf16,
            rows_bf16,
            rows_bf16,
            rows_bf16,
        ],
        smem=[core.reshape(1)],
        hbm=[cotangent, backward],
        vmem=[
            forward,
            returned,
            picking,
            features_in,
            w_nbr_one,
            w_self_one,
            bias_one.reshape(1, -1),
            w_nbr_two,
            w_self_two,
            in_count,
        ],
        scratch=[
            rows_f32,
            pltpu.SemaphoreType.DMA((2,)),
            rows_f32,
        ],
        flops=20 * node_dev * width * width,
    )
    other_half = lax.ppermute(sent_half, AXES, swap)
    message_one, picked, own_half = run(
        messages,
        "messages",
        [rows_bf16, pltpu.VMEM((mirrors, width), F32), pltpu.VMEM((half, width), F32)],
        smem=[core.reshape(1)],
        vmem=[
            in_count,
            grad_z_one,
            w_nbr_one,
            picking,
            features_in,
            mean_one,
            h_one,
            cotangent_in,
            pulled,
        ],
        flops=6 * node_dev * width * width,
    )

    columns = width * (half // mirrors + 1)
    payload_shape = (devices, per_peer, columns + LANES)
    (payload,) = run(
        join_first,
        "join_first",
        [pltpu.HBM(payload_shape, BF16)],
        vmem=[own_half, other_half, picked, bias_rows],
        scratch=[pltpu.VMEM(payload_shape, BF16), pltpu.SemaphoreType.DMA],
    )
    received = exchange(payload)
    mirror_back, local_grad, mirror_rows = run(
        local_back,
        "local_back",
        [
            pltpu.VMEM((mirrors, width), F32),
            pltpu.VMEM((node_dev, width), F32),
            pltpu.VMEM((mirrors, slots), BF16),
        ],
        hbm=[counts],
        vmem=[message_one, grad_z_one, w_self_one],
        scratch=[pltpu.VMEM((node_dev, slots), BF16), pltpu.SemaphoreType.DMA((2,))],
        flops=2 * node_dev * (slots + width) * width,
    )
    norm_factor = float(node_dev * devices) ** -0.5
    payload, mirrored, bias_total = run(
        functools.partial(join_second, norm_factor),
        "join_second",
        [
            pltpu.VMEM((devices, per_peer, columns), BF16),
            pltpu.VMEM((mirrors, width), BF16),
            pltpu.VMEM((1, width), F32),
        ],
        vmem=[received, mirror_back, mirror_counts],
    )
    received = exchange(payload)
    other = lax.ppermute(received, AXES, swap)
    grad_features, grad_weights, grad_bias = run(
        finish,
        "finish",
        [
            pltpu.HBM((node_dev, width), BF16),
            pltpu.HBM((2 * half, width), F32),
            pltpu.HBM((1, width), F32),
        ],
        smem=[core.reshape(1)],
        vmem=[received, mirrored, picking, mirror_rows, local_grad, bias_total],
        scratch=[
            pltpu.VMEM((node_dev, width), BF16),
            pltpu.VMEM((half, width), F32),
            pltpu.SemaphoreType.DMA((3,)),
        ],
        flops=6 * node_dev * mirrors * width,
    )
    (grad_weights,) = run(
        finish_other,
        "finish_other",
        [pltpu.HBM((2 * half, width), F32)],
        smem=[core.reshape(1)],
        hbm=[grad_weights],
        vmem=[other],
        scratch=[pltpu.VMEM((half, width), F32), pltpu.SemaphoreType.DMA],
        aliases={1: 0},
    )
    return (
        grad_features,
        grad_weights.reshape(4, width, width),
        grad_bias.reshape(width),
    )


def solution(mesh):
    by_device = P(AXES)
    return jax.shard_map(
        shards,
        mesh=mesh,
        in_specs=(
            P(AXES, None),
            P(AXES, None),
            P(),
            P(),
            P(),
            P(),
            P(),
            by_device,
            P(AXES, None, None),
            P(AXES, None),
            P(AXES, None),
            by_device,
        ),
        out_specs=(P(AXES, None), P(), P()),
        check_vma=False,
    )
```

```python
import functools

import jax
import jax.numpy as jnp
from jax import lax
from jax.experimental import pallas as pl
from jax.experimental.pallas import tpu as pltpu
from jax.sharding import PartitionSpec as P

AXES = ("dom", "sub")
BF16 = jnp.bfloat16
F8 = jnp.float8_e4m3fn
F32 = jnp.float32
I32 = jnp.int32
I16 = jnp.int16
LANES = 128
BLOCK = 256
ROWS = 512
VMEM_LIMIT = 24 * 2**20


def tdot(left, right):
    return lax.dot_general(left, right, (((0,), (0,)), ((), ())), preferred_element_type=F32)


def dot_transposed(left, right):
    return lax.dot_general(left, right, (((1,), (1,)), ((), ())), preferred_element_type=F32)


def dot(left, right):
    return jnp.dot(left, right, preferred_element_type=F32)


def exchange(rows):
    return lax.all_to_all(rows, AXES, split_axis=0, concat_axis=0, tiled=True)


def run(kernel, name, outs, vmem=(), hbm=(), smem=(), scratch=(), flops=0, moved=0, aliases=None):
    in_place = pl.BlockSpec(memory_space=pltpu.VMEM)
    remote = pl.BlockSpec(memory_space=pltpu.HBM)
    return pl.pallas_call(
        kernel,
        out_shape=tuple(outs),
        in_specs=[pl.BlockSpec(memory_space=pltpu.SMEM)] * len(smem)
        + [remote] * len(hbm)
        + [in_place] * len(vmem),
        out_specs=tuple(remote if out.memory_space == pltpu.HBM else in_place for out in outs),
        scratch_shapes=tuple(scratch),
        compiler_params=pltpu.CompilerParams(vmem_limit_bytes=VMEM_LIMIT),
        cost_estimate=pl.CostEstimate(flops=flops, bytes_accessed=moved, transcendentals=0),
        input_output_aliases=aliases or {},
        name=name,
    )(
        *smem,
        *[pltpu.with_memory_space_constraint(arg, pltpu.HBM) for arg in hbm],
        *[pltpu.with_memory_space_constraint(arg, pltpu.VMEM) for arg in vmem],
    )


def staged_for(count, *arrays):
    buffers = [pltpu.VMEM(array.shape, array.dtype) for array in arrays]
    return buffers + [pltpu.SemaphoreType.DMA((count,))]


def start_all(sources, buffers, semaphores):
    copies = [
        pltpu.make_async_copy(source, buffer, semaphores.at[index])
        for index, (source, buffer) in enumerate(zip(sources, buffers))
    ]
    for copy in copies:
        copy.start()
    return copies


def iota(shape, dim, dtype=I32):
    return lax.broadcasted_iota(dtype, shape, dim)


def one_hot(mask, dtype):
    return jnp.where(mask, 1.0, 0.0).astype(dtype)


def edge_hot(mask):
    return jnp.where(mask, jnp.ones(mask.shape, BF16), jnp.zeros(mask.shape, BF16)).astype(F8)


def by_peer(rows, devices):
    return rows.reshape(devices, rows.shape[0] // devices, rows.shape[1]).astype(BF16)


def by_row(parts):
    return parts.astype(F32).reshape(parts.shape[0] * parts.shape[1], parts.shape[2])


def inverse_columns(in_count):
    return (1.0 / jnp.maximum(in_count[...], 1).astype(F32)).T


def send(array, out, semaphore):
    copy = pltpu.make_async_copy(array, out, semaphore)
    copy.start()
    copy.wait()


def pick_rows(
    features_at,
    cotangent_at,
    in_count_at,
    sent_at,
    sources_at,
    targets_at,
    payload,
    scaled,
    picking,
    sources,
    targets,
    features,
    cotangent,
    in_count,
    sent,
    semaphores,
    rows_out,
    out_semaphore,
):
    node_dev, width = features.shape
    per_peer, devices = sent.shape
    mirrors = devices * per_peer
    copies = start_all(
        [sent_at, in_count_at, cotangent_at, features_at, sources_at, targets_at],
        [sent, in_count, cotangent, features, sources, targets],
        semaphores,
    )
    copies[0].wait()
    spread_out = one_hot(
        iota((mirrors, devices), 0) // per_peer == iota((mirrors, devices), 1), BF16
    )
    high = dot_transposed(spread_out, (sent[...] >> 5).astype(F32).astype(BF16))
    low = dot_transposed(spread_out, (sent[...] & 31).astype(F32).astype(BF16))
    within = iota((mirrors, per_peer), 0) % per_peer == iota((mirrors, per_peer), 1)
    owner = jnp.sum(jnp.where(within, high * 32.0 + low, 0.0), axis=1, keepdims=True).astype(I32)
    picked = iota((mirrors, node_dev), 1) == owner
    picks = one_hot(picked, BF16)
    picking[...] = picks
    copies[1].wait()
    inverse_rows = 1.0 / jnp.maximum(in_count[...], 1).astype(F32)
    owner_inverse = jnp.zeros((mirrors, LANES), F32)
    for block in range(node_dev // LANES):
        lanes = slice(block * LANES, (block + 1) * LANES)
        owner_inverse += jnp.where(picked[:, lanes], inverse_rows[block : block + 1, :], 0.0)
    owner_inverse = jnp.sum(owner_inverse, axis=1, keepdims=True)
    copies[2].wait()
    back = dot(picks, cotangent[...]) * owner_inverse
    rows_out[:, :, width:] = by_peer(back, devices)
    copies[3].wait()
    rows_out[:, :, :width] = by_peer(dot(picks, features[...]), devices)
    out_copy = pltpu.make_async_copy(rows_out, payload, out_semaphore)
    out_copy.start()
    columns = inverse_rows.T
    for block in range(node_dev // LANES):
        rows = pl.ds(block * LANES, LANES)
        scaled[rows, :] = (
            cotangent[rows, :].astype(F32) * columns[:, block : block + 1]
        ).astype(BF16)
    copies[4].wait()
    copies[5].wait()
    out_copy.wait()


def count_edges(
    edge_count,
    features_at,
    scaled,
    sources,
    targets,
    counts_out,
    scaled_at,
    mirror_rows,
    partial_out,
    features,
    semaphore,
    from_hot,
    into_hot,
    counts,
    out_semaphores,
):
    node_dev, width = features.shape
    slots, edges = into_hot.shape
    feature_copy = pltpu.make_async_copy(features_at, features, semaphore)
    feature_copy.start()
    sends = [pltpu.make_async_copy(scaled, scaled_at, out_semaphores.at[node_dev // BLOCK])]
    sends[0].start()
    source_columns = sources[...].T
    lane_ids = iota((LANES, slots), 1, I16)
    for block in range(edges // LANES):
        column = jnp.broadcast_to(source_columns[:, block : block + 1], (LANES, LANES)).astype(I16)
        column = jnp.concatenate([column] * (slots // LANES), axis=1)
        from_hot[pl.ds(block * LANES, LANES), :] = edge_hot(lane_ids == column)
    edge_ids = iota(targets.shape, 0) * LANES + iota(targets.shape, 1)
    target_rows = jnp.where(edge_ids < edge_count[0], targets[...], -1).astype(I16)
    row_ids = iota((LANES, LANES), 0, I16)
    for start in range(0, slots, BLOCK):
        size = min(BLOCK, slots - start)
        for block in range(edges // LANES):
            target_row = target_rows[block : block + 1, :]
            for part in range(start, start + size, LANES):
                into_hot[pl.ds(part, LANES), pl.ds(block * LANES, LANES)] = edge_hot(
                    row_ids + jnp.int16(part) == target_row
                )
        rows = pl.ds(start, size)
        block_counts = dot(into_hot[rows, :], from_hot[...]).astype(BF16)
        if start < node_dev:
            counts[rows, :] = block_counts
            copy = pltpu.make_async_copy(
                counts.at[rows], counts_out.at[rows], out_semaphores.at[start // BLOCK]
            )
            copy.start()
            sends.append(copy)
        else:
            mirror_rows[pl.ds(start - node_dev, size), :] = block_counts
    feature_copy.wait()
    partial_out[:, :width] = dot(mirror_rows[:, :node_dev], features[...])
    partial_out[:, width:] = tdot(counts[:, node_dev:], scaled[...])
    for copy in sends:
        copy.wait()


def mirror_sums(partial_in, mirror_rows, mirrored, payload, rows_out, out_semaphore):
    devices, _, columns = rows_out.shape
    width = columns // 2
    received = mirrored[...]
    mirror_counts = mirror_rows[:, mirror_rows.shape[1] - mirror_rows.shape[0] :]
    front = partial_in[:, :width] + dot(mirror_counts, received[:, :width])
    back = partial_in[:, width:] + tdot(mirror_counts, received[:, width:])
    rows_out[:, :, :width] = by_peer(front, devices)
    rows_out[:, :, width:] = by_peer(back, devices)
    send(rows_out, payload, out_semaphore)


def local_sums(
    counts_at,
    features_at,
    scaled_at,
    mirrored,
    mirror_rows,
    forward,
    features,
    backward_at,
    mirror_at,
    counts,
    scaled,
    backward,
    block_semaphores,
    out_semaphores,
    semaphores,
):
    node_dev, width = features.shape
    blocks = [(start, BLOCK) for start in range(0, node_dev, BLOCK)]
    loads = start_all([scaled_at], [scaled], semaphores)
    mirror_copy = pltpu.make_async_copy(mirror_rows, mirror_at, semaphores.at[2])
    mirror_copy.start()
    copies = []
    for index, (start, size) in enumerate(blocks):
        rows = pl.ds(start, size)
        copy = pltpu.make_async_copy(
            counts_at.at[rows], counts.at[rows], block_semaphores.at[index]
        )
        copy.start()
        copies.append(copy)
    loads.append(pltpu.make_async_copy(features_at, features, semaphores.at[1]))
    loads[1].start()
    for copy in [loads[0]] + copies:
        copy.wait()
    sends = []
    for index, start in enumerate(range(0, node_dev, BLOCK)):
        rows = pl.ds(start, BLOCK)
        backward[rows, :] = tdot(counts[:, rows], scaled[...]) + tdot(
            mirror_rows[:, rows], mirrored[:, width:]
        )
        copy = pltpu.make_async_copy(
            backward.at[rows], backward_at.at[rows], out_semaphores.at[index]
        )
        copy.start()
        sends.append(copy)
    for copy in loads[1:]:
        copy.wait()
    for start in range(0, node_dev, BLOCK):
        rows = pl.ds(start, BLOCK)
        forward[rows, :] = dot(counts[rows, :node_dev], features[...]) + dot(
            counts[rows, node_dev:], mirrored[:, :width]
        )
    for copy in sends + [mirror_copy]:
        copy.wait()


def block_inverse(columns, index, size=BLOCK):
    first = index * size // LANES
    return jnp.concatenate(
        [columns[:, b : b + 1] for b in range(first, first + size // LANES)], axis=0
    )


def middle(
    core,
    cotangent_at,
    backward_at,
    forward,
    returned,
    picking,
    features,
    w_nbr_one,
    w_self_one,
    bias_one,
    w_nbr_two,
    w_self_two,
    in_count,
    grad_z,
    sent_half,
    bias_rows,
    mean_one,
    h_one,
    pulled,
    cotangent,
    backward,
    semaphores,
    slope,
):
    node_dev, width = features.shape
    blocks = [pl.ds(start, ROWS) for start in range(0, node_dev, ROWS)]
    copies = start_all(
        [backward_at, cotangent_at],
        [backward, cotangent],
        semaphores,
    )
    columns = inverse_columns(in_count)
    for index, rows in enumerate(blocks):
        placed = tdot(picking[:, rows], returned[:, :width])
        mean = ((forward[rows, :] + placed) * block_inverse(columns, index, ROWS)).astype(BF16)
        mean_one[rows, :] = mean
        z_one = (
            dot(features[rows, :], w_self_one[...]) + dot(mean, w_nbr_one[...]) + bias_one[...]
        )
        sigmoid = 1.0 / (1.0 + jnp.exp(-z_one))
        h_one[rows, :] = (z_one * sigmoid).astype(BF16)
        slope[rows, :] = sigmoid * (1.0 + z_one * (1.0 - sigmoid))
    for copy in copies:
        copy.wait()
    bias_total = jnp.zeros((1, width), F32)
    for rows in blocks:
        pull = (backward[rows, :] + tdot(picking[:, rows], returned[:, width:])).astype(BF16)
        pulled[rows, :] = pull
        grad_h = dot_transposed(cotangent[rows, :], w_self_two[...]) + dot_transposed(
            pull, w_nbr_two[...]
        )
        grad = (grad_h * slope[rows, :]).astype(BF16)
        grad_z[rows, :] = grad
        bias_total += jnp.sum(grad.astype(F32), axis=0, keepdims=True)
    bias_high = bias_total.astype(BF16).astype(F32)
    bias_low = bias_total - bias_high
    for row, part in enumerate((bias_high, bias_low)):
        for block in range(width // LANES):
            bias_rows[row * (width // LANES) + block : row * (width // LANES) + block + 1, :] = (
                part[:, block * LANES : (block + 1) * LANES]
            )

    @pl.when(core[0] == 0)
    def _():
        sent_half[:width, :] = tdot(h_one[...], cotangent[...]).astype(BF16)
        sent_half[width:, :] = tdot(h_one[...], pulled[...]).astype(BF16)

    @pl.when(core[0] == 1)
    def _():
        sent_half[:width, :] = tdot(features[...], grad_z[...]).astype(BF16)
        sent_half[width:, :] = tdot(mean_one[...], grad_z[...]).astype(BF16)


def messages(
    core,
    in_count,
    grad_z,
    w_nbr_one,
    picking,
    features,
    mean_one,
    h_one,
    cotangent,
    pulled,
    message_one,
    picked,
    own_half,
):
    node_dev, width = grad_z.shape
    columns = inverse_columns(in_count)
    for index, start in enumerate(range(0, node_dev, BLOCK)):
        rows = pl.ds(start, BLOCK)
        message_one[rows, :] = (
            dot_transposed(grad_z[rows, :], w_nbr_one[...]) * block_inverse(columns, index)
        ).astype(BF16)
    picked[...] = dot(picking[...], message_one[...])

    @pl.when(core[0] == 0)
    def _():
        own_half[:width, :] = tdot(features[...], grad_z[...])
        own_half[width:, :] = tdot(mean_one[...], grad_z[...])

    @pl.when(core[0] == 1)
    def _():
        own_half[:width, :] = tdot(h_one[...], cotangent[...])
        own_half[width:, :] = tdot(h_one[...], pulled[...])


def join_first(own_half, other_half, picked, bias_rows, payload, rows_out, out_semaphore):
    devices, per_peer, _ = rows_out.shape
    mirrors, width = picked.shape
    groups = own_half.shape[0] // mirrors
    rows_out[:, :, :width] = by_peer(picked[...], devices)
    for group in range(groups):
        rows = pl.ds(group * mirrors, mirrors)
        rows_out[:, :, (group + 1) * width : (group + 2) * width] = by_peer(
            own_half[rows, :] + other_half[rows, :].astype(F32), devices
        )
    rows_out[:, :, (groups + 1) * width :] = jnp.broadcast_to(
        bias_rows[...][None], (devices, per_peer, LANES)
    ).astype(BF16)
    send(rows_out, payload, out_semaphore)


def local_back(
    counts_at,
    mirror_at,
    message_one,
    grad_z,
    w_self_one,
    mirror_out,
    local_out,
    mirror_rows,
    counts,
    semaphores,
):
    node_dev, width = grad_z.shape
    copies = start_all([counts_at, mirror_at], [counts, mirror_rows], semaphores)
    for start in range(0, node_dev, BLOCK):
        rows = pl.ds(start, BLOCK)
        local_out[rows, :] = dot_transposed(grad_z[rows, :], w_self_one[...])
    for copy in copies:
        copy.wait()
    mirror_out[...] = tdot(counts[:, node_dev:], message_one[...])
    for start in range(0, node_dev, BLOCK):
        rows = pl.ds(start, BLOCK)
        local_out[rows, :] += tdot(counts[:, rows], message_one[...])


def join_second(
    norm_factor,
    received,
    mirror_partial,
    mirror_rows,
    payload,
    mirrored_out,
    bias_total,
):
    devices, per_peer, _ = payload.shape
    mirrors, width = mirror_partial.shape
    groups = payload.shape[2] // width - 1
    mirrored = by_row(received[:, :, :width]).astype(BF16)
    mirrored_out[...] = mirrored
    partial_sums = mirror_partial[...] + tdot(
        mirror_rows[:, mirror_rows.shape[1] - mirrors :], mirrored
    )
    payload[:, :, :width] = by_peer(partial_sums, devices)
    for group in range(groups):
        lanes = slice((group + 1) * width, (group + 2) * width)
        owned = (
            jnp.sum(
                received[:, :, lanes].astype(F32).reshape(devices // 2, 2, per_peer, width), axis=0
            )
            * norm_factor
        ).astype(BF16)
        payload[:, :, lanes] = jnp.broadcast_to(
            owned[None], (devices // 2, 2, per_peer, width)
        ).reshape(devices, per_peer, width)
    sums = (
        jnp.sum(received[:, :, (groups + 1) * width :].astype(F32), axis=0) * norm_factor
    )
    parts = width // LANES
    for block in range(parts):
        bias_total[:, block * LANES : (block + 1) * LANES] = (
            sums[block : block + 1, :] + sums[parts + block : parts + block + 1, :]
        )


def finish(
    core,
    received,
    mirrored,
    picking,
    mirror_rows,
    local_grad,
    bias_total,
    features_at,
    weights_at,
    bias_at,
    features_out,
    weights_out,
    semaphores,
):
    devices, per_peer, _ = received.shape
    node_dev, width = local_grad.shape
    mirrors = picking.shape[0]
    half = weights_out.shape[0]
    for group in range(half // mirrors):
        weights_out[pl.ds(group * mirrors, mirrors), :] = by_row(
            received[:, :, (group + 1) * width : (group + 2) * width]
        )
    mine = pl.multiple_of(core[0] * half, half)
    weights_copy = pltpu.make_async_copy(
        weights_out, weights_at.at[pl.ds(mine, half)], semaphores.at[0]
    )
    weights_copy.start()
    bias_copy = pltpu.make_async_copy(bias_total, bias_at, semaphores.at[2])
    bias_copy.start()
    returned = by_row(received[:, :, :width]).astype(BF16)
    for start in range(0, node_dev, BLOCK):
        rows = pl.ds(start, BLOCK)
        features_out[rows, :] = (
            local_grad[rows, :]
            + tdot(picking[:, rows], returned)
            + tdot(mirror_rows[:, rows], mirrored[...])
        ).astype(BF16)
    features_copy = pltpu.make_async_copy(features_out, features_at, semaphores.at[1])
    features_copy.start()
    weights_copy.wait()
    bias_copy.wait()
    features_copy.wait()


def finish_other(core, weights_in, received, weights_at, weights_out, semaphore):
    half, width = weights_out.shape
    devices, per_peer, columns = received.shape
    mirrors = devices * per_peer
    for group in range(half // mirrors):
        weights_out[pl.ds(group * mirrors, mirrors), :] = by_row(
            received[:, :, (group + 1) * width : (group + 2) * width]
        )
    other = pl.multiple_of((1 - core[0]) * half, half)
    send(weights_out, weights_at.at[pl.ds(other, half)], semaphore)


def shards(
    features,
    cotangent,
    w_self_one,
    w_nbr_one,
    bias_one,
    w_self_two,
    w_nbr_two,
    in_count,
    send_list,
    src_slot,
    dst_slot,
    edge_count,
):
    node_dev, width = features.shape
    devices = lax.axis_size("dom") * lax.axis_size("sub")
    per_peer = send_list.shape[2]
    mirrors = devices * per_peer
    slots = node_dev + mirrors
    edges = src_slot.shape[1]
    core = lax.axis_index("sub") % 2
    swap = [(i, i ^ 1) for i in range(devices)]
    in_count = in_count.reshape(-1, LANES)
    sent = send_list[0].T
    sources = src_slot.reshape(-1, LANES)
    targets = dst_slot.reshape(-1, LANES)
    blocks = node_dev // BLOCK

    payload_shape = (devices, per_peer, 2 * width)
    payload, scaled, picking, sources, targets = run(
        pick_rows,
        "pick_rows",
        [
            pltpu.HBM(payload_shape, BF16),
            pltpu.VMEM((node_dev, width), BF16),
            pltpu.VMEM((mirrors, node_dev), BF16),
            pltpu.VMEM(sources.shape, I32),
            pltpu.VMEM(targets.shape, I32),
        ],
        hbm=[features, cotangent, in_count, sent, sources, targets],
        scratch=staged_for(6, features, cotangent, in_count, sent)
        + [pltpu.VMEM(payload_shape, BF16), pltpu.SemaphoreType.DMA],
        flops=4 * mirrors * node_dev * width,
    )
    mirrored = exchange(payload).reshape(mirrors, 2 * width)

    rows_bf16 = pltpu.VMEM((node_dev, width), BF16)
    rows_f32 = pltpu.VMEM((node_dev, width), F32)
    counts, scaled, mirror_rows, partial_sums = run(
        count_edges,
        "count_edges",
        [
            pltpu.HBM((node_dev, slots), BF16),
            pltpu.HBM((node_dev, width), BF16),
            pltpu.VMEM((mirrors, slots), BF16),
            pltpu.VMEM((mirrors, 2 * width), F32),
        ],
        smem=[edge_count],
        hbm=[features],
        vmem=[scaled, sources, targets],
        scratch=[
            rows_bf16,
            pltpu.SemaphoreType.DMA,
            pltpu.VMEM((edges, slots), F8),
            pltpu.VMEM((slots, edges), F8),
            pltpu.VMEM((node_dev, slots), BF16),
            pltpu.SemaphoreType.DMA((blocks + 1,)),
        ],
        flops=2 * slots * edges * slots,
    )
    (payload,) = run(
        mirror_sums,
        "mirror_sums",
        [pltpu.HBM(payload_shape, BF16)],
        vmem=[partial_sums, mirror_rows, mirrored],
        scratch=[pltpu.VMEM(payload_shape, BF16), pltpu.SemaphoreType.DMA],
        flops=4 * mirrors * mirrors * width,
    )
    returned = exchange(payload).reshape(mirrors, 2 * width)
    forward, features_in, backward, mirror_rows = run(
        local_sums,
        "local_sums",
        [
            rows_f32,
            rows_bf16,
            pltpu.HBM((node_dev, width), F32),
            pltpu.HBM((mirrors, slots), BF16),
        ],
        hbm=[counts, features, scaled],
        vmem=[mirrored, mirror_rows],
        scratch=[
            pltpu.VMEM((node_dev, slots), BF16),
            rows_bf16,
            rows_f32,
            pltpu.SemaphoreType.DMA((blocks,)),
            pltpu.SemaphoreType.DMA((node_dev // BLOCK,)),
            pltpu.SemaphoreType.DMA((3,)),
        ],
        flops=4 * node_dev * slots * width,
    )

    half = 2 * width
    grad_z_one, sent_half, bias_rows, mean_one, h_one, pulled, cotangent_in = run(
        middle,
        "middle",
        [
            rows_bf16,
            pltpu.VMEM((half, width), BF16),
            pltpu.VMEM((2 * width // LANES, LANES), F32),
            rows_bf16,
            rows_bf16,
            rows_bf16,
            rows_bf16,
        ],
        smem=[core.reshape(1)],
        hbm=[cotangent, backward],
        vmem=[
            forward,
            returned,
            picking,
            features_in,
            w_nbr_one,
            w_self_one,
            bias_one.reshape(1, -1),
            w_nbr_two,
            w_self_two,
            in_count,
        ],
        scratch=[
            rows_f32,
            pltpu.SemaphoreType.DMA((2,)),
            rows_f32,
        ],
        flops=20 * node_dev * width * width,
    )
    other_half = lax.ppermute(sent_half, AXES, swap)
    message_one, picked, own_half = run(
        messages,
        "messages",
        [rows_bf16, pltpu.VMEM((mirrors, width), F32), pltpu.VMEM((half, width), F32)],
        smem=[core.reshape(1)],
        vmem=[
            in_count,
            grad_z_one,
            w_nbr_one,
            picking,
            features_in,
            mean_one,
            h_one,
            cotangent_in,
            pulled,
        ],
        flops=6 * node_dev * width * width,
    )

    columns = width * (half // mirrors + 1)
    payload_shape = (devices, per_peer, columns + LANES)
    (payload,) = run(
        join_first,
        "join_first",
        [pltpu.HBM(payload_shape, BF16)],
        vmem=[own_half, other_half, picked, bias_rows],
        scratch=[pltpu.VMEM(payload_shape, BF16), pltpu.SemaphoreType.DMA],
    )
    received = exchange(payload)
    mirror_back, local_grad, mirror_rows = run(
        local_back,
        "local_back",
        [
            pltpu.VMEM((mirrors, width), F32),
            pltpu.VMEM((node_dev, width), F32),
            pltpu.VMEM((mirrors, slots), BF16),
        ],
        hbm=[counts, mirror_rows],
        vmem=[message_one, grad_z_one, w_self_one],
        scratch=[pltpu.VMEM((node_dev, slots), BF16), pltpu.SemaphoreType.DMA((2,))],
        flops=2 * node_dev * (slots + width) * width,
    )
    norm_factor = float(node_dev * devices) ** -0.5
    payload, mirrored, bias_total = run(
        functools.partial(join_second, norm_factor),
        "join_second",
        [
            pltpu.VMEM((devices, per_peer, columns), BF16),
            pltpu.VMEM((mirrors, width), BF16),
            pltpu.VMEM((1, width), F32),
        ],
        vmem=[received, mirror_back, mirror_rows],
    )
    received = exchange(payload)
    other = lax.ppermute(received, AXES, swap)
    grad_features, grad_weights, grad_bias = run(
        finish,
        "finish",
        [
            pltpu.HBM((node_dev, width), BF16),
            pltpu.HBM((2 * half, width), F32),
            pltpu.HBM((1, width), F32),
        ],
        smem=[core.reshape(1)],
        vmem=[received, mirrored, picking, mirror_rows, local_grad, bias_total],
        scratch=[
            pltpu.VMEM((node_dev, width), BF16),
            pltpu.VMEM((half, width), F32),
            pltpu.SemaphoreType.DMA((3,)),
        ],
        flops=6 * node_dev * mirrors * width,
    )
    (grad_weights,) = run(
        finish_other,
        "finish_other",
        [pltpu.HBM((2 * half, width), F32)],
        smem=[core.reshape(1)],
        hbm=[grad_weights],
        vmem=[other],
        scratch=[pltpu.VMEM((half, width), F32), pltpu.SemaphoreType.DMA],
        aliases={1: 0},
    )
    return (
        grad_features,
        grad_weights.reshape(4, width, width),
        grad_bias.reshape(width),
    )


def solution(mesh):
    by_device = P(AXES)
    return jax.shard_map(
        shards,
        mesh=mesh,
        in_specs=(
            P(AXES, None),
            P(AXES, None),
            P(),
            P(),
            P(),
            P(),
            P(),
            by_device,
            P(AXES, None, None),
            P(AXES, None),
            P(AXES, None),
            by_device,
        ),
        out_specs=(P(AXES, None), P(), P()),
        check_vma=False,
    )
```

```python
import functools

import jax
import jax.numpy as jnp
from jax import lax
from jax.experimental import pallas as pl
from jax.experimental.pallas import tpu as pltpu
from jax.sharding import PartitionSpec as P

AXES = ("dom", "sub")
BF16 = jnp.bfloat16
F8 = jnp.float8_e4m3fn
F32 = jnp.float32
I32 = jnp.int32
I16 = jnp.int16
LANES = 128
BLOCK = 256
ROWS = 512
EARLY = 2
VMEM_LIMIT = 24 * 2**20


def tdot(left, right):
    return lax.dot_general(left, right, (((0,), (0,)), ((), ())), preferred_element_type=F32)


def dot_transposed(left, right):
    return lax.dot_general(left, right, (((1,), (1,)), ((), ())), preferred_element_type=F32)


def dot(left, right):
    return jnp.dot(left, right, preferred_element_type=F32)


def exchange(rows):
    return lax.all_to_all(rows, AXES, split_axis=0, concat_axis=0, tiled=True)


def run(kernel, name, outs, vmem=(), hbm=(), smem=(), scratch=(), flops=0, moved=0, aliases=None):
    in_place = pl.BlockSpec(memory_space=pltpu.VMEM)
    remote = pl.BlockSpec(memory_space=pltpu.HBM)
    return pl.pallas_call(
        kernel,
        out_shape=tuple(outs),
        in_specs=[pl.BlockSpec(memory_space=pltpu.SMEM)] * len(smem)
        + [remote] * len(hbm)
        + [in_place] * len(vmem),
        out_specs=tuple(remote if out.memory_space == pltpu.HBM else in_place for out in outs),
        scratch_shapes=tuple(scratch),
        compiler_params=pltpu.CompilerParams(vmem_limit_bytes=VMEM_LIMIT),
        cost_estimate=pl.CostEstimate(flops=flops, bytes_accessed=moved, transcendentals=0),
        input_output_aliases=aliases or {},
        name=name,
    )(
        *smem,
        *[pltpu.with_memory_space_constraint(arg, pltpu.HBM) for arg in hbm],
        *[pltpu.with_memory_space_constraint(arg, pltpu.VMEM) for arg in vmem],
    )


def staged_for(count, *arrays):
    buffers = [pltpu.VMEM(array.shape, array.dtype) for array in arrays]
    return buffers + [pltpu.SemaphoreType.DMA((count,))]


def start_all(sources, buffers, semaphores):
    copies = [
        pltpu.make_async_copy(source, buffer, semaphores.at[index])
        for index, (source, buffer) in enumerate(zip(sources, buffers))
    ]
    for copy in copies:
        copy.start()
    return copies


def iota(shape, dim, dtype=I32):
    return lax.broadcasted_iota(dtype, shape, dim)


def one_hot(mask, dtype):
    return jnp.where(mask, 1.0, 0.0).astype(dtype)


def edge_hot(mask):
    return jnp.where(mask, jnp.ones(mask.shape, BF16), jnp.zeros(mask.shape, BF16)).astype(F8)


def by_peer(rows, devices):
    return rows.reshape(devices, rows.shape[0] // devices, rows.shape[1]).astype(BF16)


def by_row(parts):
    return parts.astype(F32).reshape(parts.shape[0] * parts.shape[1], parts.shape[2])


def inverse_columns(in_count):
    return (1.0 / jnp.maximum(in_count[...], 1).astype(F32)).T


def send(array, out, semaphore):
    copy = pltpu.make_async_copy(array, out, semaphore)
    copy.start()
    copy.wait()


def pick_rows(
    features_at,
    cotangent_at,
    in_count_at,
    sent_at,
    sources_at,
    targets_at,
    payload,
    scaled,
    picking,
    sources,
    targets,
    features,
    cotangent,
    in_count,
    sent,
    semaphores,
    rows_out,
    out_semaphore,
):
    node_dev, width = features.shape
    per_peer, devices = sent.shape
    mirrors = devices * per_peer
    copies = start_all(
        [sent_at, in_count_at, cotangent_at, features_at, sources_at, targets_at],
        [sent, in_count, cotangent, features, sources, targets],
        semaphores,
    )
    copies[0].wait()
    spread_out = one_hot(
        iota((mirrors, devices), 0) // per_peer == iota((mirrors, devices), 1), BF16
    )
    high = dot_transposed(spread_out, (sent[...] >> 5).astype(F32).astype(BF16))
    low = dot_transposed(spread_out, (sent[...] & 31).astype(F32).astype(BF16))
    within = iota((mirrors, per_peer), 0) % per_peer == iota((mirrors, per_peer), 1)
    owner = jnp.sum(jnp.where(within, high * 32.0 + low, 0.0), axis=1, keepdims=True).astype(I32)
    picked = iota((mirrors, node_dev), 1) == owner
    picks = one_hot(picked, BF16)
    picking[...] = picks
    copies[1].wait()
    inverse_rows = 1.0 / jnp.maximum(in_count[...], 1).astype(F32)
    owner_inverse = jnp.zeros((mirrors, LANES), F32)
    for block in range(node_dev // LANES):
        lanes = slice(block * LANES, (block + 1) * LANES)
        owner_inverse += jnp.where(picked[:, lanes], inverse_rows[block : block + 1, :], 0.0)
    owner_inverse = jnp.sum(owner_inverse, axis=1, keepdims=True)
    copies[2].wait()
    back = dot(picks, cotangent[...]) * owner_inverse
    rows_out[:, :, width:] = by_peer(back, devices)
    copies[3].wait()
    rows_out[:, :, :width] = by_peer(dot(picks, features[...]), devices)
    out_copy = pltpu.make_async_copy(rows_out, payload, out_semaphore)
    out_copy.start()
    columns = inverse_rows.T
    for block in range(node_dev // LANES):
        rows = pl.ds(block * LANES, LANES)
        scaled[rows, :] = (
            cotangent[rows, :].astype(F32) * columns[:, block : block + 1]
        ).astype(BF16)
    copies[4].wait()
    copies[5].wait()
    out_copy.wait()


def fill_from_hot(from_hot, sources):
    edges, slots = from_hot.shape
    source_columns = sources[...].T
    lane_ids = iota((LANES, slots), 1, I16)
    for block in range(edges // LANES):
        column = jnp.broadcast_to(source_columns[:, block : block + 1], (LANES, LANES)).astype(I16)
        column = jnp.concatenate([column] * (slots // LANES), axis=1)
        from_hot[pl.ds(block * LANES, LANES), :] = edge_hot(lane_ids == column)


def fill_into_hot(into_hot, targets, edge_count, first, place, size):
    edge_ids = iota(targets.shape, 0) * LANES + iota(targets.shape, 1)
    target_rows = jnp.where(edge_ids < edge_count[0], targets[...], -1).astype(I16)
    row_ids = iota((LANES, LANES), 0, I16)
    for block in range(into_hot.shape[1] // LANES):
        target_row = target_rows[block : block + 1, :]
        for part in range(0, size, LANES):
            into_hot[pl.ds(place + part, LANES), pl.ds(block * LANES, LANES)] = edge_hot(
                row_ids + jnp.int16(first + part) == target_row
            )


def count_edges(
    edge_count,
    features_at,
    scaled,
    sources,
    targets,
    counts_at,
    scaled_at,
    mirror_rows,
    partial_out,
    features,
    semaphore,
    from_hot,
    into_hot,
    counts,
    out_semaphores,
):
    node_dev, width = features.shape
    slots, edges = into_hot.shape
    early = counts.shape[0]
    feature_copy = pltpu.make_async_copy(features_at, features, semaphore)
    feature_copy.start()
    sends = [pltpu.make_async_copy(scaled, scaled_at, out_semaphores.at[early // BLOCK])]
    sends[0].start()
    fill_from_hot(from_hot, sources)
    for start in range(0, early, BLOCK):
        rows = pl.ds(start, BLOCK)
        fill_into_hot(into_hot, targets, edge_count, start, start, BLOCK)
        counts[rows, :] = dot(into_hot[rows, :], from_hot[...]).astype(BF16)
        copy = pltpu.make_async_copy(
            counts.at[rows], counts_at.at[rows], out_semaphores.at[start // BLOCK]
        )
        copy.start()
        sends.append(copy)
    fill_into_hot(into_hot, targets, edge_count, early, early, slots - early)
    mirror_rows[...] = dot(into_hot[node_dev:, :], from_hot[...]).astype(BF16)
    late_columns = dot(into_hot[early:node_dev, :], from_hot[:, node_dev:]).astype(BF16)
    feature_copy.wait()
    partial_out[:, :width] = dot(mirror_rows[:, :node_dev], features[...])
    partial_out[:, width:] = tdot(counts[:, node_dev:], scaled[:early, :]) + tdot(
        late_columns, scaled[early:, :]
    )
    for copy in sends:
        copy.wait()


def mirror_sums(partial_in, mirror_rows, mirrored, payload, rows_out, out_semaphore):
    devices, _, columns = rows_out.shape
    width = columns // 2
    received = mirrored[...]
    mirror_counts = mirror_rows[:, mirror_rows.shape[1] - mirror_rows.shape[0] :]
    front = partial_in[:, :width] + dot(mirror_counts, received[:, :width])
    back = partial_in[:, width:] + tdot(mirror_counts, received[:, width:])
    rows_out[:, :, :width] = by_peer(front, devices)
    rows_out[:, :, width:] = by_peer(back, devices)
    send(rows_out, payload, out_semaphore)


def local_sums(
    edge_count,
    early_at,
    features_at,
    scaled_at,
    sources,
    targets,
    mirrored,
    mirror_rows,
    forward,
    features,
    backward_at,
    mirror_at,
    late_at,
    from_hot,
    into_hot,
    counts,
    scaled,
    backward,
    semaphores,
    out_semaphores,
):
    node_dev, width = features.shape
    early = early_at.shape[0]
    loads = start_all(
        [scaled_at, early_at, features_at],
        [scaled, counts.at[pl.ds(0, early)], features],
        semaphores,
    )
    blocks = node_dev // BLOCK
    sends = [pltpu.make_async_copy(mirror_rows, mirror_at, out_semaphores.at[blocks])]
    sends[0].start()
    fill_from_hot(from_hot, sources)
    for start in range(early, node_dev, BLOCK):
        rows = pl.ds(start - early, BLOCK)
        fill_into_hot(into_hot, targets, edge_count, start, start - early, BLOCK)
        counts[pl.ds(start, BLOCK), :] = dot(into_hot[rows, :], from_hot[...]).astype(BF16)
    late = pl.ds(early, node_dev - early)
    sends.append(
        pltpu.make_async_copy(counts.at[late], late_at, out_semaphores.at[blocks + 1])
    )
    sends[1].start()
    for copy in loads:
        copy.wait()
    for index, start in enumerate(range(0, node_dev, BLOCK)):
        rows = pl.ds(start, BLOCK)
        backward[rows, :] = tdot(counts[:, rows], scaled[...]) + tdot(
            mirror_rows[:, rows], mirrored[:, width:]
        )
        copy = pltpu.make_async_copy(
            backward.at[rows], backward_at.at[rows], out_semaphores.at[index]
        )
        copy.start()
        sends.append(copy)
    for start in range(0, node_dev, BLOCK):
        rows = pl.ds(start, BLOCK)
        forward[rows, :] = dot(counts[rows, :node_dev], features[...]) + dot(
            counts[rows, node_dev:], mirrored[:, :width]
        )
    for copy in sends:
        copy.wait()


def block_inverse(columns, index, size=BLOCK):
    first = index * size // LANES
    return jnp.concatenate(
        [columns[:, b : b + 1] for b in range(first, first + size // LANES)], axis=0
    )


def middle(
    core,
    cotangent_at,
    backward_at,
    forward,
    returned,
    picking,
    features,
    w_nbr_one,
    w_self_one,
    bias_one,
    w_nbr_two,
    w_self_two,
    in_count,
    grad_z,
    sent_half,
    bias_rows,
    mean_one,
    h_one,
    pulled,
    cotangent,
    backward,
    semaphores,
    slope,
):
    node_dev, width = features.shape
    blocks = [pl.ds(start, ROWS) for start in range(0, node_dev, ROWS)]
    copies = start_all(
        [backward_at, cotangent_at],
        [backward, cotangent],
        semaphores,
    )
    columns = inverse_columns(in_count)
    for index, rows in enumerate(blocks):
        placed = tdot(picking[:, rows], returned[:, :width])
        mean = ((forward[rows, :] + placed) * block_inverse(columns, index, ROWS)).astype(BF16)
        mean_one[rows, :] = mean
        z_one = (
            dot(features[rows, :], w_self_one[...]) + dot(mean, w_nbr_one[...]) + bias_one[...]
        )
        sigmoid = 1.0 / (1.0 + jnp.exp(-z_one))
        h_one[rows, :] = (z_one * sigmoid).astype(BF16)
        slope[rows, :] = sigmoid * (1.0 + z_one * (1.0 - sigmoid))
    for copy in copies:
        copy.wait()
    bias_total = jnp.zeros((1, width), F32)
    for rows in blocks:
        pull = (backward[rows, :] + tdot(picking[:, rows], returned[:, width:])).astype(BF16)
        pulled[rows, :] = pull
        grad_h = dot_transposed(cotangent[rows, :], w_self_two[...]) + dot_transposed(
            pull, w_nbr_two[...]
        )
        grad = (grad_h * slope[rows, :]).astype(BF16)
        grad_z[rows, :] = grad
        bias_total += jnp.sum(grad.astype(F32), axis=0, keepdims=True)
    bias_high = bias_total.astype(BF16).astype(F32)
    bias_low = bias_total - bias_high
    for row, part in enumerate((bias_high, bias_low)):
        for block in range(width // LANES):
            bias_rows[row * (width // LANES) + block : row * (width // LANES) + block + 1, :] = (
                part[:, block * LANES : (block + 1) * LANES]
            )

    @pl.when(core[0] == 0)
    def _():
        sent_half[:width, :] = tdot(h_one[...], cotangent[...]).astype(BF16)
        sent_half[width:, :] = tdot(h_one[...], pulled[...]).astype(BF16)

    @pl.when(core[0] == 1)
    def _():
        sent_half[:width, :] = tdot(features[...], grad_z[...]).astype(BF16)
        sent_half[width:, :] = tdot(mean_one[...], grad_z[...]).astype(BF16)


def messages(
    core,
    in_count,
    grad_z,
    w_nbr_one,
    picking,
    features,
    mean_one,
    h_one,
    cotangent,
    pulled,
    message_one,
    picked,
    own_half,
):
    node_dev, width = grad_z.shape
    columns = inverse_columns(in_count)
    for index, start in enumerate(range(0, node_dev, BLOCK)):
        rows = pl.ds(start, BLOCK)
        message_one[rows, :] = (
            dot_transposed(grad_z[rows, :], w_nbr_one[...]) * block_inverse(columns, index)
        ).astype(BF16)
    picked[...] = dot(picking[...], message_one[...])

    @pl.when(core[0] == 0)
    def _():
        own_half[:width, :] = tdot(features[...], grad_z[...])
        own_half[width:, :] = tdot(mean_one[...], grad_z[...])

    @pl.when(core[0] == 1)
    def _():
        own_half[:width, :] = tdot(h_one[...], cotangent[...])
        own_half[width:, :] = tdot(h_one[...], pulled[...])


def join_first(own_half, other_half, picked, bias_rows, payload, rows_out, out_semaphore):
    devices, per_peer, _ = rows_out.shape
    mirrors, width = picked.shape
    groups = own_half.shape[0] // mirrors
    rows_out[:, :, :width] = by_peer(picked[...], devices)
    for group in range(groups):
        rows = pl.ds(group * mirrors, mirrors)
        rows_out[:, :, (group + 1) * width : (group + 2) * width] = by_peer(
            own_half[rows, :] + other_half[rows, :].astype(F32), devices
        )
    rows_out[:, :, (groups + 1) * width :] = jnp.broadcast_to(
        bias_rows[...][None], (devices, per_peer, LANES)
    ).astype(BF16)
    send(rows_out, payload, out_semaphore)


def local_back(
    early_at,
    late_at,
    mirror_at,
    message_one,
    grad_z,
    w_self_one,
    mirror_out,
    local_out,
    mirror_rows,
    counts,
    semaphores,
):
    node_dev, width = grad_z.shape
    early = early_at.shape[0]
    copies = start_all(
        [early_at, late_at, mirror_at],
        [counts.at[pl.ds(0, early)], counts.at[pl.ds(early, node_dev - early)], mirror_rows],
        semaphores,
    )
    for start in range(0, node_dev, BLOCK):
        rows = pl.ds(start, BLOCK)
        local_out[rows, :] = dot_transposed(grad_z[rows, :], w_self_one[...])
    for copy in copies:
        copy.wait()
    mirror_out[...] = tdot(counts[:, node_dev:], message_one[...])
    for start in range(0, node_dev, BLOCK):
        rows = pl.ds(start, BLOCK)
        local_out[rows, :] += tdot(counts[:, rows], message_one[...])


def join_second(
    norm_factor,
    received,
    mirror_partial,
    mirror_rows,
    payload,
    mirrored_out,
    bias_total,
):
    devices, per_peer, _ = payload.shape
    mirrors, width = mirror_partial.shape
    groups = payload.shape[2] // width - 1
    mirrored = by_row(received[:, :, :width]).astype(BF16)
    mirrored_out[...] = mirrored
    partial_sums = mirror_partial[...] + tdot(
        mirror_rows[:, mirror_rows.shape[1] - mirrors :], mirrored
    )
    payload[:, :, :width] = by_peer(partial_sums, devices)
    for group in range(groups):
        lanes = slice((group + 1) * width, (group + 2) * width)
        owned = (
            jnp.sum(
                received[:, :, lanes].astype(F32).reshape(devices // 2, 2, per_peer, width), axis=0
            )
            * norm_factor
        ).astype(BF16)
        payload[:, :, lanes] = jnp.broadcast_to(
            owned[None], (devices // 2, 2, per_peer, width)
        ).reshape(devices, per_peer, width)
    sums = (
        jnp.sum(received[:, :, (groups + 1) * width :].astype(F32), axis=0) * norm_factor
    )
    parts = width // LANES
    for block in range(parts):
        bias_total[:, block * LANES : (block + 1) * LANES] = (
            sums[block : block + 1, :] + sums[parts + block : parts + block + 1, :]
        )


def finish(
    core,
    received,
    mirrored,
    picking,
    mirror_rows,
    local_grad,
    bias_total,
    features_at,
    weights_at,
    bias_at,
    features_out,
    weights_out,
    semaphores,
):
    devices, per_peer, _ = received.shape
    node_dev, width = local_grad.shape
    mirrors = picking.shape[0]
    half = weights_out.shape[0]
    for group in range(half // mirrors):
        weights_out[pl.ds(group * mirrors, mirrors), :] = by_row(
            received[:, :, (group + 1) * width : (group + 2) * width]
        )
    mine = pl.multiple_of(core[0] * half, half)
    weights_copy = pltpu.make_async_copy(
        weights_out, weights_at.at[pl.ds(mine, half)], semaphores.at[0]
    )
    weights_copy.start()
    bias_copy = pltpu.make_async_copy(bias_total, bias_at, semaphores.at[2])
    bias_copy.start()
    returned = by_row(received[:, :, :width]).astype(BF16)
    for start in range(0, node_dev, BLOCK):
        rows = pl.ds(start, BLOCK)
        features_out[rows, :] = (
            local_grad[rows, :]
            + tdot(picking[:, rows], returned)
            + tdot(mirror_rows[:, rows], mirrored[...])
        ).astype(BF16)
    features_copy = pltpu.make_async_copy(features_out, features_at, semaphores.at[1])
    features_copy.start()
    weights_copy.wait()
    bias_copy.wait()
    features_copy.wait()


def finish_other(core, weights_in, received, weights_at, weights_out, semaphore):
    half, width = weights_out.shape
    devices, per_peer, columns = received.shape
    mirrors = devices * per_peer
    for group in range(half // mirrors):
        weights_out[pl.ds(group * mirrors, mirrors), :] = by_row(
            received[:, :, (group + 1) * width : (group + 2) * width]
        )
    other = pl.multiple_of((1 - core[0]) * half, half)
    send(weights_out, weights_at.at[pl.ds(other, half)], semaphore)


def shards(
    features,
    cotangent,
    w_self_one,
    w_nbr_one,
    bias_one,
    w_self_two,
    w_nbr_two,
    in_count,
    send_list,
    src_slot,
    dst_slot,
    edge_count,
):
    node_dev, width = features.shape
    devices = lax.axis_size("dom") * lax.axis_size("sub")
    per_peer = send_list.shape[2]
    mirrors = devices * per_peer
    slots = node_dev + mirrors
    edges = src_slot.shape[1]
    core = lax.axis_index("sub") % 2
    swap = [(i, i ^ 1) for i in range(devices)]
    in_count = in_count.reshape(-1, LANES)
    sent = send_list[0].T
    sources = src_slot.reshape(-1, LANES)
    targets = dst_slot.reshape(-1, LANES)
    blocks = node_dev // BLOCK

    payload_shape = (devices, per_peer, 2 * width)
    payload, scaled, picking, sources, targets = run(
        pick_rows,
        "pick_rows",
        [
            pltpu.HBM(payload_shape, BF16),
            pltpu.VMEM((node_dev, width), BF16),
            pltpu.VMEM((mirrors, node_dev), BF16),
            pltpu.VMEM(sources.shape, I32),
            pltpu.VMEM(targets.shape, I32),
        ],
        hbm=[features, cotangent, in_count, sent, sources, targets],
        scratch=staged_for(6, features, cotangent, in_count, sent)
        + [pltpu.VMEM(payload_shape, BF16), pltpu.SemaphoreType.DMA],
        flops=4 * mirrors * node_dev * width,
    )
    mirrored = exchange(payload).reshape(mirrors, 2 * width)

    rows_bf16 = pltpu.VMEM((node_dev, width), BF16)
    rows_f32 = pltpu.VMEM((node_dev, width), F32)
    early = node_dev * EARLY // 4
    early_counts, scaled, mirror_rows, partial_sums = run(
        count_edges,
        "count_edges",
        [
            pltpu.HBM((early, slots), BF16),
            pltpu.HBM((node_dev, width), BF16),
            pltpu.VMEM((mirrors, slots), BF16),
            pltpu.VMEM((mirrors, 2 * width), F32),
        ],
        smem=[edge_count],
        hbm=[features],
        vmem=[scaled, sources, targets],
        scratch=[
            rows_bf16,
            pltpu.SemaphoreType.DMA,
            pltpu.VMEM((edges, slots), F8),
            pltpu.VMEM((slots, edges), F8),
            pltpu.VMEM((early, slots), BF16),
            pltpu.SemaphoreType.DMA((early // BLOCK + 1,)),
        ],
        flops=2 * (early + 2 * mirrors) * edges * slots,
    )
    (payload,) = run(
        mirror_sums,
        "mirror_sums",
        [pltpu.HBM(payload_shape, BF16)],
        vmem=[partial_sums, mirror_rows, mirrored],
        scratch=[pltpu.VMEM(payload_shape, BF16), pltpu.SemaphoreType.DMA],
        flops=4 * mirrors * mirrors * width,
    )
    returned = exchange(payload).reshape(mirrors, 2 * width)
    forward, features_in, backward, mirror_rows, late_counts = run(
        local_sums,
        "local_sums",
        [
            rows_f32,
            rows_bf16,
            pltpu.HBM((node_dev, width), F32),
            pltpu.HBM((mirrors, slots), BF16),
            pltpu.HBM((node_dev - early, slots), BF16),
        ],
        smem=[edge_count],
        hbm=[early_counts, features, scaled],
        vmem=[sources, targets, mirrored, mirror_rows],
        scratch=[
            pltpu.VMEM((edges, slots), F8),
            pltpu.VMEM((node_dev - early, edges), F8),
            pltpu.VMEM((node_dev, slots), BF16),
            rows_bf16,
            rows_f32,
            pltpu.SemaphoreType.DMA((3,)),
            pltpu.SemaphoreType.DMA((blocks + 2,)),
        ],
        flops=4 * node_dev * slots * width + 2 * (node_dev - early) * edges * slots,
    )

    half = 2 * width
    grad_z_one, sent_half, bias_rows, mean_one, h_one, pulled, cotangent_in = run(
        middle,
        "middle",
        [
            rows_bf16,
            pltpu.VMEM((half, width), BF16),
            pltpu.VMEM((2 * width // LANES, LANES), F32),
            rows_bf16,
            rows_bf16,
            rows_bf16,
            rows_bf16,
        ],
        smem=[core.reshape(1)],
        hbm=[cotangent, backward],
        vmem=[
            forward,
            returned,
            picking,
            features_in,
            w_nbr_one,
            w_self_one,
            bias_one.reshape(1, -1),
            w_nbr_two,
            w_self_two,
            in_count,
        ],
        scratch=[
            rows_f32,
            pltpu.SemaphoreType.DMA((2,)),
            rows_f32,
        ],
        flops=20 * node_dev * width * width,
    )
    other_half = lax.ppermute(sent_half, AXES, swap)
    message_one, picked, own_half = run(
        messages,
        "messages",
        [rows_bf16, pltpu.VMEM((mirrors, width), F32), pltpu.VMEM((half, width), F32)],
        smem=[core.reshape(1)],
        vmem=[
            in_count,
            grad_z_one,
            w_nbr_one,
            picking,
            features_in,
            mean_one,
            h_one,
            cotangent_in,
            pulled,
        ],
        flops=6 * node_dev * width * width,
    )

    columns = width * (half // mirrors + 1)
    payload_shape = (devices, per_peer, columns + LANES)
    (payload,) = run(
        join_first,
        "join_first",
        [pltpu.HBM(payload_shape, BF16)],
        vmem=[own_half, other_half, picked, bias_rows],
        scratch=[pltpu.VMEM(payload_shape, BF16), pltpu.SemaphoreType.DMA],
    )
    received = exchange(payload)
    mirror_back, local_grad, mirror_rows = run(
        local_back,
        "local_back",
        [
            pltpu.VMEM((mirrors, width), F32),
            pltpu.VMEM((node_dev, width), F32),
            pltpu.VMEM((mirrors, slots), BF16),
        ],
        hbm=[early_counts, late_counts, mirror_rows],
        vmem=[message_one, grad_z_one, w_self_one],
        scratch=[pltpu.VMEM((node_dev, slots), BF16), pltpu.SemaphoreType.DMA((3,))],
        flops=2 * node_dev * (slots + width) * width,
    )
    norm_factor = float(node_dev * devices) ** -0.5
    payload, mirrored, bias_total = run(
        functools.partial(join_second, norm_factor),
        "join_second",
        [
            pltpu.VMEM((devices, per_peer, columns), BF16),
            pltpu.VMEM((mirrors, width), BF16),
            pltpu.VMEM((1, width), F32),
        ],
        vmem=[received, mirror_back, mirror_rows],
    )
    received = exchange(payload)
    other = lax.ppermute(received, AXES, swap)
    grad_features, grad_weights, grad_bias = run(
        finish,
        "finish",
        [
            pltpu.HBM((node_dev, width), BF16),
            pltpu.HBM((2 * half, width), F32),
            pltpu.HBM((1, width), F32),
        ],
        smem=[core.reshape(1)],
        vmem=[received, mirrored, picking, mirror_rows, local_grad, bias_total],
        scratch=[
            pltpu.VMEM((node_dev, width), BF16),
            pltpu.VMEM((half, width), F32),
            pltpu.SemaphoreType.DMA((3,)),
        ],
        flops=6 * node_dev * mirrors * width,
    )
    (grad_weights,) = run(
        finish_other,
        "finish_other",
        [pltpu.HBM((2 * half, width), F32)],
        smem=[core.reshape(1)],
        hbm=[grad_weights],
        vmem=[other],
        scratch=[pltpu.VMEM((half, width), F32), pltpu.SemaphoreType.DMA],
        aliases={1: 0},
    )
    return (
        grad_features,
        grad_weights.reshape(4, width, width),
        grad_bias.reshape(width),
    )


def solution(mesh):
    by_device = P(AXES)
    return jax.shard_map(
        shards,
        mesh=mesh,
        in_specs=(
            P(AXES, None),
            P(AXES, None),
            P(),
            P(),
            P(),
            P(),
            P(),
            by_device,
            P(AXES, None, None),
            P(AXES, None),
            P(AXES, None),
            by_device,
        ),
        out_specs=(P(AXES, None), P(), P()),
        check_vma=False,
    )
```

```python
import functools

import jax
import jax.numpy as jnp
from jax import lax
from jax.experimental import pallas as pl
from jax.experimental.pallas import tpu as pltpu
from jax.sharding import PartitionSpec as P

AXES = ("dom", "sub")
BF16 = jnp.bfloat16
F8 = jnp.float8_e4m3fn
F32 = jnp.float32
I32 = jnp.int32
I16 = jnp.int16
LANES = 128
BLOCK = 256
ROWS = 512
EARLY = 2
VMEM_LIMIT = 24 * 2**20


def tdot(left, right):
    return lax.dot_general(left, right, (((0,), (0,)), ((), ())), preferred_element_type=F32)


def dot_transposed(left, right):
    return lax.dot_general(left, right, (((1,), (1,)), ((), ())), preferred_element_type=F32)


def dot(left, right):
    return jnp.dot(left, right, preferred_element_type=F32)


def exchange(rows):
    return lax.all_to_all(rows, AXES, split_axis=0, concat_axis=0, tiled=True)


def run(kernel, name, outs, vmem=(), hbm=(), smem=(), scratch=(), flops=0, moved=0):
    in_place = pl.BlockSpec(memory_space=pltpu.VMEM)
    remote = pl.BlockSpec(memory_space=pltpu.HBM)
    return pl.pallas_call(
        kernel,
        out_shape=tuple(outs),
        in_specs=[pl.BlockSpec(memory_space=pltpu.SMEM)] * len(smem)
        + [remote] * len(hbm)
        + [in_place] * len(vmem),
        out_specs=tuple(remote if out.memory_space == pltpu.HBM else in_place for out in outs),
        scratch_shapes=tuple(scratch),
        compiler_params=pltpu.CompilerParams(vmem_limit_bytes=VMEM_LIMIT),
        cost_estimate=pl.CostEstimate(flops=flops, bytes_accessed=moved, transcendentals=0),
        name=name,
    )(
        *smem,
        *[pltpu.with_memory_space_constraint(arg, pltpu.HBM) for arg in hbm],
        *[pltpu.with_memory_space_constraint(arg, pltpu.VMEM) for arg in vmem],
    )


def staged_for(count, *arrays):
    buffers = [pltpu.VMEM(array.shape, array.dtype) for array in arrays]
    return buffers + [pltpu.SemaphoreType.DMA((count,))]


def start_all(sources, buffers, semaphores):
    copies = [
        pltpu.make_async_copy(source, buffer, semaphores.at[index])
        for index, (source, buffer) in enumerate(zip(sources, buffers))
    ]
    for copy in copies:
        copy.start()
    return copies


def iota(shape, dim, dtype=I32):
    return lax.broadcasted_iota(dtype, shape, dim)


def one_hot(mask, dtype):
    return jnp.where(mask, 1.0, 0.0).astype(dtype)


def edge_hot(mask):
    return jnp.where(mask, jnp.ones(mask.shape, BF16), jnp.zeros(mask.shape, BF16)).astype(F8)


def by_peer(rows, devices):
    return rows.reshape(devices, rows.shape[0] // devices, rows.shape[1]).astype(BF16)


def by_row(parts):
    return parts.astype(F32).reshape(parts.shape[0] * parts.shape[1], parts.shape[2])


def inverse_columns(in_count):
    return (1.0 / jnp.maximum(in_count[...], 1).astype(F32)).T


def send(array, out, semaphore):
    copy = pltpu.make_async_copy(array, out, semaphore)
    copy.start()
    copy.wait()


def pick_rows(
    features_at,
    cotangent_at,
    in_count_at,
    sent_at,
    sources_at,
    targets_at,
    payload,
    scaled,
    picking,
    sources,
    targets,
    features,
    cotangent,
    in_count,
    sent,
    semaphores,
    rows_out,
    out_semaphore,
):
    node_dev, width = features.shape
    per_peer, devices = sent.shape
    mirrors = devices * per_peer
    copies = start_all(
        [sent_at, in_count_at, cotangent_at, features_at, sources_at, targets_at],
        [sent, in_count, cotangent, features, sources, targets],
        semaphores,
    )
    copies[0].wait()
    spread_out = one_hot(
        iota((mirrors, devices), 0) // per_peer == iota((mirrors, devices), 1), BF16
    )
    high = dot_transposed(spread_out, (sent[...] >> 5).astype(F32).astype(BF16))
    low = dot_transposed(spread_out, (sent[...] & 31).astype(F32).astype(BF16))
    within = iota((mirrors, per_peer), 0) % per_peer == iota((mirrors, per_peer), 1)
    owner = jnp.sum(jnp.where(within, high * 32.0 + low, 0.0), axis=1, keepdims=True).astype(I32)
    picked = iota((mirrors, node_dev), 1) == owner
    picks = one_hot(picked, BF16)
    picking[...] = picks
    copies[1].wait()
    inverse_rows = 1.0 / jnp.maximum(in_count[...], 1).astype(F32)
    owner_inverse = jnp.zeros((mirrors, LANES), F32)
    for block in range(node_dev // LANES):
        lanes = slice(block * LANES, (block + 1) * LANES)
        owner_inverse += jnp.where(picked[:, lanes], inverse_rows[block : block + 1, :], 0.0)
    owner_inverse = jnp.sum(owner_inverse, axis=1, keepdims=True)
    copies[2].wait()
    back = dot(picks, cotangent[...]) * owner_inverse
    rows_out[:, :, width:] = by_peer(back, devices)
    copies[3].wait()
    rows_out[:, :, :width] = by_peer(dot(picks, features[...]), devices)
    out_copy = pltpu.make_async_copy(rows_out, payload, out_semaphore)
    out_copy.start()
    columns = inverse_rows.T
    for block in range(node_dev // LANES):
        rows = pl.ds(block * LANES, LANES)
        scaled[rows, :] = (
            cotangent[rows, :].astype(F32) * columns[:, block : block + 1]
        ).astype(BF16)
    copies[4].wait()
    copies[5].wait()
    out_copy.wait()


def fill_from_hot(from_hot, sources):
    edges, slots = from_hot.shape
    source_columns = sources[...].T
    lane_ids = iota((LANES, slots), 1, I16)
    for block in range(edges // LANES):
        column = jnp.broadcast_to(source_columns[:, block : block + 1], (LANES, LANES)).astype(I16)
        column = jnp.concatenate([column] * (slots // LANES), axis=1)
        from_hot[pl.ds(block * LANES, LANES), :] = edge_hot(lane_ids == column)


def fill_into_hot(into_hot, targets, edge_count, first, place, size):
    edge_ids = iota(targets.shape, 0) * LANES + iota(targets.shape, 1)
    target_rows = jnp.where(edge_ids < edge_count[0], targets[...], -1).astype(I16)
    row_ids = iota((LANES, LANES), 0, I16)
    for block in range(into_hot.shape[1] // LANES):
        target_row = target_rows[block : block + 1, :]
        for part in range(0, size, LANES):
            into_hot[pl.ds(place + part, LANES), pl.ds(block * LANES, LANES)] = edge_hot(
                row_ids + jnp.int16(first + part) == target_row
            )


def count_edges(
    edge_count,
    features_at,
    scaled,
    sources,
    targets,
    counts_at,
    scaled_at,
    mirror_rows,
    partial_out,
    features,
    semaphore,
    from_hot,
    into_hot,
    counts,
    out_semaphores,
):
    node_dev, width = features.shape
    slots, edges = into_hot.shape
    early = counts.shape[0]
    feature_copy = pltpu.make_async_copy(features_at, features, semaphore)
    feature_copy.start()
    sends = [pltpu.make_async_copy(scaled, scaled_at, out_semaphores.at[early // BLOCK])]
    sends[0].start()
    fill_from_hot(from_hot, sources)
    for start in range(0, early, BLOCK):
        rows = pl.ds(start, BLOCK)
        fill_into_hot(into_hot, targets, edge_count, start, start, BLOCK)
        counts[rows, :] = dot(into_hot[rows, :], from_hot[...]).astype(BF16)
        copy = pltpu.make_async_copy(
            counts.at[rows], counts_at.at[rows], out_semaphores.at[start // BLOCK]
        )
        copy.start()
        sends.append(copy)
    fill_into_hot(into_hot, targets, edge_count, early, early, slots - early)
    mirror_rows[...] = dot(into_hot[node_dev:, :], from_hot[...]).astype(BF16)
    late_columns = dot(into_hot[early:node_dev, :], from_hot[:, node_dev:]).astype(BF16)
    feature_copy.wait()
    partial_out[:, :width] = dot(mirror_rows[:, :node_dev], features[...])
    partial_out[:, width:] = tdot(counts[:, node_dev:], scaled[:early, :]) + tdot(
        late_columns, scaled[early:, :]
    )
    for copy in sends:
        copy.wait()


def mirror_sums(partial_in, mirror_rows, mirrored, payload, rows_out, out_semaphore):
    devices, _, columns = rows_out.shape
    width = columns // 2
    received = mirrored[...]
    mirror_counts = mirror_rows[:, mirror_rows.shape[1] - mirror_rows.shape[0] :]
    front = partial_in[:, :width] + dot(mirror_counts, received[:, :width])
    back = partial_in[:, width:] + tdot(mirror_counts, received[:, width:])
    rows_out[:, :, :width] = by_peer(front, devices)
    rows_out[:, :, width:] = by_peer(back, devices)
    send(rows_out, payload, out_semaphore)


def local_sums(
    edge_count,
    early_at,
    features_at,
    scaled_at,
    sources,
    targets,
    mirrored,
    mirror_rows,
    forward,
    features,
    backward_at,
    mirror_at,
    late_at,
    from_hot,
    into_hot,
    counts,
    scaled,
    backward,
    semaphores,
    out_semaphores,
):
    node_dev, width = features.shape
    early = early_at.shape[0]
    loads = start_all(
        [scaled_at, early_at, features_at],
        [scaled, counts.at[pl.ds(0, early)], features],
        semaphores,
    )
    blocks = node_dev // BLOCK
    sends = [pltpu.make_async_copy(mirror_rows, mirror_at, out_semaphores.at[blocks])]
    sends[0].start()
    fill_from_hot(from_hot, sources)
    for start in range(early, node_dev, BLOCK):
        rows = pl.ds(start - early, BLOCK)
        fill_into_hot(into_hot, targets, edge_count, start, start - early, BLOCK)
        counts[pl.ds(start, BLOCK), :] = dot(into_hot[rows, :], from_hot[...]).astype(BF16)
    late = pl.ds(early, node_dev - early)
    sends.append(
        pltpu.make_async_copy(counts.at[late], late_at, out_semaphores.at[blocks + 1])
    )
    sends[1].start()
    for copy in loads:
        copy.wait()
    for index, start in enumerate(range(0, node_dev, BLOCK)):
        rows = pl.ds(start, BLOCK)
        backward[rows, :] = tdot(counts[:, rows], scaled[...]) + tdot(
            mirror_rows[:, rows], mirrored[:, width:]
        )
        copy = pltpu.make_async_copy(
            backward.at[rows], backward_at.at[rows], out_semaphores.at[index]
        )
        copy.start()
        sends.append(copy)
    for start in range(0, node_dev, BLOCK):
        rows = pl.ds(start, BLOCK)
        forward[rows, :] = dot(counts[rows, :node_dev], features[...]) + dot(
            counts[rows, node_dev:], mirrored[:, :width]
        )
    for copy in sends:
        copy.wait()


def block_inverse(columns, index, size=BLOCK):
    first = index * size // LANES
    return jnp.concatenate(
        [columns[:, b : b + 1] for b in range(first, first + size // LANES)], axis=0
    )


def middle(
    core,
    cotangent_at,
    backward_at,
    early_at,
    forward,
    returned,
    picking,
    features,
    w_nbr_one,
    w_self_one,
    bias_one,
    w_nbr_two,
    w_self_two,
    in_count,
    grad_z,
    sent_half,
    bias_rows,
    mean_one,
    h_one,
    pulled,
    cotangent,
    early_counts,
    backward,
    semaphores,
    slope,
):
    node_dev, width = features.shape
    blocks = [pl.ds(start, ROWS) for start in range(0, node_dev, ROWS)]
    copies = start_all(
        [backward_at, cotangent_at],
        [backward, cotangent],
        semaphores,
    )
    columns = inverse_columns(in_count)
    for index, rows in enumerate(blocks):
        placed = tdot(picking[:, rows], returned[:, :width])
        mean = ((forward[rows, :] + placed) * block_inverse(columns, index, ROWS)).astype(BF16)
        mean_one[rows, :] = mean
        z_one = (
            dot(features[rows, :], w_self_one[...]) + dot(mean, w_nbr_one[...]) + bias_one[...]
        )
        sigmoid = 1.0 / (1.0 + jnp.exp(-z_one))
        h_one[rows, :] = (z_one * sigmoid).astype(BF16)
        slope[rows, :] = sigmoid * (1.0 + z_one * (1.0 - sigmoid))
    for copy in copies:
        copy.wait()
    early_copy = pltpu.make_async_copy(early_at, early_counts, semaphores.at[2])
    early_copy.start()
    bias_total = jnp.zeros((1, width), F32)
    for rows in blocks:
        pull = (backward[rows, :] + tdot(picking[:, rows], returned[:, width:])).astype(BF16)
        pulled[rows, :] = pull
        grad_h = dot_transposed(cotangent[rows, :], w_self_two[...]) + dot_transposed(
            pull, w_nbr_two[...]
        )
        grad = (grad_h * slope[rows, :]).astype(BF16)
        grad_z[rows, :] = grad
        bias_total += jnp.sum(grad.astype(F32), axis=0, keepdims=True)
    bias_high = bias_total.astype(BF16).astype(F32)
    bias_low = bias_total - bias_high
    for row, part in enumerate((bias_high, bias_low)):
        for block in range(width // LANES):
            bias_rows[row * (width // LANES) + block : row * (width // LANES) + block + 1, :] = (
                part[:, block * LANES : (block + 1) * LANES]
            )

    @pl.when(core[0] == 0)
    def _():
        sent_half[:width, :] = tdot(h_one[...], cotangent[...]).astype(BF16)
        sent_half[width:, :] = tdot(h_one[...], pulled[...]).astype(BF16)

    @pl.when(core[0] == 1)
    def _():
        sent_half[:width, :] = tdot(features[...], grad_z[...]).astype(BF16)
        sent_half[width:, :] = tdot(mean_one[...], grad_z[...]).astype(BF16)

    early_copy.wait()


def messages(
    core,
    late_at,
    mirror_at,
    in_count,
    grad_z,
    w_nbr_one,
    picking,
    features,
    mean_one,
    h_one,
    cotangent,
    pulled,
    message_one,
    picked,
    own_half,
    late_counts,
    mirror_rows,
    semaphores,
):
    node_dev, width = grad_z.shape
    copies = start_all([late_at, mirror_at], [late_counts, mirror_rows], semaphores)
    columns = inverse_columns(in_count)
    for index, start in enumerate(range(0, node_dev, BLOCK)):
        rows = pl.ds(start, BLOCK)
        message_one[rows, :] = (
            dot_transposed(grad_z[rows, :], w_nbr_one[...]) * block_inverse(columns, index)
        ).astype(BF16)
    picked[...] = dot(picking[...], message_one[...])

    @pl.when(core[0] == 0)
    def _():
        own_half[:width, :] = tdot(features[...], grad_z[...])
        own_half[width:, :] = tdot(mean_one[...], grad_z[...])

    @pl.when(core[0] == 1)
    def _():
        own_half[:width, :] = tdot(h_one[...], cotangent[...])
        own_half[width:, :] = tdot(h_one[...], pulled[...])

    for copy in copies:
        copy.wait()


def join_first(own_half, other_half, picked, bias_rows, payload):
    devices, per_peer, _ = payload.shape
    mirrors, width = picked.shape
    groups = own_half.shape[0] // mirrors
    payload[:, :, :width] = by_peer(picked[...], devices)
    for group in range(groups):
        rows = pl.ds(group * mirrors, mirrors)
        payload[:, :, (group + 1) * width : (group + 2) * width] = by_peer(
            own_half[rows, :] + other_half[rows, :].astype(F32), devices
        )
    payload[:, :, (groups + 1) * width :] = jnp.broadcast_to(
        bias_rows[...][None], (devices, per_peer, LANES)
    ).astype(BF16)


def join_second(
    norm_factor,
    received,
    message_one,
    early_counts,
    late_counts,
    mirror_rows,
    payload,
    mirrored_out,
    bias_total,
):
    devices, per_peer, _ = payload.shape
    node_dev, width = message_one.shape
    mirrors = mirror_rows.shape[0]
    early = early_counts.shape[0]
    groups = payload.shape[2] // width - 1
    mirrored = by_row(received[:, :, :width]).astype(BF16)
    mirrored_out[...] = mirrored
    partial_sums = (
        tdot(early_counts[:, node_dev:], message_one[:early, :])
        + tdot(late_counts[:, node_dev:], message_one[early:, :])
        + tdot(mirror_rows[:, node_dev:], mirrored)
    )
    payload[:, :, :width] = by_peer(partial_sums, devices)
    for group in range(groups):
        lanes = slice((group + 1) * width, (group + 2) * width)
        owned = (
            jnp.sum(
                received[:, :, lanes].astype(F32).reshape(devices // 2, 2, per_peer, width), axis=0
            )
            * norm_factor
        ).astype(BF16)
        payload[:, :, lanes] = jnp.broadcast_to(
            owned[None], (devices // 2, 2, per_peer, width)
        ).reshape(devices, per_peer, width)
    sums = (
        jnp.sum(received[:, :, (groups + 1) * width :].astype(F32), axis=0) * norm_factor
    )
    parts = width // LANES
    for block in range(parts):
        bias_total[:, block * LANES : (block + 1) * LANES] = (
            sums[block : block + 1, :] + sums[parts + block : parts + block + 1, :]
        )


def finish(
    received,
    mirrored,
    picking,
    early_counts,
    late_counts,
    mirror_rows,
    message_one,
    grad_z,
    w_self_one,
    grad_features,
    own_weights,
):
    node_dev, width = grad_z.shape
    mirrors = picking.shape[0]
    early = early_counts.shape[0]
    returned = by_row(received[:, :, :width]).astype(BF16)
    for start in range(0, node_dev, BLOCK):
        rows = pl.ds(start, BLOCK)
        grad_features[rows, :] = (
            dot_transposed(grad_z[rows, :], w_self_one[...])
            + tdot(early_counts[:, rows], message_one[:early, :])
            + tdot(late_counts[:, rows], message_one[early:, :])
            + tdot(picking[:, rows], returned)
            + tdot(mirror_rows[:, rows], mirrored[...])
        ).astype(BF16)
    for group in range(own_weights.shape[0] // mirrors):
        own_weights[pl.ds(group * mirrors, mirrors), :] = by_row(
            received[:, :, (group + 1) * width : (group + 2) * width]
        )


def write_out(
    core,
    other,
    grad_features,
    own_weights,
    bias_total,
    features_at,
    weights_at,
    bias_at,
    other_weights,
    semaphores,
):
    half, width = own_weights.shape
    mirrors = other.shape[0] * other.shape[1]
    mine = pl.multiple_of(core[0] * half, half)
    theirs = pl.multiple_of((1 - core[0]) * half, half)
    copies = [
        pltpu.make_async_copy(grad_features, features_at, semaphores.at[0]),
        pltpu.make_async_copy(own_weights, weights_at.at[pl.ds(mine, half)], semaphores.at[1]),
        pltpu.make_async_copy(bias_total, bias_at, semaphores.at[2]),
    ]
    for copy in copies:
        copy.start()
    for group in range(half // mirrors):
        other_weights[pl.ds(group * mirrors, mirrors), :] = by_row(
            other[:, :, (group + 1) * width : (group + 2) * width]
        )
    copies.append(
        pltpu.make_async_copy(
            other_weights, weights_at.at[pl.ds(theirs, half)], semaphores.at[3]
        )
    )
    copies[3].start()
    for copy in copies:
        copy.wait()


def shards(
    features,
    cotangent,
    w_self_one,
    w_nbr_one,
    bias_one,
    w_self_two,
    w_nbr_two,
    in_count,
    send_list,
    src_slot,
    dst_slot,
    edge_count,
):
    node_dev, width = features.shape
    devices = lax.axis_size("dom") * lax.axis_size("sub")
    per_peer = send_list.shape[2]
    mirrors = devices * per_peer
    slots = node_dev + mirrors
    edges = src_slot.shape[1]
    core = lax.axis_index("sub") % 2
    swap = [(i, i ^ 1) for i in range(devices)]
    in_count = in_count.reshape(-1, LANES)
    sent = send_list[0].T
    sources = src_slot.reshape(-1, LANES)
    targets = dst_slot.reshape(-1, LANES)
    blocks = node_dev // BLOCK

    payload_shape = (devices, per_peer, 2 * width)
    payload, scaled, picking, sources, targets = run(
        pick_rows,
        "pick_rows",
        [
            pltpu.HBM(payload_shape, BF16),
            pltpu.VMEM((node_dev, width), BF16),
            pltpu.VMEM((mirrors, node_dev), BF16),
            pltpu.VMEM(sources.shape, I32),
            pltpu.VMEM(targets.shape, I32),
        ],
        hbm=[features, cotangent, in_count, sent, sources, targets],
        scratch=staged_for(6, features, cotangent, in_count, sent)
        + [pltpu.VMEM(payload_shape, BF16), pltpu.SemaphoreType.DMA],
        flops=4 * mirrors * node_dev * width,
    )
    mirrored = exchange(payload).reshape(mirrors, 2 * width)

    rows_bf16 = pltpu.VMEM((node_dev, width), BF16)
    rows_f32 = pltpu.VMEM((node_dev, width), F32)
    early = node_dev * EARLY // 4
    early_counts, scaled, mirror_rows, partial_sums = run(
        count_edges,
        "count_edges",
        [
            pltpu.HBM((early, slots), BF16),
            pltpu.HBM((node_dev, width), BF16),
            pltpu.VMEM((mirrors, slots), BF16),
            pltpu.VMEM((mirrors, 2 * width), F32),
        ],
        smem=[edge_count],
        hbm=[features],
        vmem=[scaled, sources, targets],
        scratch=[
            rows_bf16,
            pltpu.SemaphoreType.DMA,
            pltpu.VMEM((edges, slots), F8),
            pltpu.VMEM((slots, edges), F8),
            pltpu.VMEM((early, slots), BF16),
            pltpu.SemaphoreType.DMA((early // BLOCK + 1,)),
        ],
        flops=2 * (early + 2 * mirrors) * edges * slots,
    )
    (payload,) = run(
        mirror_sums,
        "mirror_sums",
        [pltpu.HBM(payload_shape, BF16)],
        vmem=[partial_sums, mirror_rows, mirrored],
        scratch=[pltpu.VMEM(payload_shape, BF16), pltpu.SemaphoreType.DMA],
        flops=4 * mirrors * mirrors * width,
    )
    returned = exchange(payload).reshape(mirrors, 2 * width)
    forward, features_in, backward, mirror_rows, late_counts = run(
        local_sums,
        "local_sums",
        [
            rows_f32,
            rows_bf16,
            pltpu.HBM((node_dev, width), F32),
            pltpu.HBM((mirrors, slots), BF16),
            pltpu.HBM((node_dev - early, slots), BF16),
        ],
        smem=[edge_count],
        hbm=[early_counts, features, scaled],
        vmem=[sources, targets, mirrored, mirror_rows],
        scratch=[
            pltpu.VMEM((edges, slots), F8),
            pltpu.VMEM((node_dev - early, edges), F8),
            pltpu.VMEM((node_dev, slots), BF16),
            rows_bf16,
            rows_f32,
            pltpu.SemaphoreType.DMA((3,)),
            pltpu.SemaphoreType.DMA((blocks + 2,)),
        ],
        flops=4 * node_dev * slots * width + 2 * (node_dev - early) * edges * slots,
    )

    half = 2 * width
    grad_z_one, sent_half, bias_rows, mean_one, h_one, pulled, cotangent_in, early_counts = run(
        middle,
        "middle",
        [
            rows_bf16,
            pltpu.VMEM((half, width), BF16),
            pltpu.VMEM((2 * width // LANES, LANES), F32),
            rows_bf16,
            rows_bf16,
            rows_bf16,
            rows_bf16,
            pltpu.VMEM((early, slots), BF16),
        ],
        smem=[core.reshape(1)],
        hbm=[cotangent, backward, early_counts],
        vmem=[
            forward,
            returned,
            picking,
            features_in,
            w_nbr_one,
            w_self_one,
            bias_one.reshape(1, -1),
            w_nbr_two,
            w_self_two,
            in_count,
        ],
        scratch=[
            rows_f32,
            pltpu.SemaphoreType.DMA((3,)),
            rows_f32,
        ],
        flops=20 * node_dev * width * width,
    )
    other_half = lax.ppermute(sent_half, AXES, swap)
    message_one, picked, own_half, late_counts, mirror_rows = run(
        messages,
        "messages",
        [
            rows_bf16,
            pltpu.VMEM((mirrors, width), F32),
            pltpu.VMEM((half, width), F32),
            pltpu.VMEM((node_dev - early, slots), BF16),
            pltpu.VMEM((mirrors, slots), BF16),
        ],
        smem=[core.reshape(1)],
        hbm=[late_counts, mirror_rows],
        scratch=[pltpu.SemaphoreType.DMA((2,))],
        vmem=[
            in_count,
            grad_z_one,
            w_nbr_one,
            picking,
            features_in,
            mean_one,
            h_one,
            cotangent_in,
            pulled,
        ],
        flops=6 * node_dev * width * width,
    )

    columns = width * (half // mirrors + 1)
    payload_shape = (devices, per_peer, columns + LANES)
    (payload,) = run(
        join_first,
        "join_first",
        [pltpu.VMEM(payload_shape, BF16)],
        vmem=[own_half, other_half, picked, bias_rows],
    )
    received = exchange(payload)
    norm_factor = float(node_dev * devices) ** -0.5
    payload, mirrored, bias_total = run(
        functools.partial(join_second, norm_factor),
        "join_second",
        [
            pltpu.VMEM((devices, per_peer, columns), BF16),
            pltpu.VMEM((mirrors, width), BF16),
            pltpu.VMEM((1, width), F32),
        ],
        vmem=[received, message_one, early_counts, late_counts, mirror_rows],
    )
    received = exchange(payload)
    other = lax.ppermute(received, AXES, swap)
    grad_features, own_weights = run(
        finish,
        "finish",
        [rows_bf16, pltpu.VMEM((half, width), F32)],
        vmem=[
            received,
            mirrored,
            picking,
            early_counts,
            late_counts,
            mirror_rows,
            message_one,
            grad_z_one,
            w_self_one,
        ],
        flops=2 * node_dev * (slots + mirrors + width) * width,
        moved=4 * node_dev * slots,
    )
    grad_features, grad_weights, grad_bias = run(
        write_out,
        "write_out",
        [
            pltpu.HBM((node_dev, width), BF16),
            pltpu.HBM((2 * half, width), F32),
            pltpu.HBM((1, width), F32),
        ],
        smem=[core.reshape(1)],
        vmem=[other, grad_features, own_weights, bias_total],
        scratch=[pltpu.VMEM((half, width), F32), pltpu.SemaphoreType.DMA((4,))],
    )
    return (
        grad_features,
        grad_weights.reshape(4, width, width),
        grad_bias.reshape(width),
    )


def solution(mesh):
    by_device = P(AXES)
    return jax.shard_map(
        shards,
        mesh=mesh,
        in_specs=(
            P(AXES, None),
            P(AXES, None),
            P(),
            P(),
            P(),
            P(),
            P(),
            by_device,
            P(AXES, None, None),
            P(AXES, None),
            P(AXES, None),
            by_device,
        ),
        out_specs=(P(AXES, None), P(), P()),
        check_vma=False,
    )
```

```python
import functools

import jax
import jax.numpy as jnp
from jax import lax
from jax.experimental import pallas as pl
from jax.experimental.pallas import tpu as pltpu
from jax.sharding import PartitionSpec as P

AXES = ("dom", "sub")
BF16 = jnp.bfloat16
F8 = jnp.float8_e4m3fn
F32 = jnp.float32
I32 = jnp.int32
I16 = jnp.int16
LANES = 128
BLOCK = 256
ROWS = 512
EARLY = 2
VMEM_LIMIT = 24 * 2**20


def tdot(left, right):
    return lax.dot_general(left, right, (((0,), (0,)), ((), ())), preferred_element_type=F32)


def dot_transposed(left, right):
    return lax.dot_general(left, right, (((1,), (1,)), ((), ())), preferred_element_type=F32)


def dot(left, right):
    return jnp.dot(left, right, preferred_element_type=F32)


def exchange(rows):
    return lax.all_to_all(rows, AXES, split_axis=0, concat_axis=0, tiled=True)


def run(kernel, name, outs, vmem=(), hbm=(), smem=(), scratch=(), flops=0, moved=0):
    in_place = pl.BlockSpec(memory_space=pltpu.VMEM)
    remote = pl.BlockSpec(memory_space=pltpu.HBM)
    return pl.pallas_call(
        kernel,
        out_shape=tuple(outs),
        in_specs=[pl.BlockSpec(memory_space=pltpu.SMEM)] * len(smem)
        + [remote] * len(hbm)
        + [in_place] * len(vmem),
        out_specs=tuple(remote if out.memory_space == pltpu.HBM else in_place for out in outs),
        scratch_shapes=tuple(scratch),
        compiler_params=pltpu.CompilerParams(vmem_limit_bytes=VMEM_LIMIT),
        cost_estimate=pl.CostEstimate(flops=flops, bytes_accessed=moved, transcendentals=0),
        name=name,
    )(
        *smem,
        *[pltpu.with_memory_space_constraint(arg, pltpu.HBM) for arg in hbm],
        *[pltpu.with_memory_space_constraint(arg, pltpu.VMEM) for arg in vmem],
    )


def staged_for(count, *arrays):
    buffers = [pltpu.VMEM(array.shape, array.dtype) for array in arrays]
    return buffers + [pltpu.SemaphoreType.DMA((count,))]


def start_all(sources, buffers, semaphores):
    copies = [
        pltpu.make_async_copy(source, buffer, semaphores.at[index])
        for index, (source, buffer) in enumerate(zip(sources, buffers))
    ]
    for copy in copies:
        copy.start()
    return copies


def iota(shape, dim, dtype=I32):
    return lax.broadcasted_iota(dtype, shape, dim)


def one_hot(mask, dtype):
    return jnp.where(mask, 1.0, 0.0).astype(dtype)


def edge_hot(mask):
    return jnp.where(mask, jnp.ones(mask.shape, BF16), jnp.zeros(mask.shape, BF16)).astype(F8)


def by_peer(rows, devices):
    return rows.reshape(devices, rows.shape[0] // devices, rows.shape[1]).astype(BF16)


def by_row(parts):
    return parts.astype(F32).reshape(parts.shape[0] * parts.shape[1], parts.shape[2])


def inverse_columns(in_count):
    return (1.0 / jnp.maximum(in_count[...], 1).astype(F32)).T


def send(array, out, semaphore):
    copy = pltpu.make_async_copy(array, out, semaphore)
    copy.start()
    copy.wait()


def pick_rows(
    features_at,
    cotangent_at,
    in_count_at,
    sent_at,
    sources_at,
    targets_at,
    payload,
    scaled,
    picking,
    sources,
    targets,
    features,
    cotangent,
    in_count,
    sent,
    semaphores,
    rows_out,
    out_semaphore,
):
    node_dev, width = features.shape
    per_peer, devices = sent.shape
    mirrors = devices * per_peer
    copies = start_all(
        [sent_at, in_count_at, cotangent_at, features_at, sources_at, targets_at],
        [sent, in_count, cotangent, features, sources, targets],
        semaphores,
    )
    copies[0].wait()
    spread_out = one_hot(
        iota((mirrors, devices), 0) // per_peer == iota((mirrors, devices), 1), BF16
    )
    high = dot_transposed(spread_out, (sent[...] >> 5).astype(F32).astype(BF16))
    low = dot_transposed(spread_out, (sent[...] & 31).astype(F32).astype(BF16))
    within = iota((mirrors, per_peer), 0) % per_peer == iota((mirrors, per_peer), 1)
    owner = jnp.sum(jnp.where(within, high * 32.0 + low, 0.0), axis=1, keepdims=True).astype(I32)
    picked = iota((mirrors, node_dev), 1) == owner
    picks = one_hot(picked, BF16)
    picking[...] = picks
    copies[1].wait()
    inverse_rows = 1.0 / jnp.maximum(in_count[...], 1).astype(F32)
    owner_inverse = jnp.zeros((mirrors, LANES), F32)
    for block in range(node_dev // LANES):
        lanes = slice(block * LANES, (block + 1) * LANES)
        owner_inverse += jnp.where(picked[:, lanes], inverse_rows[block : block + 1, :], 0.0)
    owner_inverse = jnp.sum(owner_inverse, axis=1, keepdims=True)
    copies[2].wait()
    back = dot(picks, cotangent[...]) * owner_inverse
    rows_out[:, :, width:] = by_peer(back, devices)
    copies[3].wait()
    rows_out[:, :, :width] = by_peer(dot(picks, features[...]), devices)
    out_copy = pltpu.make_async_copy(rows_out, payload, out_semaphore)
    out_copy.start()
    columns = inverse_rows.T
    for block in range(node_dev // LANES):
        rows = pl.ds(block * LANES, LANES)
        scaled[rows, :] = (
            cotangent[rows, :].astype(F32) * columns[:, block : block + 1]
        ).astype(BF16)
    copies[4].wait()
    copies[5].wait()
    out_copy.wait()


def fill_from_hot(from_hot, sources):
    edges, slots = from_hot.shape
    source_columns = sources[...].T
    lane_ids = iota((LANES, slots), 1, I16)
    for block in range(edges // LANES):
        column = jnp.broadcast_to(source_columns[:, block : block + 1], (LANES, LANES)).astype(I16)
        column = jnp.concatenate([column] * (slots // LANES), axis=1)
        from_hot[pl.ds(block * LANES, LANES), :] = edge_hot(lane_ids == column)


def fill_into_hot(into_hot, targets, edge_count, first, place, size):
    edge_ids = iota(targets.shape, 0) * LANES + iota(targets.shape, 1)
    target_rows = jnp.where(edge_ids < edge_count[0], targets[...], -1).astype(I16)
    row_ids = iota((LANES, LANES), 0, I16)
    for block in range(into_hot.shape[1] // LANES):
        target_row = target_rows[block : block + 1, :]
        for part in range(0, size, LANES):
            into_hot[pl.ds(place + part, LANES), pl.ds(block * LANES, LANES)] = edge_hot(
                row_ids + jnp.int16(first + part) == target_row
            )


def count_edges(
    edge_count,
    features_at,
    scaled,
    sources,
    targets,
    counts_at,
    scaled_at,
    mirror_rows,
    partial_out,
    features,
    semaphore,
    from_hot,
    into_hot,
    counts,
    out_semaphores,
):
    node_dev, width = features.shape
    slots, edges = into_hot.shape
    early = counts.shape[0]
    feature_copy = pltpu.make_async_copy(features_at, features, semaphore)
    feature_copy.start()
    sends = [pltpu.make_async_copy(scaled, scaled_at, out_semaphores.at[early // BLOCK])]
    sends[0].start()
    fill_from_hot(from_hot, sources)
    for start in range(0, early, BLOCK):
        rows = pl.ds(start, BLOCK)
        fill_into_hot(into_hot, targets, edge_count, start, start, BLOCK)
        counts[rows, :] = dot(into_hot[rows, :], from_hot[...]).astype(BF16)
        copy = pltpu.make_async_copy(
            counts.at[rows], counts_at.at[rows], out_semaphores.at[start // BLOCK]
        )
        copy.start()
        sends.append(copy)
    fill_into_hot(into_hot, targets, edge_count, early, early, slots - early)
    mirror_rows[...] = dot(into_hot[node_dev:, :], from_hot[...]).astype(BF16)
    late_columns = dot(into_hot[early:node_dev, :], from_hot[:, node_dev:]).astype(BF16)
    feature_copy.wait()
    partial_out[:, :width] = dot(mirror_rows[:, :node_dev], features[...])
    partial_out[:, width:] = tdot(counts[:, node_dev:], scaled[:early, :]) + tdot(
        late_columns, scaled[early:, :]
    )
    for copy in sends:
        copy.wait()


def mirror_sums(partial_in, mirror_rows, mirrored, payload, rows_out, out_semaphore):
    devices, _, columns = rows_out.shape
    width = columns // 2
    received = mirrored[...]
    mirror_counts = mirror_rows[:, mirror_rows.shape[1] - mirror_rows.shape[0] :]
    front = partial_in[:, :width] + dot(mirror_counts, received[:, :width])
    back = partial_in[:, width:] + tdot(mirror_counts, received[:, width:])
    rows_out[:, :, :width] = by_peer(front, devices)
    rows_out[:, :, width:] = by_peer(back, devices)
    send(rows_out, payload, out_semaphore)


def local_sums(
    edge_count,
    early_at,
    features_at,
    scaled_at,
    sources,
    targets,
    mirrored,
    mirror_rows,
    forward,
    features,
    backward_at,
    mirror_at,
    late_at,
    from_hot,
    into_hot,
    counts,
    scaled,
    backward,
    semaphores,
    out_semaphores,
):
    node_dev, width = features.shape
    early = early_at.shape[0]
    loads = start_all(
        [scaled_at, early_at, features_at],
        [scaled, counts.at[pl.ds(0, early)], features],
        semaphores,
    )
    blocks = node_dev // BLOCK
    sends = [pltpu.make_async_copy(mirror_rows, mirror_at, out_semaphores.at[blocks])]
    sends[0].start()
    fill_from_hot(from_hot, sources)
    for start in range(early, node_dev, BLOCK):
        rows = pl.ds(start - early, BLOCK)
        fill_into_hot(into_hot, targets, edge_count, start, start - early, BLOCK)
        counts[pl.ds(start, BLOCK), :] = dot(into_hot[rows, :], from_hot[...]).astype(BF16)
    late = pl.ds(early, node_dev - early)
    sends.append(
        pltpu.make_async_copy(counts.at[late], late_at, out_semaphores.at[blocks + 1])
    )
    sends[1].start()
    for copy in loads:
        copy.wait()
    for index, start in enumerate(range(0, node_dev, BLOCK)):
        rows = pl.ds(start, BLOCK)
        backward[rows, :] = tdot(counts[:, rows], scaled[...]) + tdot(
            mirror_rows[:, rows], mirrored[:, width:]
        )
        copy = pltpu.make_async_copy(
            backward.at[rows], backward_at.at[rows], out_semaphores.at[index]
        )
        copy.start()
        sends.append(copy)
    for start in range(0, node_dev, BLOCK):
        rows = pl.ds(start, BLOCK)
        forward[rows, :] = dot(counts[rows, :node_dev], features[...]) + dot(
            counts[rows, node_dev:], mirrored[:, :width]
        )
    for copy in sends:
        copy.wait()


def block_inverse(columns, index, size=BLOCK):
    first = index * size // LANES
    return jnp.concatenate(
        [columns[:, b : b + 1] for b in range(first, first + size // LANES)], axis=0
    )


def middle(
    core,
    cotangent_at,
    backward_at,
    forward,
    returned,
    picking,
    features,
    w_nbr_one,
    w_self_one,
    bias_one,
    w_nbr_two,
    w_self_two,
    in_count,
    grad_z,
    sent_half,
    bias_rows,
    mean_one,
    h_one,
    pulled,
    cotangent,
    backward,
    semaphores,
    slope,
):
    node_dev, width = features.shape
    blocks = [pl.ds(start, ROWS) for start in range(0, node_dev, ROWS)]
    copies = start_all(
        [backward_at, cotangent_at],
        [backward, cotangent],
        semaphores,
    )
    columns = inverse_columns(in_count)
    for index, rows in enumerate(blocks):
        placed = tdot(picking[:, rows], returned[:, :width])
        mean = ((forward[rows, :] + placed) * block_inverse(columns, index, ROWS)).astype(BF16)
        mean_one[rows, :] = mean
        z_one = (
            dot(features[rows, :], w_self_one[...]) + dot(mean, w_nbr_one[...]) + bias_one[...]
        )
        sigmoid = 1.0 / (1.0 + jnp.exp(-z_one))
        h_one[rows, :] = (z_one * sigmoid).astype(BF16)
        slope[rows, :] = sigmoid * (1.0 + z_one * (1.0 - sigmoid))
    for copy in copies:
        copy.wait()
    bias_total = jnp.zeros((1, width), F32)
    for rows in blocks:
        pull = (backward[rows, :] + tdot(picking[:, rows], returned[:, width:])).astype(BF16)
        pulled[rows, :] = pull
        grad_h = dot_transposed(cotangent[rows, :], w_self_two[...]) + dot_transposed(
            pull, w_nbr_two[...]
        )
        grad = (grad_h * slope[rows, :]).astype(BF16)
        grad_z[rows, :] = grad
        bias_total += jnp.sum(grad.astype(F32), axis=0, keepdims=True)
    bias_high = bias_total.astype(BF16).astype(F32)
    bias_low = bias_total - bias_high
    for row, part in enumerate((bias_high, bias_low)):
        for block in range(width // LANES):
            bias_rows[row * (width // LANES) + block : row * (width // LANES) + block + 1, :] = (
                part[:, block * LANES : (block + 1) * LANES]
            )

    @pl.when(core[0] == 0)
    def _():
        sent_half[:width, :] = tdot(h_one[...], cotangent[...]).astype(BF16)
        sent_half[width:, :] = tdot(h_one[...], pulled[...]).astype(BF16)

    @pl.when(core[0] == 1)
    def _():
        sent_half[:width, :] = tdot(features[...], grad_z[...]).astype(BF16)
        sent_half[width:, :] = tdot(mean_one[...], grad_z[...]).astype(BF16)


def messages(
    core,
    in_count,
    grad_z,
    w_nbr_one,
    picking,
    features,
    mean_one,
    h_one,
    cotangent,
    pulled,
    message_one,
    picked,
    own_half,
):
    node_dev, width = grad_z.shape
    columns = inverse_columns(in_count)
    for index, start in enumerate(range(0, node_dev, BLOCK)):
        rows = pl.ds(start, BLOCK)
        message_one[rows, :] = (
            dot_transposed(grad_z[rows, :], w_nbr_one[...]) * block_inverse(columns, index)
        ).astype(BF16)
    picked[...] = dot(picking[...], message_one[...])

    @pl.when(core[0] == 0)
    def _():
        own_half[:width, :] = tdot(features[...], grad_z[...])
        own_half[width:, :] = tdot(mean_one[...], grad_z[...])

    @pl.when(core[0] == 1)
    def _():
        own_half[:width, :] = tdot(h_one[...], cotangent[...])
        own_half[width:, :] = tdot(h_one[...], pulled[...])


def join_first(own_half, other_half, picked, bias_rows, payload):
    devices, per_peer, _ = payload.shape
    mirrors, width = picked.shape
    groups = own_half.shape[0] // mirrors
    payload[:, :, :width] = by_peer(picked[...], devices)
    for group in range(groups):
        rows = pl.ds(group * mirrors, mirrors)
        payload[:, :, (group + 1) * width : (group + 2) * width] = by_peer(
            own_half[rows, :] + other_half[rows, :].astype(F32), devices
        )
    payload[:, :, (groups + 1) * width :] = jnp.broadcast_to(
        bias_rows[...][None], (devices, per_peer, LANES)
    ).astype(BF16)


def join_second(
    norm_factor,
    received,
    message_one,
    early_counts,
    late_counts,
    mirror_rows,
    payload,
    mirrored_out,
    bias_total,
):
    devices, per_peer, _ = payload.shape
    node_dev, width = message_one.shape
    mirrors = mirror_rows.shape[0]
    early = early_counts.shape[0]
    groups = payload.shape[2] // width - 1
    mirrored = by_row(received[:, :, :width]).astype(BF16)
    mirrored_out[...] = mirrored
    partial_sums = (
        tdot(early_counts[:, node_dev:], message_one[:early, :])
        + tdot(late_counts[:, node_dev:], message_one[early:, :])
        + tdot(mirror_rows[:, node_dev:], mirrored)
    )
    payload[:, :, :width] = by_peer(partial_sums, devices)
    for group in range(groups):
        lanes = slice((group + 1) * width, (group + 2) * width)
        owned = (
            jnp.sum(
                received[:, :, lanes].astype(F32).reshape(devices // 2, 2, per_peer, width), axis=0
            )
            * norm_factor
        ).astype(BF16)
        payload[:, :, lanes] = jnp.broadcast_to(
            owned[None], (devices // 2, 2, per_peer, width)
        ).reshape(devices, per_peer, width)
    sums = (
        jnp.sum(received[:, :, (groups + 1) * width :].astype(F32), axis=0) * norm_factor
    )
    parts = width // LANES
    for block in range(parts):
        bias_total[:, block * LANES : (block + 1) * LANES] = (
            sums[block : block + 1, :] + sums[parts + block : parts + block + 1, :]
        )


def finish(
    received,
    mirrored,
    picking,
    early_counts,
    late_counts,
    mirror_rows,
    message_one,
    grad_z,
    w_self_one,
    grad_features,
    own_weights,
):
    node_dev, width = grad_z.shape
    mirrors = picking.shape[0]
    early = early_counts.shape[0]
    returned = by_row(received[:, :, :width]).astype(BF16)
    for start in range(0, node_dev, BLOCK):
        rows = pl.ds(start, BLOCK)
        grad_features[rows, :] = (
            dot_transposed(grad_z[rows, :], w_self_one[...])
            + tdot(early_counts[:, rows], message_one[:early, :])
            + tdot(late_counts[:, rows], message_one[early:, :])
            + tdot(picking[:, rows], returned)
            + tdot(mirror_rows[:, rows], mirrored[...])
        ).astype(BF16)
    for group in range(own_weights.shape[0] // mirrors):
        own_weights[pl.ds(group * mirrors, mirrors), :] = by_row(
            received[:, :, (group + 1) * width : (group + 2) * width]
        )


def write_out(
    core,
    other,
    grad_features,
    own_weights,
    bias_total,
    features_at,
    weights_at,
    bias_at,
    other_weights,
    semaphores,
):
    half, width = own_weights.shape
    mirrors = other.shape[0] * other.shape[1]
    mine = pl.multiple_of(core[0] * half, half)
    theirs = pl.multiple_of((1 - core[0]) * half, half)
    copies = [
        pltpu.make_async_copy(grad_features, features_at, semaphores.at[0]),
        pltpu.make_async_copy(own_weights, weights_at.at[pl.ds(mine, half)], semaphores.at[1]),
        pltpu.make_async_copy(bias_total, bias_at, semaphores.at[2]),
    ]
    for copy in copies:
        copy.start()
    for group in range(half // mirrors):
        other_weights[pl.ds(group * mirrors, mirrors), :] = by_row(
            other[:, :, (group + 1) * width : (group + 2) * width]
        )
    copies.append(
        pltpu.make_async_copy(
            other_weights, weights_at.at[pl.ds(theirs, half)], semaphores.at[3]
        )
    )
    copies[3].start()
    for copy in copies:
        copy.wait()


def shards(
    features,
    cotangent,
    w_self_one,
    w_nbr_one,
    bias_one,
    w_self_two,
    w_nbr_two,
    in_count,
    send_list,
    src_slot,
    dst_slot,
    edge_count,
):
    node_dev, width = features.shape
    devices = lax.axis_size("dom") * lax.axis_size("sub")
    per_peer = send_list.shape[2]
    mirrors = devices * per_peer
    slots = node_dev + mirrors
    edges = src_slot.shape[1]
    core = lax.axis_index("sub") % 2
    swap = [(i, i ^ 1) for i in range(devices)]
    in_count = in_count.reshape(-1, LANES)
    sent = send_list[0].T
    sources = src_slot.reshape(-1, LANES)
    targets = dst_slot.reshape(-1, LANES)
    blocks = node_dev // BLOCK

    payload_shape = (devices, per_peer, 2 * width)
    payload, scaled, picking, sources, targets = run(
        pick_rows,
        "pick_rows",
        [
            pltpu.HBM(payload_shape, BF16),
            pltpu.VMEM((node_dev, width), BF16),
            pltpu.VMEM((mirrors, node_dev), BF16),
            pltpu.VMEM(sources.shape, I32),
            pltpu.VMEM(targets.shape, I32),
        ],
        hbm=[features, cotangent, in_count, sent, sources, targets],
        scratch=staged_for(6, features, cotangent, in_count, sent)
        + [pltpu.VMEM(payload_shape, BF16), pltpu.SemaphoreType.DMA],
        flops=4 * mirrors * node_dev * width,
    )
    mirrored = exchange(payload).reshape(mirrors, 2 * width)

    rows_bf16 = pltpu.VMEM((node_dev, width), BF16)
    rows_f32 = pltpu.VMEM((node_dev, width), F32)
    early = node_dev * EARLY // 4
    early_counts, scaled, mirror_rows, partial_sums = run(
        count_edges,
        "count_edges",
        [
            pltpu.HBM((early, slots), BF16),
            pltpu.HBM((node_dev, width), BF16),
            pltpu.VMEM((mirrors, slots), BF16),
            pltpu.VMEM((mirrors, 2 * width), F32),
        ],
        smem=[edge_count],
        hbm=[features],
        vmem=[scaled, sources, targets],
        scratch=[
            rows_bf16,
            pltpu.SemaphoreType.DMA,
            pltpu.VMEM((edges, slots), F8),
            pltpu.VMEM((slots, edges), F8),
            pltpu.VMEM((early, slots), BF16),
            pltpu.SemaphoreType.DMA((early // BLOCK + 1,)),
        ],
        flops=2 * (early + 2 * mirrors) * edges * slots,
    )
    (payload,) = run(
        mirror_sums,
        "mirror_sums",
        [pltpu.HBM(payload_shape, BF16)],
        vmem=[partial_sums, mirror_rows, mirrored],
        scratch=[pltpu.VMEM(payload_shape, BF16), pltpu.SemaphoreType.DMA],
        flops=4 * mirrors * mirrors * width,
    )
    returned = exchange(payload).reshape(mirrors, 2 * width)
    forward, features_in, backward, mirror_rows, late_counts = run(
        local_sums,
        "local_sums",
        [
            rows_f32,
            rows_bf16,
            pltpu.HBM((node_dev, width), F32),
            pltpu.HBM((mirrors, slots), BF16),
            pltpu.HBM((node_dev - early, slots), BF16),
        ],
        smem=[edge_count],
        hbm=[early_counts, features, scaled],
        vmem=[sources, targets, mirrored, mirror_rows],
        scratch=[
            pltpu.VMEM((edges, slots), F8),
            pltpu.VMEM((node_dev - early, edges), F8),
            pltpu.VMEM((node_dev, slots), BF16),
            rows_bf16,
            rows_f32,
            pltpu.SemaphoreType.DMA((3,)),
            pltpu.SemaphoreType.DMA((blocks + 2,)),
        ],
        flops=4 * node_dev * slots * width + 2 * (node_dev - early) * edges * slots,
    )

    half = 2 * width
    grad_z_one, sent_half, bias_rows, mean_one, h_one, pulled, cotangent_in = run(
        middle,
        "middle",
        [
            rows_bf16,
            pltpu.VMEM((half, width), BF16),
            pltpu.VMEM((2 * width // LANES, LANES), F32),
            rows_bf16,
            rows_bf16,
            rows_bf16,
            rows_bf16,
        ],
        smem=[core.reshape(1)],
        hbm=[cotangent, backward],
        vmem=[
            forward,
            returned,
            picking,
            features_in,
            w_nbr_one,
            w_self_one,
            bias_one.reshape(1, -1),
            w_nbr_two,
            w_self_two,
            in_count,
        ],
        scratch=[
            rows_f32,
            pltpu.SemaphoreType.DMA((2,)),
            rows_f32,
        ],
        flops=20 * node_dev * width * width,
    )
    other_half = lax.ppermute(sent_half, AXES, swap)
    message_one, picked, own_half = run(
        messages,
        "messages",
        [
            rows_bf16,
            pltpu.VMEM((mirrors, width), F32),
            pltpu.VMEM((half, width), F32),
        ],
        smem=[core.reshape(1)],
        vmem=[
            in_count,
            grad_z_one,
            w_nbr_one,
            picking,
            features_in,
            mean_one,
            h_one,
            cotangent_in,
            pulled,
        ],
        flops=6 * node_dev * width * width,
    )

    columns = width * (half // mirrors + 1)
    payload_shape = (devices, per_peer, columns + LANES)
    (payload,) = run(
        join_first,
        "join_first",
        [pltpu.VMEM(payload_shape, BF16)],
        vmem=[own_half, other_half, picked, bias_rows],
    )
    received = exchange(payload)
    norm_factor = float(node_dev * devices) ** -0.5
    payload, mirrored, bias_total = run(
        functools.partial(join_second, norm_factor),
        "join_second",
        [
            pltpu.VMEM((devices, per_peer, columns), BF16),
            pltpu.VMEM((mirrors, width), BF16),
            pltpu.VMEM((1, width), F32),
        ],
        vmem=[received, message_one, early_counts, late_counts, mirror_rows],
    )
    received = exchange(payload)
    other = lax.ppermute(received, AXES, swap)
    grad_features, own_weights = run(
        finish,
        "finish",
        [rows_bf16, pltpu.VMEM((half, width), F32)],
        vmem=[
            received,
            mirrored,
            picking,
            early_counts,
            late_counts,
            mirror_rows,
            message_one,
            grad_z_one,
            w_self_one,
        ],
        flops=2 * node_dev * (slots + mirrors + width) * width,
        moved=4 * node_dev * slots,
    )
    grad_features, grad_weights, grad_bias = run(
        write_out,
        "write_out",
        [
            pltpu.HBM((node_dev, width), BF16),
            pltpu.HBM((2 * half, width), F32),
            pltpu.HBM((1, width), F32),
        ],
        smem=[core.reshape(1)],
        vmem=[other, grad_features, own_weights, bias_total],
        scratch=[pltpu.VMEM((half, width), F32), pltpu.SemaphoreType.DMA((4,))],
    )
    return (
        grad_features,
        grad_weights.reshape(4, width, width),
        grad_bias.reshape(width),
    )


def solution(mesh):
    by_device = P(AXES)
    return jax.shard_map(
        shards,
        mesh=mesh,
        in_specs=(
            P(AXES, None),
            P(AXES, None),
            P(),
            P(),
            P(),
            P(),
            P(),
            by_device,
            P(AXES, None, None),
            P(AXES, None),
            P(AXES, None),
            by_device,
        ),
        out_specs=(P(AXES, None), P(), P()),
        check_vma=False,
    )
```

```python
import functools

import jax
import jax.numpy as jnp
from jax import lax
from jax.experimental import pallas as pl
from jax.experimental.pallas import tpu as pltpu
from jax.sharding import PartitionSpec as P

AXES = ("dom", "sub")
BF16 = jnp.bfloat16
F8 = jnp.float8_e4m3fn
F32 = jnp.float32
I32 = jnp.int32
I16 = jnp.int16
LANES = 128
BLOCK = 256
ROWS = 512
EARLY = 2
VMEM_LIMIT = 24 * 2**20


def tdot(left, right):
    return lax.dot_general(left, right, (((0,), (0,)), ((), ())), preferred_element_type=F32)


def dot_transposed(left, right):
    return lax.dot_general(left, right, (((1,), (1,)), ((), ())), preferred_element_type=F32)


def dot(left, right):
    return jnp.dot(left, right, preferred_element_type=F32)


def exchange(rows):
    return lax.all_to_all(rows, AXES, split_axis=0, concat_axis=0, tiled=True)


def run(kernel, name, outs, vmem=(), hbm=(), smem=(), scratch=(), flops=0, moved=0):
    in_place = pl.BlockSpec(memory_space=pltpu.VMEM)
    remote = pl.BlockSpec(memory_space=pltpu.HBM)
    return pl.pallas_call(
        kernel,
        out_shape=tuple(outs),
        in_specs=[pl.BlockSpec(memory_space=pltpu.SMEM)] * len(smem)
        + [remote] * len(hbm)
        + [in_place] * len(vmem),
        out_specs=tuple(remote if out.memory_space == pltpu.HBM else in_place for out in outs),
        scratch_shapes=tuple(scratch),
        compiler_params=pltpu.CompilerParams(vmem_limit_bytes=VMEM_LIMIT),
        cost_estimate=pl.CostEstimate(flops=flops, bytes_accessed=moved, transcendentals=0),
        name=name,
    )(
        *smem,
        *[pltpu.with_memory_space_constraint(arg, pltpu.HBM) for arg in hbm],
        *[pltpu.with_memory_space_constraint(arg, pltpu.VMEM) for arg in vmem],
    )


def staged_for(count, *arrays):
    buffers = [pltpu.VMEM(array.shape, array.dtype) for array in arrays]
    return buffers + [pltpu.SemaphoreType.DMA((count,))]


def start_all(sources, buffers, semaphores):
    copies = [
        pltpu.make_async_copy(source, buffer, semaphores.at[index])
        for index, (source, buffer) in enumerate(zip(sources, buffers))
    ]
    for copy in copies:
        copy.start()
    return copies


def iota(shape, dim, dtype=I32):
    return lax.broadcasted_iota(dtype, shape, dim)


def one_hot(mask, dtype):
    return jnp.where(mask, 1.0, 0.0).astype(dtype)


def edge_hot(mask):
    return jnp.where(mask, jnp.ones(mask.shape, BF16), jnp.zeros(mask.shape, BF16)).astype(F8)


def by_peer(rows, devices):
    return rows.reshape(devices, rows.shape[0] // devices, rows.shape[1]).astype(BF16)


def by_row(parts):
    return parts.astype(F32).reshape(parts.shape[0] * parts.shape[1], parts.shape[2])


def inverse_columns(in_count):
    return (1.0 / jnp.maximum(in_count[...], 1).astype(F32)).T


def send(array, out, semaphore):
    copy = pltpu.make_async_copy(array, out, semaphore)
    copy.start()
    copy.wait()


def pick_rows(
    features_at,
    cotangent_at,
    in_count_at,
    sent_at,
    sources_at,
    targets_at,
    payload,
    scaled,
    picking,
    sources,
    targets,
    features,
    cotangent,
    in_count,
    sent,
    semaphores,
    rows_out,
    out_semaphore,
):
    node_dev, width = features.shape
    per_peer, devices = sent.shape
    mirrors = devices * per_peer
    copies = start_all(
        [sent_at, in_count_at, cotangent_at, features_at, sources_at, targets_at],
        [sent, in_count, cotangent, features, sources, targets],
        semaphores,
    )
    copies[0].wait()
    spread_out = one_hot(
        iota((mirrors, devices), 0) // per_peer == iota((mirrors, devices), 1), BF16
    )
    high = dot_transposed(spread_out, (sent[...] >> 5).astype(F32).astype(BF16))
    low = dot_transposed(spread_out, (sent[...] & 31).astype(F32).astype(BF16))
    within = iota((mirrors, per_peer), 0) % per_peer == iota((mirrors, per_peer), 1)
    owner = jnp.sum(jnp.where(within, high * 32.0 + low, 0.0), axis=1, keepdims=True).astype(I32)
    picked = iota((mirrors, node_dev), 1) == owner
    picks = one_hot(picked, BF16)
    picking[...] = picks
    copies[1].wait()
    inverse_rows = 1.0 / jnp.maximum(in_count[...], 1).astype(F32)
    owner_inverse = jnp.zeros((mirrors, LANES), F32)
    for block in range(node_dev // LANES):
        lanes = slice(block * LANES, (block + 1) * LANES)
        owner_inverse += jnp.where(picked[:, lanes], inverse_rows[block : block + 1, :], 0.0)
    owner_inverse = jnp.sum(owner_inverse, axis=1, keepdims=True)
    copies[2].wait()
    back = dot(picks, cotangent[...]) * owner_inverse
    rows_out[:, :, width:] = by_peer(back, devices)
    copies[3].wait()
    rows_out[:, :, :width] = by_peer(dot(picks, features[...]), devices)
    out_copy = pltpu.make_async_copy(rows_out, payload, out_semaphore)
    out_copy.start()
    columns = inverse_rows.T
    for block in range(node_dev // LANES):
        rows = pl.ds(block * LANES, LANES)
        scaled[rows, :] = (
            cotangent[rows, :].astype(F32) * columns[:, block : block + 1]
        ).astype(BF16)
    copies[4].wait()
    copies[5].wait()
    out_copy.wait()


def fill_from_hot(from_hot, sources):
    edges, slots = from_hot.shape
    source_columns = sources[...].T
    lane_ids = iota((LANES, slots), 1, I16)
    for block in range(edges // LANES):
        column = jnp.broadcast_to(source_columns[:, block : block + 1], (LANES, LANES)).astype(I16)
        column = jnp.concatenate([column] * (slots // LANES), axis=1)
        from_hot[pl.ds(block * LANES, LANES), :] = edge_hot(lane_ids == column)


def fill_into_hot(into_hot, targets, edge_count, first, place, size):
    edge_ids = iota(targets.shape, 0) * LANES + iota(targets.shape, 1)
    target_rows = jnp.where(edge_ids < edge_count[0], targets[...], -1).astype(I16)
    row_ids = iota((LANES, LANES), 0, I16)
    for block in range(into_hot.shape[1] // LANES):
        target_row = target_rows[block : block + 1, :]
        for part in range(0, size, LANES):
            into_hot[pl.ds(place + part, LANES), pl.ds(block * LANES, LANES)] = edge_hot(
                row_ids + jnp.int16(first + part) == target_row
            )


def count_edges(
    edge_count,
    features_at,
    scaled,
    sources,
    targets,
    counts_at,
    scaled_at,
    mirror_rows,
    partial_out,
    features,
    semaphore,
    from_hot,
    into_hot,
    counts,
    out_semaphores,
):
    node_dev, width = features.shape
    slots, edges = into_hot.shape
    early = counts.shape[0]
    feature_copy = pltpu.make_async_copy(features_at, features, semaphore)
    feature_copy.start()
    sends = [pltpu.make_async_copy(scaled, scaled_at, out_semaphores.at[early // BLOCK])]
    sends[0].start()
    fill_from_hot(from_hot, sources)
    for start in range(0, early, BLOCK):
        rows = pl.ds(start, BLOCK)
        fill_into_hot(into_hot, targets, edge_count, start, start, BLOCK)
        counts[rows, :] = dot(into_hot[rows, :], from_hot[...]).astype(BF16)
        copy = pltpu.make_async_copy(
            counts.at[rows], counts_at.at[rows], out_semaphores.at[start // BLOCK]
        )
        copy.start()
        sends.append(copy)
    fill_into_hot(into_hot, targets, edge_count, early, early, slots - early)
    mirror_rows[...] = dot(into_hot[node_dev:, :], from_hot[...]).astype(BF16)
    late_columns = dot(into_hot[early:node_dev, :], from_hot[:, node_dev:]).astype(BF16)
    feature_copy.wait()
    partial_out[:, :width] = dot(mirror_rows[:, :node_dev], features[...])
    partial_out[:, width:] = tdot(counts[:, node_dev:], scaled[:early, :]) + tdot(
        late_columns, scaled[early:, :]
    )
    for copy in sends:
        copy.wait()


def mirror_sums(partial_in, mirror_rows, mirrored, payload, rows_out, out_semaphore):
    devices, _, columns = rows_out.shape
    width = columns // 2
    received = mirrored[...]
    mirror_counts = mirror_rows[:, mirror_rows.shape[1] - mirror_rows.shape[0] :]
    front = partial_in[:, :width] + dot(mirror_counts, received[:, :width])
    back = partial_in[:, width:] + tdot(mirror_counts, received[:, width:])
    rows_out[:, :, :width] = by_peer(front, devices)
    rows_out[:, :, width:] = by_peer(back, devices)
    send(rows_out, payload, out_semaphore)


def local_sums(
    edge_count,
    early_at,
    features_at,
    scaled_at,
    sources,
    targets,
    mirrored,
    mirror_rows,
    forward,
    features,
    backward_at,
    mirror_at,
    late_at,
    from_hot,
    into_hot,
    counts,
    scaled,
    backward,
    semaphores,
    out_semaphores,
):
    node_dev, width = features.shape
    early = early_at.shape[0]
    loads = start_all(
        [scaled_at, early_at, features_at],
        [scaled, counts.at[pl.ds(0, early)], features],
        semaphores,
    )
    blocks = node_dev // BLOCK
    sends = [pltpu.make_async_copy(mirror_rows, mirror_at, out_semaphores.at[blocks])]
    sends[0].start()
    fill_from_hot(from_hot, sources)
    for start in range(early, node_dev, BLOCK):
        rows = pl.ds(start - early, BLOCK)
        fill_into_hot(into_hot, targets, edge_count, start, start - early, BLOCK)
        counts[pl.ds(start, BLOCK), :] = dot(into_hot[rows, :], from_hot[...]).astype(BF16)
    late = pl.ds(early, node_dev - early)
    sends.append(
        pltpu.make_async_copy(counts.at[late], late_at, out_semaphores.at[blocks + 1])
    )
    sends[1].start()
    for copy in loads:
        copy.wait()
    for index, start in enumerate(range(0, node_dev, BLOCK)):
        rows = pl.ds(start, BLOCK)
        backward[rows, :] = tdot(counts[:, rows], scaled[...]) + tdot(
            mirror_rows[:, rows], mirrored[:, width:]
        )
        copy = pltpu.make_async_copy(
            backward.at[rows], backward_at.at[rows], out_semaphores.at[index]
        )
        copy.start()
        sends.append(copy)
    for start in range(0, node_dev, BLOCK):
        rows = pl.ds(start, BLOCK)
        forward[rows, :] = dot(counts[rows, :node_dev], features[...]) + dot(
            counts[rows, node_dev:], mirrored[:, :width]
        )
    for copy in sends:
        copy.wait()


def block_inverse(columns, index, size=BLOCK):
    first = index * size // LANES
    return jnp.concatenate(
        [columns[:, b : b + 1] for b in range(first, first + size // LANES)], axis=0
    )


def middle(
    core,
    cotangent_at,
    backward_at,
    forward,
    returned,
    picking,
    features,
    w_nbr_one,
    w_self_one,
    bias_one,
    w_nbr_two,
    w_self_two,
    in_count,
    grad_z,
    sent_half,
    bias_rows,
    mean_one,
    h_one,
    pulled,
    cotangent,
    backward,
    semaphores,
    slope,
):
    node_dev, width = features.shape
    blocks = [pl.ds(start, ROWS) for start in range(0, node_dev, ROWS)]
    copies = start_all(
        [backward_at, cotangent_at],
        [backward, cotangent],
        semaphores,
    )
    columns = inverse_columns(in_count)
    for index, rows in enumerate(blocks):
        placed = tdot(picking[:, rows], returned[:, :width])
        mean = ((forward[rows, :] + placed) * block_inverse(columns, index, ROWS)).astype(BF16)
        mean_one[rows, :] = mean
        z_one = (
            dot(features[rows, :], w_self_one[...]) + dot(mean, w_nbr_one[...]) + bias_one[...]
        )
        sigmoid = 1.0 / (1.0 + jnp.exp(-z_one))
        h_one[rows, :] = (z_one * sigmoid).astype(BF16)
        slope[rows, :] = sigmoid * (1.0 + z_one * (1.0 - sigmoid))
    for copy in copies:
        copy.wait()
    bias_total = jnp.zeros((1, width), F32)
    for rows in blocks:
        pull = (backward[rows, :] + tdot(picking[:, rows], returned[:, width:])).astype(BF16)
        pulled[rows, :] = pull
        grad_h = dot_transposed(cotangent[rows, :], w_self_two[...]) + dot_transposed(
            pull, w_nbr_two[...]
        )
        grad = (grad_h * slope[rows, :]).astype(BF16)
        grad_z[rows, :] = grad
        bias_total += jnp.sum(grad.astype(F32), axis=0, keepdims=True)
    bias_high = bias_total.astype(BF16).astype(F32)
    bias_low = bias_total - bias_high
    for row, part in enumerate((bias_high, bias_low)):
        for block in range(width // LANES):
            bias_rows[row * (width // LANES) + block : row * (width // LANES) + block + 1, :] = (
                part[:, block * LANES : (block + 1) * LANES]
            )

    @pl.when(core[0] == 0)
    def _():
        sent_half[:width, :] = tdot(h_one[...], cotangent[...]).astype(BF16)
        sent_half[width:, :] = tdot(h_one[...], pulled[...]).astype(BF16)

    @pl.when(core[0] == 1)
    def _():
        sent_half[:width, :] = tdot(features[...], grad_z[...]).astype(BF16)
        sent_half[width:, :] = tdot(mean_one[...], grad_z[...]).astype(BF16)


def messages(
    core,
    in_count,
    grad_z,
    w_nbr_one,
    picking,
    features,
    mean_one,
    h_one,
    cotangent,
    pulled,
    message_one,
    picked,
    own_half,
):
    node_dev, width = grad_z.shape
    columns = inverse_columns(in_count)
    for index, start in enumerate(range(0, node_dev, BLOCK)):
        rows = pl.ds(start, BLOCK)
        message_one[rows, :] = (
            dot_transposed(grad_z[rows, :], w_nbr_one[...]) * block_inverse(columns, index)
        ).astype(BF16)
    picked[...] = dot(picking[...], message_one[...])

    @pl.when(core[0] == 0)
    def _():
        own_half[:width, :] = tdot(features[...], grad_z[...])
        own_half[width:, :] = tdot(mean_one[...], grad_z[...])

    @pl.when(core[0] == 1)
    def _():
        own_half[:width, :] = tdot(h_one[...], cotangent[...])
        own_half[width:, :] = tdot(h_one[...], pulled[...])


def join_first(own_half, other_half, picked, bias_rows, payload):
    devices, per_peer, _ = payload.shape
    mirrors, width = picked.shape
    groups = own_half.shape[0] // mirrors
    payload[:, :, :width] = by_peer(picked[...], devices)
    for group in range(groups):
        rows = pl.ds(group * mirrors, mirrors)
        payload[:, :, (group + 1) * width : (group + 2) * width] = by_peer(
            own_half[rows, :] + other_half[rows, :].astype(F32), devices
        )
    payload[:, :, (groups + 1) * width :] = jnp.broadcast_to(
        bias_rows[...][None], (devices, per_peer, LANES)
    ).astype(BF16)


def join_second(
    norm_factor,
    received,
    message_one,
    early_counts,
    late_counts,
    mirror_rows,
    payload,
    mirrored_out,
    bias_total,
):
    devices, per_peer, _ = payload.shape
    node_dev, width = message_one.shape
    mirrors = mirror_rows.shape[0]
    early = early_counts.shape[0]
    groups = payload.shape[2] // width - 1
    mirrored = by_row(received[:, :, :width]).astype(BF16)
    mirrored_out[...] = mirrored
    partial_sums = (
        tdot(early_counts[:, node_dev:], message_one[:early, :])
        + tdot(late_counts[:, node_dev:], message_one[early:, :])
        + tdot(mirror_rows[:, node_dev:], mirrored)
    )
    payload[:, :, :width] = by_peer(partial_sums, devices)
    for group in range(groups):
        lanes = slice((group + 1) * width, (group + 2) * width)
        owned = (
            jnp.sum(
                received[:, :, lanes].astype(F32).reshape(devices // 2, 2, per_peer, width), axis=0
            )
            * norm_factor
        ).astype(BF16)
        payload[:, :, lanes] = jnp.broadcast_to(
            owned[None], (devices // 2, 2, per_peer, width)
        ).reshape(devices, per_peer, width)
    sums = (
        jnp.sum(received[:, :, (groups + 1) * width :].astype(F32), axis=0) * norm_factor
    )
    parts = width // LANES
    for block in range(parts):
        bias_total[:, block * LANES : (block + 1) * LANES] = (
            sums[block : block + 1, :] + sums[parts + block : parts + block + 1, :]
        )


def finish(
    received,
    mirrored,
    picking,
    early_counts,
    late_counts,
    mirror_rows,
    message_one,
    grad_z,
    w_self_one,
    features_at,
    own_weights,
    grad_features,
    semaphore,
):
    node_dev, width = grad_z.shape
    mirrors = picking.shape[0]
    early = early_counts.shape[0]
    returned = by_row(received[:, :, :width]).astype(BF16)
    for start in range(0, node_dev, BLOCK):
        rows = pl.ds(start, BLOCK)
        grad_features[rows, :] = (
            dot_transposed(grad_z[rows, :], w_self_one[...])
            + tdot(early_counts[:, rows], message_one[:early, :])
            + tdot(late_counts[:, rows], message_one[early:, :])
            + tdot(picking[:, rows], returned)
            + tdot(mirror_rows[:, rows], mirrored[...])
        ).astype(BF16)
    copy = pltpu.make_async_copy(grad_features, features_at, semaphore)
    copy.start()
    for group in range(own_weights.shape[0] // mirrors):
        own_weights[pl.ds(group * mirrors, mirrors), :] = by_row(
            received[:, :, (group + 1) * width : (group + 2) * width]
        )
    copy.wait()


def write_out(
    core,
    other,
    own_weights,
    bias_total,
    weights_at,
    bias_at,
    other_weights,
    semaphores,
):
    half, width = own_weights.shape
    mirrors = other.shape[0] * other.shape[1]
    mine = pl.multiple_of(core[0] * half, half)
    theirs = pl.multiple_of((1 - core[0]) * half, half)
    copies = [
        pltpu.make_async_copy(own_weights, weights_at.at[pl.ds(mine, half)], semaphores.at[0]),
        pltpu.make_async_copy(bias_total, bias_at, semaphores.at[1]),
    ]
    for copy in copies:
        copy.start()
    for group in range(half // mirrors):
        other_weights[pl.ds(group * mirrors, mirrors), :] = by_row(
            other[:, :, (group + 1) * width : (group + 2) * width]
        )
    copies.append(
        pltpu.make_async_copy(
            other_weights, weights_at.at[pl.ds(theirs, half)], semaphores.at[2]
        )
    )
    copies[2].start()
    for copy in copies:
        copy.wait()


def shards(
    features,
    cotangent,
    w_self_one,
    w_nbr_one,
    bias_one,
    w_self_two,
    w_nbr_two,
    in_count,
    send_list,
    src_slot,
    dst_slot,
    edge_count,
):
    node_dev, width = features.shape
    devices = lax.axis_size("dom") * lax.axis_size("sub")
    per_peer = send_list.shape[2]
    mirrors = devices * per_peer
    slots = node_dev + mirrors
    edges = src_slot.shape[1]
    core = lax.axis_index("sub") % 2
    swap = [(i, i ^ 1) for i in range(devices)]
    in_count = in_count.reshape(-1, LANES)
    sent = send_list[0].T
    sources = src_slot.reshape(-1, LANES)
    targets = dst_slot.reshape(-1, LANES)
    blocks = node_dev // BLOCK

    payload_shape = (devices, per_peer, 2 * width)
    payload, scaled, picking, sources, targets = run(
        pick_rows,
        "pick_rows",
        [
            pltpu.HBM(payload_shape, BF16),
            pltpu.VMEM((node_dev, width), BF16),
            pltpu.VMEM((mirrors, node_dev), BF16),
            pltpu.VMEM(sources.shape, I32),
            pltpu.VMEM(targets.shape, I32),
        ],
        hbm=[features, cotangent, in_count, sent, sources, targets],
        scratch=staged_for(6, features, cotangent, in_count, sent)
        + [pltpu.VMEM(payload_shape, BF16), pltpu.SemaphoreType.DMA],
        flops=4 * mirrors * node_dev * width,
    )
    mirrored = exchange(payload).reshape(mirrors, 2 * width)

    rows_bf16 = pltpu.VMEM((node_dev, width), BF16)
    rows_f32 = pltpu.VMEM((node_dev, width), F32)
    early = node_dev * EARLY // 4
    early_counts, scaled, mirror_rows, partial_sums = run(
        count_edges,
        "count_edges",
        [
            pltpu.HBM((early, slots), BF16),
            pltpu.HBM((node_dev, width), BF16),
            pltpu.VMEM((mirrors, slots), BF16),
            pltpu.VMEM((mirrors, 2 * width), F32),
        ],
        smem=[edge_count],
        hbm=[features],
        vmem=[scaled, sources, targets],
        scratch=[
            rows_bf16,
            pltpu.SemaphoreType.DMA,
            pltpu.VMEM((edges, slots), F8),
            pltpu.VMEM((slots, edges), F8),
            pltpu.VMEM((early, slots), BF16),
            pltpu.SemaphoreType.DMA((early // BLOCK + 1,)),
        ],
        flops=2 * (early + 2 * mirrors) * edges * slots,
    )
    (payload,) = run(
        mirror_sums,
        "mirror_sums",
        [pltpu.HBM(payload_shape, BF16)],
        vmem=[partial_sums, mirror_rows, mirrored],
        scratch=[pltpu.VMEM(payload_shape, BF16), pltpu.SemaphoreType.DMA],
        flops=4 * mirrors * mirrors * width,
    )
    returned = exchange(payload).reshape(mirrors, 2 * width)
    forward, features_in, backward, mirror_rows, late_counts = run(
        local_sums,
        "local_sums",
        [
            rows_f32,
            rows_bf16,
            pltpu.HBM((node_dev, width), F32),
            pltpu.HBM((mirrors, slots), BF16),
            pltpu.HBM((node_dev - early, slots), BF16),
        ],
        smem=[edge_count],
        hbm=[early_counts, features, scaled],
        vmem=[sources, targets, mirrored, mirror_rows],
        scratch=[
            pltpu.VMEM((edges, slots), F8),
            pltpu.VMEM((node_dev - early, edges), F8),
            pltpu.VMEM((node_dev, slots), BF16),
            rows_bf16,
            rows_f32,
            pltpu.SemaphoreType.DMA((3,)),
            pltpu.SemaphoreType.DMA((blocks + 2,)),
        ],
        flops=4 * node_dev * slots * width + 2 * (node_dev - early) * edges * slots,
    )

    half = 2 * width
    grad_z_one, sent_half, bias_rows, mean_one, h_one, pulled, cotangent_in = run(
        middle,
        "middle",
        [
            rows_bf16,
            pltpu.VMEM((half, width), BF16),
            pltpu.VMEM((2 * width // LANES, LANES), F32),
            rows_bf16,
            rows_bf16,
            rows_bf16,
            rows_bf16,
        ],
        smem=[core.reshape(1)],
        hbm=[cotangent, backward],
        vmem=[
            forward,
            returned,
            picking,
            features_in,
            w_nbr_one,
            w_self_one,
            bias_one.reshape(1, -1),
            w_nbr_two,
            w_self_two,
            in_count,
        ],
        scratch=[
            rows_f32,
            pltpu.SemaphoreType.DMA((2,)),
            rows_f32,
        ],
        flops=20 * node_dev * width * width,
    )
    other_half = lax.ppermute(sent_half, AXES, swap)
    message_one, picked, own_half = run(
        messages,
        "messages",
        [
            rows_bf16,
            pltpu.VMEM((mirrors, width), F32),
            pltpu.VMEM((half, width), F32),
        ],
        smem=[core.reshape(1)],
        vmem=[
            in_count,
            grad_z_one,
            w_nbr_one,
            picking,
            features_in,
            mean_one,
            h_one,
            cotangent_in,
            pulled,
        ],
        flops=6 * node_dev * width * width,
    )

    columns = width * (half // mirrors + 1)
    payload_shape = (devices, per_peer, columns + LANES)
    (payload,) = run(
        join_first,
        "join_first",
        [pltpu.VMEM(payload_shape, BF16)],
        vmem=[own_half, other_half, picked, bias_rows],
    )
    received = exchange(payload)
    norm_factor = float(node_dev * devices) ** -0.5
    payload, mirrored, bias_total = run(
        functools.partial(join_second, norm_factor),
        "join_second",
        [
            pltpu.VMEM((devices, per_peer, columns), BF16),
            pltpu.VMEM((mirrors, width), BF16),
            pltpu.VMEM((1, width), F32),
        ],
        vmem=[received, message_one, early_counts, late_counts, mirror_rows],
    )
    received = exchange(payload)
    other = lax.ppermute(received, AXES, swap)
    grad_features, own_weights = run(
        finish,
        "finish",
        [pltpu.HBM((node_dev, width), BF16), pltpu.VMEM((half, width), F32)],
        scratch=[rows_bf16, pltpu.SemaphoreType.DMA],
        vmem=[
            received,
            mirrored,
            picking,
            early_counts,
            late_counts,
            mirror_rows,
            message_one,
            grad_z_one,
            w_self_one,
        ],
        flops=2 * node_dev * (slots + mirrors + width) * width,
        moved=4 * node_dev * slots,
    )
    grad_weights, grad_bias = run(
        write_out,
        "write_out",
        [
            pltpu.HBM((2 * half, width), F32),
            pltpu.HBM((1, width), F32),
        ],
        smem=[core.reshape(1)],
        vmem=[other, own_weights, bias_total],
        scratch=[pltpu.VMEM((half, width), F32), pltpu.SemaphoreType.DMA((3,))],
    )
    return (
        grad_features,
        grad_weights.reshape(4, width, width),
        grad_bias.reshape(width),
    )


def solution(mesh):
    by_device = P(AXES)
    return jax.shard_map(
        shards,
        mesh=mesh,
        in_specs=(
            P(AXES, None),
            P(AXES, None),
            P(),
            P(),
            P(),
            P(),
            P(),
            by_device,
            P(AXES, None, None),
            P(AXES, None),
            P(AXES, None),
            by_device,
        ),
        out_specs=(P(AXES, None), P(), P()),
        check_vma=False,
    )
```
